32 devices in a mesh: dp: 8 (over z, x), tensor: 4 (over y, core).
Axes of the slice: x: 2, y: 2, z: 4, core: 2. Of those that a mesh axis runs over, the one named last changes fastest.
Arguments:
- tokens: bfloat16 [8192, 2048], P('dp', 'tensor'), may hold values from -6 to 6
- cotangent: bfloat16 [8192, 2048], P('dp', 'tensor'), may hold values from -6 to 6
- doc_lengths: int32 [8, 4], P('dp'), may hold values from 0 to 1024, as said below
- norm_gain: float32 [2048], replicated, may hold values from 0.5 to 1.5
- w_inner: bfloat16 [2048, 2, 4096], P(None, None, 'tensor'), may hold values from -0.125 to 0.125
- w_step: bfloat16 [2048, 64], P(None, 'tensor'), may hold values from -0.125 to 0.125
- w_state: bfloat16 [2048, 256], replicated, may hold values from -0.125 to 0.125
- conv_inner: float32 [5, 4096], P(None, 'tensor'), may hold values from -3 to 3
- conv_state: float32 [5, 256], replicated, may hold values from -3 to 3
- step_bias: float32 [64], P('tensor'), may hold values from -4 to -1
- log_rate: float32 [64], P('tensor'), may hold values from 0 to 2.5
- skip_gain: float32 [64], P('tensor'), may hold values from 0.5 to 1.5
- gate_gain: float32 [4096], P('tensor'), may hold values from 0.5 to 1.5
- w_out: bfloat16 [4096, 2048], P('tensor'), may hold values from -0.09375 to 0.09375
Outputs:
- mixed_out: bfloat16 [8192, 2048], P('dp', 'tensor')
- grad_tokens: bfloat16 [8192, 2048], P('dp', 'tensor')
- grad_norm_gain: float32 [2048], P('tensor')
- grad_w_inner: float32 [2048, 2, 4096], P('dp', None, 'tensor')
- grad_w_step: float32 [2048, 64], P('dp', 'tensor')
- grad_w_state: float32 [2048, 256], P(('dp', 'tensor'))
- grad_conv_inner: float32 [5, 4096], P(None, 'tensor')
- grad_conv_state: float32 [5, 256], replicated
- grad_step_bias: float32 [64], P('tensor')
- grad_log_rate: float32 [64], P('tensor')
- grad_skip_gain: float32 [64], P('tensor')
- grad_gate_gain: float32 [4096], P('tensor')
- grad_w_out: float32 [4096, 2048], P('tensor', 'dp')
The draws below stay inside these ranges and needn't reach their ends.
Inputs may be any that keep to these rules, and one draw needn't show every extreme that they name: `doc_lengths`: row s lists the lengths of up to 4 documents packed from the start of slot s, followed by padding; zero is an empty document; a row's sum lies between 513 and 1024; some row is one document of 1024 tokens.
All inputs are finite; a program needn't handle non-finite values.
Results may differ from the reference program's by a relative error of at most 0.0091.
Values may be sent and summed in bfloat16 or wider, within the bound.
No kernel may reach another device: no remote copies, remote signals or barrier semaphores. Data moves between devices by JAX's collectives and lax.ppermute only.
A program may use at most 192 MiB of HBM per device.

```python
import jax
import jax.numpy as jnp
from jax import lax

D = 2048
HEADS = 64
INNER = 4096
STATE = 128
CONV = 4
BLOCK = 256
DOCS = 4
SLOT = 1024
SLOTS = 8
TOKENS = 8192


def draw_doc_lengths(key, part):
    key = jax.random.fold_in(key, 11)
    fill_key, cut_key, full_key = jax.random.split(key, 3)
    filled = jax.random.randint(fill_key, (SLOTS,), SLOT // 2 + 1, SLOT + 1)
    cut_points = jax.random.randint(cut_key, (SLOTS, DOCS - 1), 0, SLOT + 1)
    cut_points = jnp.sort(cut_points * filled[:, None] // SLOT, axis=1)
    boundary = jnp.concatenate([jnp.zeros((SLOTS, 1), jnp.int32), cut_points, filled[:, None]], axis=1)
    lengths = boundary[:, 1:] - boundary[:, :-1]
    chosen = jax.random.randint(full_key, (), 0, SLOTS)
    single = jnp.concatenate([jnp.full((1,), SLOT, jnp.int32), jnp.zeros((DOCS - 1,), jnp.int32)])
    row_index = jnp.arange(SLOTS)
    return jnp.where((row_index == chosen)[:, None], single[None, :], lengths).astype(jnp.int32)


def with_spikes(drawn, key, source, target, parts, factor):
    owner, partner = [(jnp.arange(drawn.shape[dim]) // (drawn.shape[dim] // parts)).reshape([-1 if axis == dim else 1 for axis in range(drawn.ndim)]) for dim in (source, target)]
    chosen = jax.random.permutation(key, parts)[partner]
    strong = (owner == chosen) | (owner == (partner + parts // 2) % parts)
    return jnp.where(strong, factor * drawn, drawn)


def block_scale(stream_key, extent, cuts, low, high):
    def one(position, blocks):
        steps = jax.random.uniform(jax.random.fold_in(jax.random.fold_in(stream_key, 6), position), (blocks,), jnp.float32, low / len(cuts), high / len(cuts))
        return jnp.repeat(jnp.exp(steps), extent[position] // blocks).reshape((-1,) + (1,) * (len(extent) - position - 1))

    factor_of = one(*cuts[0])
    for cut in cuts[1:]:
        factor_of = factor_of * one(*cut)
    return factor_of


def centred(key, extent, scale, most, cuts=(), held_as=jnp.bfloat16):
    drawn = jax.random.normal(key, extent, jnp.float32) * scale
    if len(cuts) > 0:
        drawn = block_scale(key, extent, cuts, -0.22, 0.18) * drawn
    return jnp.clip(drawn, min=-most, max=most).astype(held_as)


def noise_with(stream_key, dims, scale, limit, cuts, heavy, kind=jnp.bfloat16):
    drawn = scale * jax.random.normal(stream_key, dims, jnp.float32)
    if cuts:
        drawn = drawn * block_scale(stream_key, dims, cuts, -0.22, 0.18)
    return jnp.clip(with_spikes(drawn, jax.random.fold_in(stream_key, 3), *heavy), -limit, limit).astype(kind)


def setup_inputs(seed: int = 0) -> dict:
    streams_of = jax.random.split(jax.random.key(seed), 15)
    return {
        "tokens": centred(streams_of[0], (TOKENS, D), 1.0, 6.0, ((0, 8), (1, 4))),
        "cotangent": noise_with(streams_of[1], (TOKENS, D), 1.0, 6.0, ((0, 8), (1, 4)), (0, 1, 8, 2.0)),
        "doc_lengths": draw_doc_lengths(jax.random.fold_in(streams_of[14], 71), 0),
        "norm_gain": jnp.clip(1.0 + 0.1 * jax.random.normal(streams_of[3], (D,), jnp.float32), 0.5, 1.5),
        "w_inner": centred(streams_of[4], (D, 2, INNER), D ** -0.5, 0.125, ((2, 4),)),
        "w_step": centred(streams_of[5], (D, HEADS), D ** -0.5, 0.125, ((1, 4),)),
        "w_state": centred(streams_of[6], (D, 2 * STATE), D ** -0.5, 0.125),
        "conv_inner": centred(streams_of[7], (CONV + 1, INNER), CONV ** -0.5, 3.0, ((1, 4),), jnp.float32),
        "conv_state": centred(streams_of[8], (CONV + 1, 2 * STATE), CONV ** -0.5, 3.0, (), jnp.float32),
        "step_bias": jnp.clip(-4.0 + 3.0 * jax.random.uniform(streams_of[9], (HEADS,), jnp.float32) ** block_scale(streams_of[9], (HEADS,), ((0, 4),), -0.2, 0.2), -4.0, -1.0),
        "log_rate": jnp.clip(2.5 * jax.random.uniform(streams_of[10], (HEADS,), jnp.float32) ** block_scale(streams_of[10], (HEADS,), ((0, 4),), -0.2, 0.2), 0.0, 2.5),
        "skip_gain": jnp.clip(0.5 + 1.0 * jax.random.uniform(streams_of[11], (HEADS,), jnp.float32) ** block_scale(streams_of[11], (HEADS,), ((0, 4),), -0.2, 0.2), 0.5, 1.5),
        "gate_gain": jnp.clip(1.0 + 0.1 * jax.random.normal(streams_of[12], (INNER,), jnp.float32), 0.5, 1.5),
        "w_out": centred(streams_of[13], (INNER, D), INNER ** -0.5, 0.09375, ((0, 4),)),
    }


@jax.custom_vjp
def low(v):
    return lax.optimization_barrier(v.astype(jnp.bfloat16)).astype(jnp.float32)

@jax.custom_vjp
def low_back(v):
    return v

def low_keep(v):
    return (low(v), None)

def low_pass(kept, grad):
    return (grad,)

def back_keep(v):
    return (v, None)

def back_low(kept, grad):
    return (low(grad),)
low.defvjp(low_keep, low_pass)
low_back.defvjp(back_keep, back_low)
epsilon = 1e-05
highest = lax.Precision.HIGHEST

def segment_ids(lengths, length_all):
    doc_ends = jnp.cumsum(lengths.astype(jnp.int32)).astype(jnp.int32)
    places = jnp.arange(length_all, dtype=jnp.int32)
    segment = lax.optimization_barrier(jnp.sum((places[:, None] >= doc_ends[None, :]).astype(jnp.int32), axis=1)).astype(jnp.int32)
    present = (places < doc_ends[-1]).astype(jnp.float32)
    return (segment, present)

def causal_conv(values, filters, segment):
    taps_count = filters.shape[0] - 1
    result = filters[taps_count] + filters[0] * values
    for offset in range(1, taps_count):
        shifted = jnp.concatenate([jnp.zeros((offset, values.shape[1]), values.dtype), values[:-offset]], axis=0)
        earlier = jnp.concatenate([jnp.full((offset,), -1, jnp.int32), segment[:-offset]])
        result = result + filters[offset] * shifted * (earlier == segment).astype(values.dtype)[:, None]
    return jax.nn.silu(result)

def scan_block(carried, block_data):
    memory, last_doc = carried
    inputs, decay_rate, keys_in, queries, segment = block_data
    blocksize = segment.shape[0]
    rising = jnp.cumsum(decay_rate, axis=0)
    places = jnp.arange(blocksize)
    linked = (places[:, None] >= places[None, :]) & (segment[:, None] == segment[None, :])
    linked_cube = linked[:, :, None]
    spread = rising[:, None, :] - rising[None, :, :]
    weights = jnp.where(linked_cube, jnp.exp(jnp.where(linked_cube, spread, 0.0)), 0.0)
    intersection = jnp.dot(queries, keys_in.T, precision=highest)
    outputs = jnp.einsum('ijh,jhp->ihp', weights * intersection[:, :, None], inputs, precision=highest)
    entering = jnp.exp(rising) * (segment == last_doc).astype(rising.dtype)[:, None]
    outputs = outputs + entering[:, :, None] * jnp.einsum('is,hps->ihp', queries, memory, precision=highest)
    final_doc = segment[-1].astype(jnp.int32)
    leaving = jnp.where((segment == final_doc)[:, None], jnp.exp(rising[-1][None, :] - rising), 0.0)
    carry_scale = jnp.exp(rising[-1]) * (final_doc == last_doc).astype(rising.dtype)
    fresh = jnp.einsum('jhp,js->hps', leaving[:, :, None] * inputs, keys_in, precision=highest)
    memory = memory * carry_scale[:, None, None] + fresh
    return ((memory, final_doc), outputs)

def state_scan(shaped, step_size, decay_rate, keys_in, queries, segment):
    length_all, heads_all, headsize = shaped.shape
    blocks_all = length_all // BLOCK
    states = keys_in.shape[1]
    pieces = ((shaped * step_size[:, :, None]).reshape(blocks_all, BLOCK, heads_all, headsize), decay_rate.reshape(blocks_all, BLOCK, heads_all), keys_in.reshape(blocks_all, BLOCK, states), queries.reshape(blocks_all, BLOCK, states), segment.reshape(blocks_all, BLOCK))
    initial = (jnp.zeros((heads_all, headsize, states), shaped.dtype), jnp.array(-1, dtype=jnp.int32))
    _, outputs = lax.scan(jax.checkpoint(scan_block), initial, pieces)
    return outputs.reshape(length_all, heads_all, headsize)

def mixer(proj_inner, proj_step, proj_state, conv_inner, conv_state, step_bias, log_rate, skip_gain, segment):
    channels = proj_inner.shape[1] // 2
    gate_part = proj_inner[:, :channels]
    value_part = proj_inner[:, channels:]
    convolved = causal_conv(value_part, conv_inner, segment)
    state_conv = causal_conv(proj_state, conv_state, segment)
    step_size = jax.nn.softplus(proj_step + step_bias)
    decay_rate = -jnp.exp(log_rate) * step_size
    heads_all = step_size.shape[1]
    length_all = convolved.shape[0]
    shaped = convolved.reshape(length_all, heads_all, channels // heads_all)
    states = state_conv.shape[1] // 2
    mixed_heads = state_scan(shaped, step_size, decay_rate, state_conv[:, :states], state_conv[:, states:], segment)
    mixed_heads = mixed_heads + skip_gain[None, :, None] * shaped
    return mixed_heads.reshape(length_all, channels) * jax.nn.silu(gate_part)

def layer(tokens_in, norm_gain, w_inner, w_step, w_state, conv_inner, conv_state, step_bias, log_rate, skip_gain, gate_gain, w_out, segment, present):
    scale_in = lax.rsqrt(lax.optimization_barrier(jnp.mean(tokens_in * tokens_in, axis=1, keepdims=True)) + epsilon)
    normed = low(tokens_in * scale_in * norm_gain)
    proj_inner = low_back(jnp.dot(normed, w_inner.reshape(D, 2 * INNER), precision=highest))
    proj_step = low_back(jnp.dot(normed, w_step, precision=highest))
    proj_state = low_back(jnp.dot(normed, w_state, precision=highest))
    gated = mixer(proj_inner, proj_step, proj_state, conv_inner, conv_state, step_bias, log_rate, skip_gain, segment)
    scale_out = lax.rsqrt(lax.optimization_barrier(jnp.mean(gated * gated, axis=1, keepdims=True)) + epsilon)
    mixed = low(gated * scale_out * gate_gain * present[:, None])
    return tokens_in + jnp.dot(mixed, w_out, precision=highest)

def reference(tokens, cotangent, doc_lengths, norm_gain, w_inner, w_step, w_state, conv_inner, conv_state, step_bias, log_rate, skip_gain, gate_gain, w_out):
    weights = tuple((weight_arg.astype(jnp.float32) for weight_arg in (norm_gain, w_inner, w_step, w_state, conv_inner, conv_state, step_bias, log_rate, skip_gain, gate_gain, w_out)))
    slot_tokens = tokens.astype(jnp.float32).reshape(SLOTS, SLOT, D)
    slot_grads = cotangent.astype(jnp.float32).reshape(SLOTS, SLOT, D)

    def one_slot(totals, slot_data):
        tokens_in, grad_in, lengths = slot_data
        segment, present = segment_ids(lengths, SLOT)
        present = present.astype(tokens_in.dtype)

        def forward(tokens_now, *params):
            return layer(tokens_now, *params, segment, present)
        result, pullback = jax.vjp(forward, tokens_in, *weights)
        gradients = pullback(grad_in)
        totals = tuple((running + update for running, update in zip(totals, gradients[1:])))
        return (totals, (result.astype(jnp.bfloat16), gradients[0].astype(jnp.bfloat16)))
    initial = tuple((jnp.zeros_like(weight_arg) for weight_arg in weights))
    totals, (results, input_grads) = lax.scan(one_slot, initial, (slot_tokens, slot_grads, doc_lengths))
    return (results.reshape(TOKENS, D), input_grads.reshape(TOKENS, D), totals[0], totals[1], totals[2], totals[3], totals[4], totals[5], totals[6], totals[7], totals[8], totals[9], totals[10])
```

```python
import functools
import math

import jax
import jax.numpy as jnp
from jax import lax
from jax.experimental import pallas as pl
from jax.experimental.pallas import tpu as pltpu
from jax.sharding import PartitionSpec as P

F32 = jnp.float32
BF16 = jnp.bfloat16
HIGHEST = lax.Precision.HIGHEST
EPSILON = 1e-05
LOG2E = math.log2(math.e)
LANES = 128
SPAN = 128
GROUP = 256
VMEM_LIMIT = 56 * 1024 * 1024

NN = (((1,), (0,)), ((), ()))
NT = (((1,), (1,)), ((), ()))
TN = (((0,), (0,)), ((), ()))


def dot(left, right, dims=NN, precision=None):
    return lax.dot_general(left, right, dims, precision=precision, preferred_element_type=F32)


def sigmoid(a):
    return 0.5 * jnp.tanh(0.5 * a) + 0.5


def iota(shape, dim):
    return lax.broadcasted_iota(jnp.int32, shape, dim)


def tri(upper):
    rows, cols = iota((SPAN, SPAN), 0), iota((SPAN, SPAN), 1)
    return ((rows <= cols) if upper else (rows >= cols)).astype(F32)


def call(body, grid, in_specs, out_specs, out_shape, scratch=(), prefetch=0, flops=0, moved=0, name=None):
    return pl.pallas_call(
        body,
        grid_spec=pltpu.PrefetchScalarGridSpec(
            num_scalar_prefetch=prefetch,
            grid=grid,
            in_specs=in_specs,
            out_specs=out_specs,
            scratch_shapes=list(scratch),
        ),
        out_shape=out_shape,
        compiler_params=pltpu.CompilerParams(
            vmem_limit_bytes=VMEM_LIMIT, dimension_semantics=("arbitrary",) * len(grid)
        ),
        cost_estimate=pl.CostEstimate(flops=int(flops), bytes_accessed=int(moved), transcendentals=0),
        name=name,
    )


def held(shape):
    zeros = (0,) * len(shape)
    return pl.BlockSpec(shape, lambda *_: zeros, pipeline_mode=pl.Buffered(1))


def shape_of(*dims, dtype=F32):
    return jax.ShapeDtypeStruct(dims, dtype)


def conv_taps(wide, marks, filters):
    rows = wide.shape[0] - 8
    now = wide[8:]
    total = filters[4:5] + filters[0:1] * now
    shifted = [now]
    for k in range(1, 4):
        moved = wide[8 - k : 8 - k + rows] * marks[:, k - 1 : k]
        shifted.append(moved)
        total = total + filters[k : k + 1] * moved
    return total, shifted


def conv_back(later, marks, filters):
    rows = later.shape[0] - 8
    total = filters[0:1] * later[:rows]
    for k in range(1, 4):
        total = total + filters[k : k + 1] * (later[k : k + rows] * marks[k : k + rows, k - 1 : k])
    return total


def prep_kernel(
    parts, heads, groups_all, rank,
    *refs,
):
    pieces, refs = refs[:parts], refs[parts:]
    (gain, w_state, w_step, conv, bias, rate, marks, seg_row,
     normed, pre_state, maps, maps_t, per_head, rows_out, cross, cross_t, halo) = refs
    step = pl.program_id(0)
    width = w_state.shape[0]
    quarter = width // parts
    wide = [piece[...].astype(F32) for piece in pieces]
    squares = wide[0] * wide[0]
    for other in wide[1:]:
        squares = squares + other * other
    scale = lax.rsqrt(jnp.sum(squares, axis=1, keepdims=True) / width + EPSILON)
    proj = jnp.zeros((SPAN, w_state.shape[1]), F32)
    pre = jnp.zeros((SPAN, LANES), F32)
    for k in range(parts):
        at = pl.multiple_of((rank[0] ^ k) * quarter, quarter)
        low = (wide[k] * scale * gain[:, pl.ds(at, quarter)]).astype(BF16)
        normed[:, pl.ds(at, quarter)] = low
        proj = proj + dot(low, w_state[pl.ds(at, quarter), :])
        pre = pre + dot(low, w_step[pl.ds(at, quarter), :])
    pre = pre + bias[...]
    pre_state[...] = proj

    @pl.when(step == 0)
    def _():
        halo[...] = jnp.zeros_like(halo)

    mark = marks[...]
    total, _ = conv_taps(jnp.concatenate([halo[...], proj], axis=0), mark, conv[...])
    halo[...] = proj[SPAN - 8 :]
    both = total * sigmoid(total)
    maps[...] = both.astype(BF16)
    states = both.shape[1] // 2
    keys, queries = both[:, :states], both[:, states:]
    maps_t[:states] = keys.T.astype(BF16)
    maps_t[states:] = queries.T.astype(BF16)

    size = jnp.maximum(pre, 0.0) + jnp.log1p(jnp.exp(-jnp.abs(pre)))
    rising = dot(tri(False), -rate[...] * size, precision=HIGHEST)
    entering = jnp.exp(rising) * mark[:, 3:4]
    leaving = jnp.exp(rising[SPAN - 1 :] - rising) * mark[:, 4:5]
    rising = rising * LOG2E
    section = iota((SPAN, LANES), 1) // heads
    packed = jnp.where(section == 0, rising, entering)
    packed = jnp.where(section == 2, leaving, packed)
    packed = jnp.where(section == 3, size, packed)
    packed = jnp.where(section == 4, pre, packed)
    packed = jnp.where(section == 5, scale, packed)
    per_head[...] = packed
    turned = rising.T
    for g in range(groups_all):
        rows_out[g] = turned[g * heads // groups_all : g * heads // groups_all + 8]

    low_keys, low_queries = keys.astype(BF16), queries.astype(BF16)
    same = mark[:, 6:7] == seg_row[0:1, :]
    rows, cols = iota((SPAN, SPAN), 0), iota((SPAN, SPAN), 1)
    cross[...] = jnp.where(same & (rows >= cols), dot(low_queries, low_keys, NT), 0.0)
    cross_t[...] = jnp.where(same & (rows <= cols), dot(low_keys, low_queries, NT), 0.0)


def spread(table, section, heads, count):
    lane = iota((table.shape[0], LANES), 1)
    tiles = []
    for pair in range(count // 2):
        at = section * heads + 2 * pair
        tiles.append(jnp.where(lane < LANES // 2, table[:, at : at + 1], table[:, at + 1 : at + 2]))
    return jnp.concatenate(tiles, axis=1)


def forward_kernel(
    heads, normed, w_gate, w_value, conv, skip, per_head, marks, rows_in, maps, maps_t, cross,
    value, gate, mixed, memory, squares, state,
):
    g = pl.program_id(0)
    length = normed.shape[0]
    states = maps.shape[1] // 2
    count = GROUP // 64
    lane = iota((SPAN, LANES), 1)
    value[0:8] = jnp.zeros((8, GROUP), F32)

    def project(i, _):
        at = pl.multiple_of(i * 256, 256)
        rows = normed[pl.ds(at, 256), :]
        value[pl.ds(at + 8, 256), :] = dot(rows, w_value[...])
        gate[pl.ds(at, 256), :] = dot(rows, w_gate[...])
        return 0

    lax.fori_loop(0, length // 256, project, 0)
    state[...] = jnp.zeros_like(state)
    turn = lax.rem(LANES - count * g, LANES)

    def block(b, _):
        at = pl.multiple_of(b * SPAN, SPAN)
        total, _ = conv_taps(value[pl.ds(at, SPAN + 8), :], marks[pl.ds(at, SPAN), :], conv[...])
        inputs = total * sigmoid(total)
        table = pltpu.roll(per_head[pl.ds(at, SPAN), :], turn, 1)
        entering, leaving, size = (spread(table, s, heads, count) for s in (1, 2, 3))
        scaled = inputs * size
        keys_t = maps_t[0:states, pl.ds(at, SPAN)]
        queries = maps[pl.ds(at, SPAN), states:]
        low_state = state[...].astype(BF16)
        memory[b] = low_state
        out = entering * dot(queries, low_state) + skip[...] * inputs
        rising_rows = rows_in[0, pl.ds(pl.multiple_of(b * 8, 8), 8), :]
        crossed = cross[pl.ds(at, SPAN), :]
        parts = []
        for pair in range(count // 2):
            weights = []
            for j in (2 * pair, 2 * pair + 1):
                gap = jnp.minimum(table[:, j : j + 1] - rising_rows[j : j + 1, :], 0.0)
                weights.append((jnp.exp2(gap) * crossed).astype(BF16))
            tile = scaled[:, pair * LANES : (pair + 1) * LANES]
            stacked = jnp.concatenate(
                [
                    jnp.where(lane < LANES // 2, tile, 0.0).astype(BF16),
                    jnp.where(lane < LANES // 2, 0.0, tile).astype(BF16),
                ],
                axis=0,
            )
            parts.append(dot(jnp.concatenate(weights, axis=1), stacked))
        out = out + jnp.concatenate(parts, axis=1)
        fresh = dot(keys_t, (leaving * scaled).astype(BF16))
        state[...] = state[...] * entering[SPAN - 1 :] + fresh
        mixed[pl.ds(at, SPAN), :] = out
        opened = gate[pl.ds(at, SPAN), :]
        gated = out * (opened * sigmoid(opened))
        power = gated * gated
        folded = power[:, :LANES]
        for tile in range(1, GROUP // LANES):
            folded = folded + power[:, tile * LANES : (tile + 1) * LANES]

        @pl.when(g == 0)
        def _():
            squares[pl.ds(at, SPAN), :] = folded

        @pl.when(g > 0)
        def _():
            squares[pl.ds(at, SPAN), :] += folded

        return 0

    lax.fori_loop(0, length // SPAN, block, 0)


def cotangent_kernel(cotangent, w_out, gate, mixed, gain, grad, sums):
    g = pl.program_id(0)

    def chunk(i, _):
        at = pl.multiple_of(i * 256, 256)
        now = dot(cotangent[pl.ds(at, 256), :], w_out[...], NT)
        grad[pl.ds(at, 256), :] = now
        opened = gate[pl.ds(at, 256), :]
        power = now * mixed[pl.ds(at, 256), :] * (opened * sigmoid(opened)) * gain[...]
        folded = power[:, :LANES]
        for tile in range(1, GROUP // LANES):
            folded = folded + power[:, tile * LANES : (tile + 1) * LANES]

        @pl.when(g == 0)
        def _():
            sums[pl.ds(at, 256), :] = folded

        @pl.when(g > 0)
        def _():
            sums[pl.ds(at, 256), :] += folded

        return 0

    lax.fori_loop(0, cotangent.shape[0] // 256, chunk, 0)


def gate_kernel(
    run, place, cotangent, grad, gate, mixed, gain, factors,
    low_mixed, grad_mixer, grad_gate, grad_gain, w_send, w_own,
):
    length = cotangent.shape[0]
    grad_gain[...] = jnp.zeros_like(grad_gain)

    def chunk(i, _):
        at = pl.ds(pl.multiple_of(i * SPAN, SPAN), SPAN)
        factor, pull = factors[at, 0:1], factors[at, 1:2]
        opened, out, now = gate[at, :], mixed[at, :], grad[at, :]
        chance = sigmoid(opened)
        swish = opened * chance
        gated = out * swish
        scaled = gated * factor
        low_mixed[at, :] = (scaled * gain[...]).astype(BF16)
        grad_gain[...] += jnp.sum(now * scaled, axis=0, keepdims=True)
        grad_gated = now * (factor * gain[...]) - gated * pull
        grad_mixer[at, :] = (grad_gated * swish).astype(BF16)
        grad_gate[at, :] = (grad_gated * out * chance * (1.0 + opened * (1.0 - chance))).astype(BF16)
        return 0

    lax.fori_loop(0, length // SPAN, chunk, 0)
    for half, target in ((1, w_send), (0, w_own)):
        for z in range(cotangent.shape[1] // (2 * run)):
            at = pl.multiple_of((2 * z + (place[0] ^ half)) * run, run)
            target[:, z * run : (z + 1) * run] = dot(
                low_mixed[...], cotangent[:, pl.ds(at, run)], TN
            ).astype(BF16)


def weight_kernel(place, left_send, left_own, right, send, own):
    send[...] = dot(left_send[...], right[...], TN).astype(BF16)
    own[...] = dot(left_own[...], right[...], TN).astype(BF16)


def backward_kernel(
    heads, groups_all, value, grad_out, mixed, memory, conv, skip, per_head, marks, rows_in, maps, maps_t,
    cross, cross_t, seg_row, pre_state, conv_state, rate,
    grad_value, grad_conv, grad_skip, grad_state, grad_step, grad_conv_state, grad_heads,
    later, grad_memory, grad_cross, folded, grad_maps, later_state,
):
    g = pl.program_id(0)
    length = grad_out.shape[0]
    blocks = length // SPAN
    states = maps.shape[1] // 2
    count = GROUP // 64
    lane = iota((SPAN, LANES), 1)
    row = iota((SPAN, GROUP), 0)
    turn = lax.rem(LANES - count * g, LANES)
    channel, target = iota((GROUP, LANES), 0), iota((GROUP, LANES), 1)
    pick_rise = (target == count * g + channel // 64).astype(BF16)
    pick_size = (target == heads + count * g + channel // 64).astype(BF16)
    later[...] = jnp.zeros_like(later)
    grad_memory[...] = jnp.zeros_like(grad_memory)
    grad_conv[...] = jnp.zeros_like(grad_conv)
    grad_skip[...] = jnp.zeros_like(grad_skip)

    @pl.when(g == 0)
    def _():
        grad_cross[...] = jnp.zeros_like(grad_cross)
        folded[...] = jnp.zeros_like(folded)
        grad_maps[...] = jnp.zeros_like(grad_maps)

    def block(i, _):
        b = blocks - 1 - i
        start = pl.multiple_of(b * SPAN, SPAN)
        at = pl.ds(start, SPAN)
        filters = conv[...]
        total, shifted = conv_taps(value[pl.ds(start, SPAN + 8), :], marks[at, :], filters)
        chance = sigmoid(total)
        inputs = total * chance
        table = pltpu.roll(per_head[at, :], turn, 1)
        entering, leaving, size = (spread(table, s, heads, count) for s in (1, 2, 3))
        scaled = inputs * size
        low_scaled = scaled.astype(BF16)
        pulled = grad_out[at, :].astype(F32)
        keys, queries_t = maps[at, 0:states], maps_t[states:, pl.ds(start, SPAN)]
        memory_now = memory[b]
        grad_next = grad_memory[...]
        low_next = grad_next.astype(BF16)
        entered = (entering * pulled).astype(BF16)
        left = (leaving * scaled).astype(BF16)
        grad_maps[at, 0:states] += dot(left, low_next, NT)
        grad_maps[at, states:] += dot(entered, memory_now, NT)
        rising_rows = rows_in[0, pl.ds(pl.multiple_of(b * 8, 8), 8), :]
        crossed_t = cross_t[at, :]
        cross_sum = jnp.zeros((SPAN, SPAN), F32)
        parts = []
        for pair in range(count // 2):
            tile = pulled[:, pair * LANES : (pair + 1) * LANES]
            one = jnp.where(lane < LANES // 2, tile, 0.0).astype(BF16)
            two = jnp.where(lane < LANES // 2, 0.0, tile).astype(BF16)
            low_tile = low_scaled[:, pair * LANES : (pair + 1) * LANES]
            weights = []
            for j, masked in ((2 * pair, one), (2 * pair + 1, two)):
                gap = table[:, j : j + 1] - rising_rows[j : j + 1, :]
                cross_sum = cross_sum + jnp.exp2(jnp.minimum(gap, 0.0)) * dot(masked, low_tile, NT)
                weights.append((jnp.exp2(jnp.minimum(-gap, 0.0)) * crossed_t).astype(BF16))
            parts.append(dot(jnp.concatenate(weights, axis=1), jnp.concatenate([one, two], axis=0)))
        grad_cross[at, :] += cross_sum
        grad_within = jnp.concatenate(parts, axis=1)
        grad_left = dot(keys, low_next)
        grad_scaled = grad_within + leaving * grad_left
        scanned = mixed[at, :] - skip[...] * inputs
        kept = left.astype(F32) * grad_left
        rise = pulled * scanned - low_scaled.astype(F32) * grad_within - kept
        carried = entering[SPAN - 1 :] * jnp.sum(low_next.astype(F32) * memory_now.astype(F32), axis=0, keepdims=True)
        rise = rise + jnp.where(row == SPAN - 1, carried + jnp.sum(kept, axis=0, keepdims=True), 0.0)
        grown = grad_scaled * inputs
        summed = folded[at, :]
        for product, pick in ((rise, pick_rise), (grown, pick_size)):
            high = product.astype(BF16)
            rest = (product - high.astype(F32)).astype(BF16)
            summed = summed + dot(high, pick) + dot(rest, pick)
        folded[at, :] = summed
        grad_skip[...] += jnp.sum(pulled * inputs, axis=0, keepdims=True)
        grad_inputs = size * grad_scaled + skip[...] * pulled
        grad_total = grad_inputs * (chance * (1.0 + total * (1.0 - chance)))
        for k in range(4):
            grad_conv[k : k + 1] += jnp.sum(grad_total * shifted[k], axis=0, keepdims=True)
        grad_conv[4:5] += jnp.sum(grad_total, axis=0, keepdims=True)
        wide = pl.ds(start, SPAN + 8)
        longer = jnp.concatenate([grad_total, later[...]], axis=0)
        later[...] = grad_total[:8]
        grad_value[at, :] = conv_back(longer, marks[wide, :], filters).astype(BF16)
        grad_memory[...] = entering[SPAN - 1 :] * grad_next + dot(queries_t, entered)
        return 0

    lax.fori_loop(0, blocks, block, 0)

    @pl.when(g == groups_all - 1)
    def _():
        later_state[...] = jnp.zeros_like(later_state)
        grad_conv_state[...] = jnp.zeros_like(grad_conv_state)
        grad_heads[...] = jnp.zeros_like(grad_heads)

        def finish(i, _):
            start = pl.multiple_of((blocks - 1 - i) * SPAN, SPAN)
            at = pl.ds(start, SPAN)
            mark = marks[at, :]
            rows, cols = iota((SPAN, SPAN), 0), iota((SPAN, SPAN), 1)
            linked = (rows >= cols) & (mark[:, 6:7] == seg_row[0:1, pl.ds(start, SPAN)])
            crossed = jnp.where(linked, grad_cross[at, :], 0.0)
            keys, queries = maps[at, 0:states], maps[at, states:]
            grad_keys = grad_maps[at, 0:states] + dot(crossed.T.astype(BF16), queries)
            grad_queries = grad_maps[at, states:] + dot(crossed.astype(BF16), keys)
            filters = conv_state[...]
            total, shifted = conv_taps(pre_state[pl.ds(start, SPAN + 8), :], mark, filters)
            chance = sigmoid(total)
            grad_total = jnp.concatenate([grad_keys, grad_queries], axis=1) * (
                chance * (1.0 + total * (1.0 - chance))
            )
            for k in range(4):
                grad_conv_state[k : k + 1] += jnp.sum(grad_total * shifted[k], axis=0, keepdims=True)
            grad_conv_state[4:5] += jnp.sum(grad_total, axis=0, keepdims=True)
            wide = pl.ds(start, SPAN + 8)
            longer = jnp.concatenate([grad_total, later_state[...]], axis=0)
            later_state[...] = grad_total[:8]
            grad_state[at, :] = conv_back(longer, marks[wide, :], filters).astype(BF16)

            summed = folded[at, :]
            table = per_head[at, :]
            grad_decay = dot(tri(True), summed, precision=HIGHEST)
            size = pltpu.roll(table, LANES - 3 * heads, 1)
            pre = pltpu.roll(table, LANES - 4 * heads, 1)
            grad_size = pltpu.roll(summed, LANES - heads, 1) - rate[...] * grad_decay
            valid = iota((SPAN, LANES), 1) < heads
            grad_pre = jnp.where(valid, grad_size * sigmoid(pre), 0.0)
            grad_step[at, :] = grad_pre.astype(BF16)
            grad_heads[0:1] += jnp.sum(grad_pre, axis=0, keepdims=True)
            grad_heads[1:2] += jnp.sum(-rate[...] * size * grad_decay, axis=0, keepdims=True)
            return 0

        lax.fori_loop(0, blocks, finish, 0)


def output_kernel(ks, rank, mixed, w_out, out):
    out[0] = dot(mixed[...], w_out[...]).astype(BF16)


def normed_kernel(ks, rank, grad_gate, grad_value, grad_state, grad_step, w_gate, w_value, w_state, w_step, out):
    total = dot(grad_gate[...], w_gate[...], NT) + dot(grad_value[...], w_value[...], NT)
    total = total + dot(grad_state[...], w_state[...], NT) + dot(grad_step[...], w_step[...], NT)
    out[0] = total.astype(BF16)


def swap(array, axis, mask):
    count = lax.axis_size(axis)
    return lax.ppermute(array, axis, [(i, i ^ mask) for i in range(count)])


def gather_pieces(own, parts):
    pieces = {0: own}
    bit = parts // 2
    while bit >= 1:
        pieces.update({k | bit: swap(piece, "tensor", bit) for k, piece in list(pieces.items())})
        bit //= 2
    return [pieces[k] for k in range(parts)]


def after(first, then):
    return lax.optimization_barrier((first, then))[1]


def sum_all(array, axis):
    bit = 1
    while bit < lax.axis_size(axis):
        array = array + swap(array, axis, bit)
        bit *= 2
    return array


def scatter_rest(own, received, dim, low_bits):
    count = lax.axis_size("dp")
    index = lax.axis_index("dp")
    left = count // 2
    place = ((index >> (low_bits + 1)) << low_bits) | (index & ((1 << low_bits) - 1))

    def original(mask):
        return ((mask >> low_bits) << (low_bits + 1)) | (mask & ((1 << low_bits) - 1))

    def cut(array, at, pieces):
        size = array.shape[dim] // pieces
        return lax.dynamic_slice_in_dim(array, at * size, size, dim)

    terms = [own] if received is None else [own, received]

    def total(at, pieces):
        return functools.reduce(jnp.add, [cut(term, at, pieces).astype(F32) for term in terms])

    while left > 4:
        half = left // 2
        top = (place // half) % 2
        sent = swap(total(1 - top, 2).astype(BF16), "dp", original(half))
        terms = [total(top, 2).astype(BF16), sent]
        left = half
    mine = place % left
    arrived = [swap(total(mine ^ k, left).astype(BF16), "dp", original(k)) for k in range(1, left)]
    result = total(mine, left)
    for piece in arrived:
        result = result + piece.astype(F32)
    return result


def shards(
    tokens,
    cotangent,
    doc_lengths,
    norm_gain,
    w_inner,
    w_step,
    w_state,
    conv_inner,
    conv_state,
    step_bias,
    log_rate,
    skip_gain,
    gate_gain,
    w_out,
):
    parts = lax.axis_size("tensor")
    groups = lax.axis_size("dp")
    rank = lax.axis_index("tensor").astype(jnp.int32)
    ranks = rank.reshape(1)
    length, quarter = tokens.shape
    width = quarter * parts
    channels = w_inner.shape[2]
    heads = w_step.shape[1]
    states2 = w_state.shape[1]
    states = states2 // 2
    blocks = length // SPAN
    steps = channels // GROUP
    repeat = LANES // heads
    piece_rows = width // groups
    low_bits = 0
    while (piece_rows << low_bits) < LANES:
        low_bits += 1
    run = piece_rows << low_bits
    half_width = width // 2
    place = ((lax.axis_index("dp") >> low_bits) & 1).astype(jnp.int32).reshape(1)

    token_pieces = gather_pieces(tokens, parts)
    grad_pieces = gather_pieces(after(token_pieces[parts // 2], cotangent), parts)
    full_grad = jnp.zeros((length, width), BF16)
    for k in range(parts):
        full_grad = lax.dynamic_update_slice(full_grad, grad_pieces[k], (0, (rank ^ k) * quarter))

    flat = w_inner.reshape(width, 2 * channels)
    step8 = jnp.tile(w_step, (1, repeat))
    step_pad = jnp.pad(w_step, ((0, 0), (0, LANES - heads)))
    bias8 = jnp.tile(step_bias, repeat)[None, :]
    rate8 = jnp.exp(jnp.tile(log_rate, repeat))[None, :]
    skip_row = jnp.repeat(skip_gain, channels // heads)[None, :]
    gain_row = gate_gain[None, :]
    conv_pad = jnp.pad(conv_inner, ((0, 3), (0, 0)))
    conv_state_pad = jnp.pad(conv_state, ((0, 3), (0, 0)))

    doc_ends = jnp.cumsum(doc_lengths[0])
    positions = jnp.arange(length, dtype=jnp.int32)
    segment = jnp.sum((positions[:, None] >= doc_ends[None, :]).astype(jnp.int32), axis=1)
    present = positions < doc_ends[-1]
    by_block = segment.reshape(blocks, SPAN)
    final = by_block[:, -1:]
    before = jnp.concatenate([jnp.full((1, 1), -1, jnp.int32), final[:-1]], axis=0)
    marks = [
        jnp.concatenate([jnp.full((k,), -1, jnp.int32), segment[:-k]]) == segment for k in (1, 2, 3)
    ]
    marks += [(by_block == before).reshape(-1), (by_block == final).reshape(-1), present]
    marks = [mark.astype(F32) for mark in marks] + [segment.astype(F32)]
    marks = jnp.pad(jnp.stack(marks, axis=1), ((0, 8), (0, LANES - len(marks))))
    seg_row = jnp.broadcast_to(segment.astype(F32)[None, :], (8, length))

    by_span = lambda cols: pl.BlockSpec((SPAN, cols), lambda b, *_: (b, 0))
    (normed, pre_state, maps, maps_t, per_head, rising_rows, cross, cross_t) = call(
        functools.partial(prep_kernel, parts, heads, steps),
        (blocks,),
        [by_span(quarter)] * parts
        + [
            held((1, width)), held((width, states2)), held((width, LANES)), held((8, states2)),
            held((1, LANES)), held((1, LANES)), by_span(LANES), pl.BlockSpec((8, SPAN), lambda b, *_: (0, b)),
        ],
        [
            by_span(width), by_span(states2), by_span(states2),
            pl.BlockSpec((states2, SPAN), lambda b, *_: (0, b)), by_span(LANES),
            pl.BlockSpec((steps, 8, SPAN), lambda b, *_: (0, b, 0)), by_span(SPAN), by_span(SPAN),
        ],
        [
            shape_of(length, width, dtype=BF16), shape_of(length, states2), shape_of(length, states2, dtype=BF16),
            shape_of(states2, length, dtype=BF16), shape_of(length, LANES), shape_of(steps, blocks * 8, SPAN),
            shape_of(length, SPAN), shape_of(length, SPAN),
        ],
        [pltpu.VMEM((8, states2), F32)],
        prefetch=1,
        flops=2 * length * width * (states2 + LANES),
        moved=length * width * 4 + width * (states2 + LANES) * 2 + length * 4000,
        name="prep",
    )(
        ranks, *token_pieces, norm_gain[None, :], w_state, step8, conv_state_pad, bias8, rate8, marks[:length], seg_row
    )
    pre_state = jnp.pad(pre_state, ((8, 0), (0, 0)))

    by_group = lambda rows: pl.BlockSpec((rows, GROUP), lambda g, *_: (0, g))
    w_rows = pl.BlockSpec((width, GROUP), lambda g, *_: (0, g))
    w_rows_value = pl.BlockSpec((width, GROUP), lambda g, *_: (0, steps + g))
    rows_spec = pl.BlockSpec((1, blocks * 8, SPAN), lambda g, *_: (g, 0, 0))
    memory_spec = pl.BlockSpec((blocks, states, GROUP), lambda g, *_: (0, 0, g))
    value, gate, mixer_out, memory, squares = call(
        functools.partial(forward_kernel, heads),
        (steps,),
        [
            held((length, width)), w_rows, w_rows_value, by_group(8), by_group(1), held((length, LANES)),
            held((length + 8, LANES)), rows_spec, held((length, states2)), held((states2, length)),
            held((length, SPAN)),
        ],
        [by_group(length + 8), by_group(length), by_group(length), memory_spec, held((length, LANES))],
        [
            shape_of(length + 8, channels), shape_of(length, channels), shape_of(length, channels),
            shape_of(blocks, states, channels, dtype=BF16), shape_of(length, LANES),
        ],
        [pltpu.VMEM((states, GROUP), F32)],
        flops=8 * length * width * channels,
        moved=length * width * 2 + width * channels * 4 + length * channels * 12,
        name="forward",
    )(
        normed, flat, flat, conv_pad, skip_row, per_head, marks, rising_rows, maps, maps_t, cross
    )

    grad_mixed, weighted = call(
        cotangent_kernel,
        (steps,),
        [
            held((length, width)), pl.BlockSpec((GROUP, width), lambda g, *_: (g, 0)),
            by_group(length), by_group(length), by_group(1),
        ],
        [by_group(length), held((length, LANES))],
        [shape_of(length, channels), shape_of(length, LANES)],
        flops=2 * length * width * channels,
        moved=length * width * 2 + width * channels * 2 + length * channels * 12,
        name="cotangent",
    )(full_grad, w_out, gate, mixer_out, gain_row)

    keep = marks[:length, 5]
    sums = jnp.stack([jnp.sum(squares, axis=1), jnp.sum(weighted, axis=1)])
    sums = sum_all(sums, "tensor")
    total_channels = channels * parts
    scale_out = lax.rsqrt(sums[0] / total_channels + EPSILON)
    factor = scale_out * keep
    pull = scale_out**3 * (sums[1] * keep) / total_channels
    factors = jnp.pad(jnp.stack([factor, pull], axis=1), ((0, 0), (0, LANES - 2)))

    by_channel = pl.BlockSpec((GROUP, half_width), lambda g, *_: (g, 0))
    low_mixed, grad_mixer, grad_gate, grad_gate_gain, out_send, out_own = call(
        functools.partial(gate_kernel, run),
        (steps,),
        [
            held((length, width)), by_group(length), by_group(length), by_group(length), by_group(1),
            held((length, LANES)),
        ],
        [by_group(length), by_group(length), by_group(length), by_group(1), by_channel, by_channel],
        [
            shape_of(length, channels, dtype=BF16), shape_of(length, channels, dtype=BF16),
            shape_of(length, channels, dtype=BF16), shape_of(1, channels),
            shape_of(channels, half_width, dtype=BF16), shape_of(channels, half_width, dtype=BF16),
        ],
        prefetch=1,
        flops=2 * length * width * channels,
        moved=length * width * 2 + length * channels * 18 + width * channels * 2,
        name="gate",
    )(place, full_grad, grad_mixed, gate, mixer_out, gain_row, factors)
    out_received = swap(out_send, "dp", 1 << low_bits)

    def weight_grads(right):
        runs = half_width // run
        columns = right.shape[1]
        out = pl.BlockSpec((run, columns), lambda j, p: (j, 0))
        shape = shape_of(half_width, columns, dtype=BF16)
        return call(
            weight_kernel,
            (runs,),
            [
                pl.BlockSpec((length, run), lambda j, p: (0, 2 * j + (p[0] ^ 1))),
                pl.BlockSpec((length, run), lambda j, p: (0, 2 * j + p[0])),
                held((length, columns)),
            ],
            [out, out],
            [shape, shape],
            prefetch=1,
            flops=2 * length * width * columns,
            moved=length * width * 2 + length * columns * 2 + width * columns * 2,
            name="weights",
        )(place, normed, normed, right)

    gate_send, gate_own = weight_grads(grad_gate)
    gate_received = swap(after(out_received, gate_send), "dp", 1 << low_bits)

    def output_part(ks):
        return call(
            functools.partial(output_kernel, ks),
            (len(ks), quarter // 256),
            [
                held((length, channels)),
                pl.BlockSpec(
                    (channels, 256),
                    lambda i, j, r: (0, (r[0] ^ (ks[0] + i * (ks[-1] - ks[0]))) * (quarter // 256) + j),
                ),
            ],
            pl.BlockSpec((1, length, 256), lambda i, j, r: (i, 0, j)),
            shape_of(len(ks), length, quarter, dtype=BF16),
            prefetch=1,
            flops=2 * length * channels * quarter * len(ks),
            moved=length * channels * 2 + channels * quarter * 2 * len(ks) + length * quarter * 2 * len(ks),
            name="output",
        )(ranks, low_mixed, w_out)

    out_far = swap(output_part((1, 3)), "tensor", 1)
    out_near = output_part((2, 0))
    out_y = swap((out_near[0].astype(F32) + out_far[1].astype(F32)).astype(BF16), "tensor", 2)
    branch = out_near[1].astype(F32) + out_far[0].astype(F32) + out_y.astype(F32)
    own_tokens = tokens.astype(F32)
    output = (own_tokens + branch).astype(BF16)

    all_lanes = held((length, LANES))
    (grad_value, grad_conv, grad_skip, grad_state, grad_step, grad_conv_state, grad_heads) = call(
        functools.partial(backward_kernel, heads, steps),
        (steps,),
        [
            by_group(length + 8), by_group(length), by_group(length), memory_spec, by_group(8), by_group(1),
            all_lanes, held((length + 8, LANES)), rows_spec, held((length, states2)), held((states2, length)),
            held((length, SPAN)), held((length, SPAN)), held((8, length)), held((length + 8, states2)),
            held((8, states2)), held((1, LANES)),
        ],
        [
            by_group(length), by_group(8), by_group(1), held((length, states2)), all_lanes,
            held((8, states2)), held((8, LANES)),
        ],
        [
            shape_of(length, channels, dtype=BF16), shape_of(8, channels), shape_of(1, channels),
            shape_of(length, states2, dtype=BF16), shape_of(length, LANES, dtype=BF16),
            shape_of(8, states2), shape_of(8, LANES),
        ],
        [
            pltpu.VMEM((8, GROUP), F32), pltpu.VMEM((states, GROUP), F32),
            pltpu.VMEM((length, SPAN), F32), pltpu.VMEM((length, LANES), F32),
            pltpu.VMEM((length, states2), F32), pltpu.VMEM((8, states2), F32),
        ],
        flops=40e9,
        moved=length * channels * 14,
        name="backward",
    )(
        value, grad_mixer, mixer_out, memory, conv_pad, skip_row, per_head, marks, rising_rows, maps, maps_t,
        cross, cross_t, seg_row, pre_state, conv_state_pad, rate8,
    )

    value_send, value_own = weight_grads(grad_value)
    value_received = swap(after(gate_received, value_send), "dp", 1 << low_bits)

    def normed_part(ks):
        def row(i, j, r):
            return (r[0] ^ (ks[0] + i * (ks[-1] - ks[0]))) * (quarter // 256) + j

        return call(
            functools.partial(normed_kernel, ks),
            (len(ks), quarter // 256),
            [
                held((length, channels)), held((length, channels)), held((length, states2)), held((length, LANES)),
                pl.BlockSpec((256, channels), lambda i, j, r: (row(i, j, r), 0)),
                pl.BlockSpec((256, channels), lambda i, j, r: (row(i, j, r), 1)),
                pl.BlockSpec((256, states2), lambda i, j, r: (row(i, j, r), 0)),
                pl.BlockSpec((256, LANES), lambda i, j, r: (row(i, j, r), 0)),
            ],
            pl.BlockSpec((1, length, 256), lambda i, j, r: (i, 0, j)),
            shape_of(len(ks), length, quarter, dtype=BF16),
            prefetch=1,
            flops=2 * length * (2 * channels + states2 + LANES) * quarter * len(ks),
            moved=length * channels * 4 + channels * quarter * 4 * len(ks) + length * quarter * 2 * len(ks),
            name="normed_grad",
        )(ranks, grad_gate, grad_value, grad_state, grad_step, flat, flat, w_state, step_pad)

    near_far = swap(normed_part((1, 3)), "tensor", 1)
    near = normed_part((2, 0))
    over_y = swap((near[0].astype(F32) + near_far[1].astype(F32)).astype(BF16), "tensor", 2)
    grad_normed = near[1].astype(F32) + near_far[0].astype(F32) + over_y.astype(F32)

    own_gain = lax.dynamic_slice_in_dim(norm_gain, rank * quarter, quarter, 0)
    scale_in = per_head[:, 5 * heads : 5 * heads + 1]
    row_norm = sum_all(jnp.sum(own_tokens * own_gain * grad_normed, axis=1), "tensor")
    grad_tokens = (
        cotangent.astype(F32)
        + scale_in * own_gain * grad_normed
        - own_tokens * scale_in**3 * row_norm[:, None] / width
    ).astype(BF16)
    grad_norm_gain = jnp.sum(grad_normed * own_tokens * scale_in, axis=0)

    state_all = grad_state
    for bit in (1, 2):
        state_all = (state_all.astype(F32) + swap(state_all, "tensor", bit).astype(F32)).astype(BF16)
    grad_w_state = dot(normed, state_all, TN).astype(BF16)
    own_rows = piece_rows // parts
    grad_w_state = lax.dynamic_slice_in_dim(
        grad_w_state.reshape(groups, parts, own_rows, states2), rank, 1, axis=1
    )
    grad_w_step = dot(grad_step[:, :heads], normed, TN).astype(BF16)
    grad_w_step = grad_w_step.reshape(heads, groups, piece_rows).transpose(1, 0, 2)
    small = jnp.concatenate(
        [grad_w_state.reshape(groups, own_rows * states2), grad_w_step.reshape(groups, heads * piece_rows)], axis=1
    ).reshape(groups // (2 << low_bits), 2, 1 << low_bits, -1)
    small_own = lax.dynamic_slice_in_dim(small, place[0], 1, 1).reshape(groups // 2, -1)
    small_send = lax.dynamic_slice_in_dim(small, 1 - place[0], 1, 1).reshape(groups // 2, -1)
    small_sum = scatter_rest(small_own, swap(small_send, "dp", 1 << low_bits), 0, low_bits)[0]
    sum_state = small_sum[: own_rows * states2].reshape(own_rows, states2)
    sum_step = small_sum[own_rows * states2 :].reshape(heads, piece_rows).T

    sum_out = scatter_rest(out_own, out_received, 1, low_bits)
    sum_gate = scatter_rest(gate_own, gate_received, 0, low_bits)
    sum_value = scatter_rest(value_own, value_received, 0, low_bits)
    sum_inner = jnp.stack([sum_gate, sum_value], axis=1)

    grad_conv_state = sum_all(grad_conv_state[:5], "tensor")
    skip_sums = jnp.sum(grad_skip.reshape(heads, channels // heads), axis=1)
    pack = [
        grad_norm_gain, grad_conv[:5].reshape(-1), grad_conv_state.reshape(-1),
        grad_heads[0, :heads], grad_heads[1, :heads], skip_sums, grad_gate_gain[0],
    ]
    sums_all = sum_all(jnp.concatenate(pack), "dp")
    split = []
    at = 0
    for piece in pack:
        split.append(sums_all[at : at + piece.shape[0]])
        at += piece.shape[0]
    return (
        output,
        grad_tokens,
        split[0],
        sum_inner,
        sum_step,
        sum_state,
        split[1].reshape(5, channels),
        split[2].reshape(5, states2),
        split[3],
        split[4],
        split[5],
        split[6],
        sum_out,
    )


def solution(mesh):
    placed = (
        P("dp", "tensor"),
        P("dp", "tensor"),
        P("dp", None),
        P(),
        P(None, None, "tensor"),
        P(None, "tensor"),
        P(),
        P(None, "tensor"),
        P(),
        P("tensor"),
        P("tensor"),
        P("tensor"),
        P("tensor"),
        P("tensor", None),
    )
    return jax.shard_map(
        shards,
        mesh=mesh,
        in_specs=placed,
        out_specs=(
            P("dp", "tensor"),
            P("dp", "tensor"),
            P("tensor"),
            P("dp", None, "tensor"),
            P("dp", "tensor"),
            P(("dp", "tensor"), None),
            P(None, "tensor"),
            P(),
            P("tensor"),
            P("tensor"),
            P("tensor"),
            P("tensor"),
            P("tensor", "dp"),
        ),
        check_vma=False,
    )
```

```python
import functools
import math

import jax
import jax.numpy as jnp
from jax import lax
from jax.experimental import pallas as pl
from jax.experimental.pallas import tpu as pltpu
from jax.sharding import PartitionSpec as P

F32 = jnp.float32
BF16 = jnp.bfloat16
HIGHEST = lax.Precision.HIGHEST
EPSILON = 1e-05
LOG2E = math.log2(math.e)
LANES = 128
SPAN = 128
GROUP = 256
UNROLL = 8
HINT = 0.02
ROWS = 512
CHUNKS = 2

NN = (((1,), (0,)), ((), ()))
NT = (((1,), (1,)), ((), ()))
TN = (((0,), (0,)), ((), ()))


def dot(left, right, dims=NN, precision=None):
    return lax.dot_general(left, right, dims, precision=precision, preferred_element_type=F32)


def sigmoid(a):
    return 0.5 * jnp.tanh(0.5 * a) + 0.5


def iota(shape, dim):
    return lax.broadcasted_iota(jnp.int32, shape, dim)


def tri(upper):
    rows, cols = iota((SPAN, SPAN), 0), iota((SPAN, SPAN), 1)
    return ((rows <= cols) if upper else (rows >= cols)).astype(F32)


def call(body, grid, in_specs, out_specs, out_shape, scratch=(), prefetch=0, flops=0, moved=0, name=None, vmem=56):
    return pl.pallas_call(
        body,
        grid_spec=pltpu.PrefetchScalarGridSpec(
            num_scalar_prefetch=prefetch,
            grid=grid,
            in_specs=in_specs,
            out_specs=out_specs,
            scratch_shapes=list(scratch),
        ),
        out_shape=out_shape,
        compiler_params=pltpu.CompilerParams(
            vmem_limit_bytes=vmem * 1024 * 1024, dimension_semantics=("arbitrary",) * len(grid)
        ),
        cost_estimate=pl.CostEstimate(
            flops=int(flops * HINT), bytes_accessed=int(moved * HINT), transcendentals=0
        ),
        name=name,
    )


def held(shape):
    zeros = (0,) * len(shape)
    return pl.BlockSpec(shape, lambda *_: zeros, pipeline_mode=pl.Buffered(1))


def shape_of(*dims, dtype=F32):
    return jax.ShapeDtypeStruct(dims, dtype)


def conv_taps(before, now, marks, filters):
    rows = now.shape[0]
    wide = jnp.concatenate([before, now], axis=0)
    total = filters[4:5] + filters[0:1] * now
    shifted = [now]
    for k in range(1, 4):
        moved = wide[8 - k : 8 - k + rows] * marks[:, k - 1 : k]
        shifted.append(moved)
        total = total + filters[k : k + 1] * moved
    return total, shifted


def rows_before(array, start):
    return array[pl.ds(pl.multiple_of(jnp.maximum(start - 8, 0), 8), 8), :]


def conv_back(later, marks, filters):
    rows = later.shape[0] - 8
    total = filters[0:1] * later[:rows]
    for k in range(1, 4):
        total = total + filters[k : k + 1] * (later[k : k + rows] * marks[k : k + rows, k - 1 : k])
    return total


def fold_lanes(power):
    folded = power[:, :LANES]
    for tile in range(1, power.shape[1] // LANES):
        folded = folded + power[:, tile * LANES : (tile + 1) * LANES]
    return folded


def spread(table, section, heads, count):
    lane = iota((table.shape[0], LANES), 1)
    tiles = []
    for pair in range(count // 2):
        at = section * heads + 2 * pair
        tiles.append(jnp.where(lane < LANES // 2, table[:, at : at + 1], table[:, at + 1 : at + 2]))
    return jnp.concatenate(tiles, axis=1)


def front_kernel(
    parts, heads, rank, *refs,
):
    pieces, refs = refs[:parts], refs[parts:]
    (gain, w_maps, conv_maps, bias, rate, seg_row, w_gate, w_value, conv, skip, marks,
     normed, pre_state, maps, maps_t, per_head, rows_out, cross_t, value, gate, mixed, low_gated, memory, squares,
     proj, cross, state) = refs
    g = pl.program_id(0)
    length, quarter = pieces[0].shape
    width = quarter * parts
    blocks = length // SPAN
    states = maps.shape[1] // 2
    count = GROUP // 64
    lane = iota((SPAN, LANES), 1)

    @pl.when(g == 0)
    def _():
        squares[...] = jnp.zeros_like(squares)

        def normalise(b, _):
            at = pl.ds(pl.multiple_of(b * SPAN, SPAN), SPAN)
            wide = [piece[at, :].astype(F32) for piece in pieces]
            total = functools.reduce(jnp.add, [array * array for array in wide])
            scale = lax.rsqrt(jnp.sum(total, axis=1, keepdims=True) / width + EPSILON)
            per_head[at, :] = jnp.broadcast_to(scale, (SPAN, LANES))
            for k in range(parts):
                to = pl.multiple_of((rank[0] ^ k) * quarter, quarter)
                normed[at, pl.ds(to, quarter)] = (wide[k] * scale * gain[:, pl.ds(to, quarter)]).astype(BF16)
            return 0

        lax.fori_loop(0, blocks, normalise, 0, unroll=2)
        proj[...] = dot(normed[...], w_maps[...])

        def tables(b, _):
            start = pl.multiple_of(b * SPAN, SPAN)
            at = pl.ds(start, SPAN)
            mark = marks[at, :]
            now = proj[at, : 2 * states]
            pre_state[at, :] = now
            total, _ = conv_taps(rows_before(proj, start)[:, : 2 * states], now, mark, conv_maps[...])
            both = total * sigmoid(total)
            keys, queries = both[:, :states], both[:, states:]
            low_keys, low_queries = keys.astype(BF16), queries.astype(BF16)
            maps[at, :states] = low_keys
            maps[at, states:] = low_queries
            maps_t[:states, pl.ds(start, SPAN)] = keys.T.astype(BF16)
            maps_t[states:, pl.ds(start, SPAN)] = queries.T.astype(BF16)

            pre = proj[at, 2 * states :] + bias[...]
            size = jnp.maximum(pre, 0.0) + jnp.log1p(jnp.exp(-jnp.abs(pre)))
            rising = dot(tri(False), -rate[...] * size, precision=HIGHEST)
            entering = jnp.exp(rising) * mark[:, 3:4]
            leaving = jnp.exp(rising[SPAN - 1 :] - rising) * mark[:, 4:5]
            rising = rising * LOG2E
            section = lane // heads
            packed = jnp.where(section == 0, rising, entering)
            packed = jnp.where(section == 2, leaving, packed)
            packed = jnp.where(section == 3, size, packed)
            packed = jnp.where(section == 4, pre, packed)
            packed = jnp.where(section == 5, per_head[at, :], packed)
            per_head[at, :] = packed
            turned = rising.T
            for group in range(rows_out.shape[0]):
                rows_out[group, pl.ds(pl.multiple_of(b * 8, 8), 8), :] = turned[group * count : group * count + 8]
            same = mark[:, 6:7] == seg_row[0:1, pl.ds(start, SPAN)]
            rows, cols = iota((SPAN, SPAN), 0), iota((SPAN, SPAN), 1)
            cross[at, :] = jnp.where(same & (rows >= cols), dot(low_queries, low_keys, NT), 0.0)
            cross_t[at, :] = jnp.where(same & (rows <= cols), dot(low_keys, low_queries, NT), 0.0)
            return 0

        lax.fori_loop(0, blocks, tables, 0, unroll=2)

    both = dot(normed[...], jnp.concatenate([w_gate[...], w_value[...]], axis=1))
    gate[...] = both[:, :GROUP].astype(BF16)
    value[...] = both[:, GROUP:]
    state[...] = jnp.zeros_like(state)
    turn = lax.rem(LANES - count * g, LANES)

    def block(b, _):
        start = pl.multiple_of(b * SPAN, SPAN)
        at = pl.ds(start, SPAN)
        total, _ = conv_taps(rows_before(value, start), value[at, :], marks[at, :], conv[...])
        inputs = total * sigmoid(total)
        table = pltpu.roll(per_head[at, :], turn, 1)
        entering, leaving, size = (spread(table, s, heads, count) for s in (1, 2, 3))
        scaled = inputs * size
        keys_t = maps_t[0:states, pl.ds(start, SPAN)]
        queries = maps[at, states:]
        low_state = state[...].astype(BF16)
        memory[b] = low_state
        out = entering * dot(queries, low_state) + skip[...] * inputs
        rising_rows = rows_out[g, pl.ds(pl.multiple_of(b * 8, 8), 8), :]
        crossed = cross[at, :]
        parts_out = []
        for pair in range(count // 2):
            weights = []
            for j in (2 * pair, 2 * pair + 1):
                gap = jnp.minimum(table[:, j : j + 1] - rising_rows[j : j + 1, :], 0.0)
                weights.append((jnp.exp2(gap) * crossed).astype(BF16))
            tile = scaled[:, pair * LANES : (pair + 1) * LANES]
            stacked = jnp.concatenate(
                [
                    jnp.where(lane < LANES // 2, tile, 0.0).astype(BF16),
                    jnp.where(lane < LANES // 2, 0.0, tile).astype(BF16),
                ],
                axis=0,
            )
            parts_out.append(dot(jnp.concatenate(weights, axis=1), stacked))
        out = out + jnp.concatenate(parts_out, axis=1)
        fresh = dot(keys_t, (leaving * scaled).astype(BF16))
        state[...] = state[...] * entering[SPAN - 1 :] + fresh
        mixed[at, :] = out
        opened = gate[at, :].astype(F32)
        gated = out * (opened * sigmoid(opened))
        low_gated[at, :] = gated.astype(BF16)
        squares[at, :] += fold_lanes(gated * gated)
        return 0

    lax.fori_loop(0, blocks, block, 0, unroll=UNROLL)


def assemble(pieces, target, sems, where):
    copies = [
        pltpu.make_async_copy(pieces[k].at[:, pl.ds(at, size)], target.at[:, pl.ds(to, size)], sems.at[i])
        for i, (k, at, to, size) in enumerate(where)
    ]
    for copy in copies:
        copy.start()
    for copy in copies:
        copy.wait()


def cotangent_kernel(parts, rank, *refs):
    pieces, (w_out, gated, gain, squares, grad, stats, sums, full, sems) = refs[:parts], refs[parts:]
    g = pl.program_id(0)
    length, quarter = pieces[0].shape

    @pl.when(g == 0)
    def _():
        sums[...] = jnp.zeros_like(sums)
        places = [pl.multiple_of((rank[0] ^ k) * quarter, quarter) for k in range(parts)]
        assemble(pieces, full, sems, [(k, 0, places[k], quarter) for k in range(parts)])

    grad[...] = dot(full[...], w_out[...], NT).astype(BF16)

    def chunk(i, _):
        at = pl.ds(pl.multiple_of(i * SPAN, SPAN), SPAN)
        sums[at, :] += fold_lanes(grad[at, :].astype(F32) * gated[at, :].astype(F32) * gain[...])
        return 0

    lax.fori_loop(0, length // SPAN, chunk, 0, unroll=2)

    @pl.when(g == pl.num_programs(0) - 1)
    def _():
        row = iota((8, LANES), 0)
        stats[...] = dot((row == 0).astype(F32), squares[...], NT, HIGHEST) + dot(
            (row == 1).astype(F32), sums[...], NT, HIGHEST
        )


def gate_kernel(
    parts, run, channels_all, place, rank, *refs,
):
    pieces, refs = refs[:parts], refs[parts:]
    (grad, gate, mixed, gain, stats, marks,
     low_mixed, grad_mixer, grad_gate, grad_gain, w_send, w_own, sent, kept, sems) = refs
    length, quarter = pieces[0].shape
    grad_gain[...] = jnp.zeros_like(grad_gain)
    pick = (iota((8, LANES), 0) == iota((8, LANES), 1)).astype(F32)
    pairs = quarter // (2 * run)
    bits = (parts * pairs - 1).bit_length()

    @pl.when(pl.program_id(0) == 0)
    def _():
        for half, target in ((1, sent), (0, kept)):
            where = []
            for k in range(parts):
                for j in range(pairs):
                    at = pl.multiple_of((2 * j + (place[0] ^ half)) * run, run)
                    to = turned((rank[0] ^ k) * pairs + j, bits) * run
                    where.append((k, at, pl.multiple_of(to, run), run))
            assemble(pieces, target, sems, where)

    def chunk(i, _):
        start = pl.multiple_of(i * SPAN, SPAN)
        at = pl.ds(start, SPAN)
        columns = dot(stats[:, pl.ds(start, SPAN)], pick, TN, HIGHEST)
        keep = marks[at, 5:6]
        scale = lax.rsqrt(columns[:, 0:1] / channels_all + EPSILON)
        factor = scale * keep
        pull = scale * scale * factor * columns[:, 1:2] / channels_all
        opened, out, now = gate[at, :].astype(F32), mixed[at, :], grad[at, :].astype(F32)
        chance = sigmoid(opened)
        swish = opened * chance
        gated = out * swish
        scaled = gated * factor
        low_mixed[at, :] = (scaled * gain[...]).astype(BF16)
        grad_gain[...] += jnp.sum(now * scaled, axis=0, keepdims=True)
        grad_gated = now * (factor * gain[...]) - gated * pull
        grad_mixer[at, :] = (grad_gated * swish).astype(BF16)
        grad_gate[at, :] = (grad_gated * out * chance * (1.0 + opened * (1.0 - chance))).astype(BF16)
        return 0

    lax.fori_loop(0, length // SPAN, chunk, 0, unroll=2)
    w_send[...] = dot(low_mixed[...], sent[...], TN).astype(BF16)
    w_own[...] = dot(low_mixed[...], kept[...], TN).astype(BF16)


def weight_kernel(place, left_send, left_own, *refs):
    parts = len(refs) // 3
    right = refs[:parts]
    for left, targets in ((left_send, refs[parts : 2 * parts]), (left_own, refs[2 * parts :])):
        for part, target in zip(right, targets):
            target[...] = dot(left[...], part[...], TN).astype(BF16)


def backward_kernel(
    heads, first, value, grad_out, mixed, memory, conv, skip, per_head, marks, rows_in, maps, maps_t, cross_t,
    grad_value, grad_conv, grad_skip, grad_cross, folded, grad_maps,
    later, grad_memory,
):
    g = pl.program_id(0) + first
    length = grad_out.shape[0]
    blocks = length // SPAN
    states = maps.shape[1] // 2
    count = GROUP // 64
    lane = iota((SPAN, LANES), 1)
    row = iota((SPAN, GROUP), 0)
    turn = lax.rem(LANES - count * g, LANES)
    channel, target = iota((GROUP, LANES), 0), iota((GROUP, LANES), 1)
    pick_rise = (target == count * g + channel // 64).astype(BF16)
    pick_size = (target == heads + count * g + channel // 64).astype(BF16)
    later[...] = jnp.zeros_like(later)
    grad_memory[...] = jnp.zeros_like(grad_memory)
    grad_conv[...] = jnp.zeros_like(grad_conv)
    grad_skip[...] = jnp.zeros_like(grad_skip)

    @pl.when(g == first)
    def _():
        grad_cross[...] = jnp.zeros_like(grad_cross)
        folded[...] = jnp.zeros_like(folded)
        grad_maps[...] = jnp.zeros_like(grad_maps)

    def block(i, _):
        b = blocks - 1 - i
        start = pl.multiple_of(b * SPAN, SPAN)
        at = pl.ds(start, SPAN)
        filters = conv[...]
        total, shifted = conv_taps(rows_before(value, start), value[at, :], marks[at, :], filters)
        chance = sigmoid(total)
        inputs = total * chance
        table = pltpu.roll(per_head[at, :], turn, 1)
        entering, leaving, size = (spread(table, s, heads, count) for s in (1, 2, 3))
        scaled = inputs * size
        low_scaled = scaled.astype(BF16)
        pulled = grad_out[at, :].astype(F32)
        keys, queries_t = maps[at, 0:states], maps_t[states:, pl.ds(start, SPAN)]
        memory_now = memory[b]
        grad_next = grad_memory[...]
        low_next = grad_next.astype(BF16)
        entered = (entering * pulled).astype(BF16)
        left = (leaving * scaled).astype(BF16)
        grad_maps[at, 0:states] += dot(left, low_next, NT)
        grad_maps[at, states:] += dot(entered, memory_now, NT)
        rising_rows = rows_in[0, pl.ds(pl.multiple_of(b * 8, 8), 8), :]
        crossed_t = cross_t[at, :]
        cross_sum = jnp.zeros((SPAN, SPAN), F32)
        parts = []
        for pair in range(count // 2):
            tile = pulled[:, pair * LANES : (pair + 1) * LANES]
            one = jnp.where(lane < LANES // 2, tile, 0.0).astype(BF16)
            two = jnp.where(lane < LANES // 2, 0.0, tile).astype(BF16)
            low_tile = low_scaled[:, pair * LANES : (pair + 1) * LANES]
            weights = []
            for j, masked in ((2 * pair, one), (2 * pair + 1, two)):
                gap = table[:, j : j + 1] - rising_rows[j : j + 1, :]
                cross_sum = cross_sum + jnp.exp2(jnp.minimum(gap, 0.0)) * dot(masked, low_tile, NT)
                weights.append((jnp.exp2(jnp.minimum(-gap, 0.0)) * crossed_t).astype(BF16))
            parts.append(dot(jnp.concatenate(weights, axis=1), jnp.concatenate([one, two], axis=0)))
        grad_cross[at, :] += cross_sum
        grad_within = jnp.concatenate(parts, axis=1)
        grad_left = dot(keys, low_next)
        grad_scaled = grad_within + leaving * grad_left
        scanned = mixed[at, :] - skip[...] * inputs
        kept = left.astype(F32) * grad_left
        rise = pulled * scanned - low_scaled.astype(F32) * grad_within - kept
        carried = entering[SPAN - 1 :] * jnp.sum(low_next.astype(F32) * memory_now.astype(F32), axis=0, keepdims=True)
        rise = rise + jnp.where(row == SPAN - 1, carried + jnp.sum(kept, axis=0, keepdims=True), 0.0)
        grown = grad_scaled * inputs
        summed = folded[at, :]
        for product, pick in ((rise, pick_rise), (grown, pick_size)):
            high = product.astype(BF16)
            rest = (product - high.astype(F32)).astype(BF16)
            summed = summed + dot(high, pick) + dot(rest, pick)
        folded[at, :] = summed
        grad_skip[...] += jnp.sum(pulled * inputs, axis=0, keepdims=True)
        grad_inputs = size * grad_scaled + skip[...] * pulled
        grad_total = grad_inputs * (chance * (1.0 + total * (1.0 - chance)))
        for k in range(4):
            grad_conv[k : k + 1] += jnp.sum(grad_total * shifted[k], axis=0, keepdims=True)
        grad_conv[4:5] += jnp.sum(grad_total, axis=0, keepdims=True)
        longer = jnp.concatenate([grad_total, later[...]], axis=0)
        later[...] = grad_total[:8]
        grad_value[at, :] = conv_back(longer, marks[pl.ds(start, SPAN + 8), :], filters).astype(BF16)
        grad_memory[...] = entering[SPAN - 1 :] * grad_next + dot(queries_t, entered)
        return 0

    lax.fori_loop(0, blocks, block, 0, unroll=UNROLL)


def finish_kernel(
    heads, calls, *refs,
):
    summed_parts, refs = refs[: 3 * calls], refs[3 * calls :]
    (per_head, marks, maps, seg_row, pre_state, conv_state, rate,
     grad_state, grad_step, grad_conv_state, grad_heads, later) = refs
    length = maps.shape[0]
    blocks = length // SPAN
    states = maps.shape[1] // 2
    later[...] = jnp.zeros_like(later)
    grad_conv_state[...] = jnp.zeros_like(grad_conv_state)
    grad_heads[...] = jnp.zeros_like(grad_heads)

    def block(i, _):
        start = pl.multiple_of((blocks - 1 - i) * SPAN, SPAN)
        at = pl.ds(start, SPAN)
        mark = marks[at, :]
        rows, cols = iota((SPAN, SPAN), 0), iota((SPAN, SPAN), 1)
        linked = (rows >= cols) & (mark[:, 6:7] == seg_row[0:1, pl.ds(start, SPAN)])
        grad_cross, summed, grad_maps = (
            functools.reduce(jnp.add, [ref[at, :] for ref in summed_parts[j::3]]) for j in range(3)
        )
        crossed = jnp.where(linked, grad_cross, 0.0)
        keys, queries = maps[at, 0:states], maps[at, states:]
        grad_keys = grad_maps[:, :states] + dot(crossed.T.astype(BF16), queries)
        grad_queries = grad_maps[:, states:] + dot(crossed.astype(BF16), keys)
        filters = conv_state[...]
        total, shifted = conv_taps(rows_before(pre_state, start), pre_state[at, :], mark, filters)
        chance = sigmoid(total)
        grad_total = jnp.concatenate([grad_keys, grad_queries], axis=1) * (chance * (1.0 + total * (1.0 - chance)))
        for k in range(4):
            grad_conv_state[k : k + 1] += jnp.sum(grad_total * shifted[k], axis=0, keepdims=True)
        grad_conv_state[4:5] += jnp.sum(grad_total, axis=0, keepdims=True)
        longer = jnp.concatenate([grad_total, later[...]], axis=0)
        later[...] = grad_total[:8]
        grad_state[at, :] = conv_back(longer, marks[pl.ds(start, SPAN + 8), :], filters).astype(BF16)

        table = per_head[at, :]
        grad_decay = dot(tri(True), summed, precision=HIGHEST)
        size = pltpu.roll(table, LANES - 3 * heads, 1)
        pre = pltpu.roll(table, LANES - 4 * heads, 1)
        grad_size = pltpu.roll(summed, LANES - heads, 1) - rate[...] * grad_decay
        valid = iota((SPAN, LANES), 1) < heads
        grad_pre = jnp.where(valid, grad_size * sigmoid(pre), 0.0)
        grad_step[at, :] = grad_pre.astype(BF16)
        grad_heads[0:1] += jnp.sum(grad_pre, axis=0, keepdims=True)
        grad_heads[1:2] += jnp.sum(-rate[...] * size * grad_decay, axis=0, keepdims=True)
        return 0

    lax.fori_loop(0, blocks, block, 0, unroll=UNROLL)


def output_kernel(chunks, rank, *refs):
    mixed, w_out, out = refs[:chunks], refs[chunks], refs[chunks + 1]
    size = mixed[0].shape[1]
    total = dot(mixed[0][...], w_out[:size])
    for c in range(1, chunks):
        total = total + dot(mixed[c][...], w_out[c * size : (c + 1) * size])
    out[0] = total.astype(BF16)


def normed_kernel(chunks, rank, *refs):
    grads, (grad_state, grad_step, w_inner, w_state, w_step, out) = refs[: 2 * chunks], refs[2 * chunks :]
    total = dot(grad_state[...], w_state[...], NT) + dot(grad_step[...], w_step[...], NT)
    at = 0
    for part in grads:
        size = part.shape[1]
        total = total + dot(part[...], w_inner[:, at : at + size], NT)
        at += size
    out[0] = total.astype(BF16)


def swap(array, axis, mask):
    count = lax.axis_size(axis)
    return lax.ppermute(array, axis, [(i, i ^ mask) for i in range(count)])


def gather_pieces(own, parts):
    pieces = {0: own}
    bit = parts // 2
    while bit >= 1:
        pieces.update({k | bit: swap(piece, "tensor", bit) for k, piece in list(pieces.items())})
        bit //= 2
    return [pieces[k] for k in range(parts)]


def tie(array, *first):
    return lax.optimization_barrier((array, *first))[0]


def meet(sums, *arrays):
    arrays = lax.optimization_barrier((*arrays, *(part.got for part in sums)))
    for part, got in zip(sums, arrays[len(arrays) - len(sums) :]):
        part.got = got
    return arrays[: len(arrays) - len(sums)]


def sum_all(array, axis):
    bit = 1
    while bit < lax.axis_size(axis):
        array = array + swap(array, axis, bit)
        bit *= 2
    return array


def rest_masks(low_bits):
    bits = (lax.axis_size("dp") - 1).bit_length()
    return [1 << bit for bit in (*range(low_bits + 1, bits), *range(low_bits - 1, -1, -1))]


def turned(index, bits):
    result = index * 0
    for bit in range(bits):
        result = result | (((index >> bit) & 1) << (bits - 1 - bit))
    return result


class Sum:
    def __init__(self, own, got, dim, low_bits):
        self.terms, self.got, self.dim, self.masks = [own], got, dim, rest_masks(low_bits)

    def advance(self):
        self.terms.append(self.got)
        mask = self.masks.pop(0)
        top = (lax.axis_index("dp") & mask) // mask
        size = self.terms[0].shape[self.dim] // 2

        def cut(half):
            return [lax.dynamic_slice_in_dim(term, half * size, size, self.dim) for term in self.terms]

        sent = functools.reduce(jnp.add, [term.astype(F32) for term in cut(1 - top)]).astype(BF16)
        self.terms, self.got = cut(top), swap(sent, "dp", mask)
        return sent

    def result(self):
        while self.masks:
            self.advance()
        return functools.reduce(jnp.add, [term.astype(F32) for term in (*self.terms, self.got)])


def add_low(left, right):
    return (left.astype(F32) + right.astype(F32)).astype(BF16)


def shards(
    tokens,
    cotangent,
    doc_lengths,
    norm_gain,
    w_inner,
    w_step,
    w_state,
    conv_inner,
    conv_state,
    step_bias,
    log_rate,
    skip_gain,
    gate_gain,
    w_out,
):
    parts = lax.axis_size("tensor")
    groups = lax.axis_size("dp")
    rank = lax.axis_index("tensor").astype(jnp.int32)
    ranks = rank.reshape(1)
    length, quarter = tokens.shape
    width = quarter * parts
    channels = w_inner.shape[2]
    heads = w_step.shape[1]
    states2 = w_state.shape[1]
    states = states2 // 2
    blocks = length // SPAN
    steps = channels // GROUP
    repeat = LANES // heads
    piece_rows = width // groups
    low_bits = 0
    while (piece_rows << low_bits) < LANES:
        low_bits += 1
    run = piece_rows << low_bits
    half_width = width // 2
    high_bits = (groups - 1).bit_length() - 1 - low_bits
    place = ((lax.axis_index("dp") >> low_bits) & 1).astype(jnp.int32).reshape(1)

    token_y = swap(tokens, "tensor", 2)
    grad_y = swap(tie(cotangent, token_y), "tensor", 2)
    flat = w_inner.reshape(width, 2 * channels)
    w_maps = jnp.concatenate([w_state, jnp.tile(w_step, (1, repeat))], axis=1)
    step_pad = jnp.pad(w_step, ((0, 0), (0, LANES - heads)))
    bias8 = jnp.tile(step_bias, repeat)[None, :]
    rate8 = jnp.exp(jnp.tile(log_rate, repeat))[None, :]
    skip_row = jnp.repeat(skip_gain, channels // heads)[None, :]
    gain_row = gate_gain[None, :]
    conv_pad = jnp.pad(conv_inner, ((0, 3), (0, 0)))
    conv_state_pad = jnp.pad(conv_state, ((0, 3), (0, 0)))

    doc_ends = jnp.cumsum(doc_lengths[0])
    positions = jnp.arange(length, dtype=jnp.int32)
    segment = jnp.sum((positions[:, None] >= doc_ends[None, :]).astype(jnp.int32), axis=1)
    present = positions < doc_ends[-1]
    by_block = segment.reshape(blocks, SPAN)
    final = by_block[:, -1:]
    before = jnp.concatenate([jnp.full((1, 1), -1, jnp.int32), final[:-1]], axis=0)
    marks = [
        jnp.concatenate([jnp.full((k,), -1, jnp.int32), segment[:-k]]) == segment for k in (1, 2, 3)
    ]
    marks += [(by_block == before).reshape(-1), (by_block == final).reshape(-1), present]
    marks = [mark.astype(F32) for mark in marks] + [segment.astype(F32)]
    marks = jnp.pad(jnp.stack(marks, axis=1), ((0, 8), (0, LANES - len(marks))))
    seg_row = jnp.broadcast_to(segment.astype(F32)[None, :], (8, length))

    token_y, flat, w_maps, step_pad, marks, seg_row, skip_row, conv_pad = lax.optimization_barrier(
        (token_y, flat, w_maps, step_pad, marks, seg_row, skip_row, conv_pad)
    )
    token_pieces = [tokens, swap(tokens, "tensor", 1), token_y, swap(token_y, "tensor", 1)]

    by_group = lambda rows: pl.BlockSpec((rows, GROUP), lambda g, *_: (0, g))
    (normed, pre_state, maps, maps_t, per_head, rising_rows, cross_t, value, gate, mixer_out, low_gated, memory, squares) = call(
        functools.partial(front_kernel, parts, heads),
        (steps,),
        [held((length, quarter))] * parts
        + [
            held((1, width)), held((width, states2 + LANES)), held((8, states2)),
            held((1, LANES)), held((1, LANES)), held((8, length)),
            pl.BlockSpec((width, GROUP), lambda g, *_: (0, g)), pl.BlockSpec((width, GROUP), lambda g, *_: (0, steps + g)),
            by_group(8), by_group(1), held((length + 8, LANES)),
        ],
        [
            held((length, width)), held((length, states2)), held((length, states2)), held((states2, length)),
            held((length, LANES)), held((steps, blocks * 8, SPAN)), held((length, SPAN)),
            by_group(length), by_group(length), by_group(length), by_group(length),
            pl.BlockSpec((blocks, states, GROUP), lambda g, *_: (0, 0, g)), held((length, LANES)),
        ],
        [
            shape_of(length, width, dtype=BF16), shape_of(length, states2), shape_of(length, states2, dtype=BF16),
            shape_of(states2, length, dtype=BF16), shape_of(length, LANES), shape_of(steps, blocks * 8, SPAN),
            shape_of(length, SPAN), shape_of(length, channels), shape_of(length, channels, dtype=BF16),
            shape_of(length, channels), shape_of(length, channels, dtype=BF16),
            shape_of(blocks, states, channels, dtype=BF16), shape_of(length, LANES),
        ],
        [
            pltpu.VMEM((length, states2 + LANES), F32), pltpu.VMEM((length, SPAN), F32),
            pltpu.VMEM((states, GROUP), F32),
        ],
        prefetch=1,
        flops=8 * length * width * channels,
        moved=length * width * 4 + width * channels * 4 + length * channels * 14,
        name="front",
        vmem=56,
    )(
        ranks, *token_pieces, norm_gain[None, :], w_maps, conv_state_pad, bias8, rate8, seg_row, flat, flat, conv_pad,
        skip_row, marks,
    )

    grad_y = tie(grad_y, squares)
    grad_pieces = [cotangent, swap(cotangent, "tensor", 1), grad_y, swap(grad_y, "tensor", 1)]
    pieces_any = [pl.BlockSpec(memory_space=pl.ANY)] * parts
    double = 2 * GROUP
    by_double = lambda rows: pl.BlockSpec((rows, double), lambda g, *_: (0, g))
    grad_mixed, stats = call(
        functools.partial(cotangent_kernel, parts),
        (channels // double,),
        pieces_any
        + [
            pl.BlockSpec((double, width), lambda g, *_: (g, 0)),
            by_double(length), by_double(1), held((length, LANES)),
        ],
        [by_double(length), held((8, length))],
        [shape_of(length, channels, dtype=BF16), shape_of(8, length)],
        [pltpu.VMEM((length, LANES), F32), pltpu.VMEM((length, width), BF16), pltpu.SemaphoreType.DMA((parts,))],
        prefetch=1,
        flops=2 * length * width * channels,
        moved=length * width * 2 + width * channels * 2 + length * channels * 12,
        name="cotangent",
        vmem=56,
    )(ranks, *grad_pieces, w_out, low_gated, gain_row, squares)
    stats = sum_all(stats, "tensor")

    spans = steps // CHUNKS

    def chunk_spec(rows, c):
        return pl.BlockSpec((rows, GROUP), lambda g, *_: (0, c * spans + g))

    def gate_part(c, stats):
        size = spans * GROUP
        by_channel = pl.BlockSpec((GROUP, half_width), lambda g, *_: (g, 0))
        return call(
            functools.partial(gate_kernel, parts, run, channels * parts),
            (spans,),
            pieces_any
            + [
                chunk_spec(length, c), chunk_spec(length, c), chunk_spec(length, c), chunk_spec(1, c),
                held((8, length)), held((length + 8, LANES)),
            ],
            [by_group(length), by_group(length), by_group(length), by_group(1), by_channel, by_channel],
            [
                shape_of(length, size, dtype=BF16), shape_of(length, size, dtype=BF16),
                shape_of(length, size, dtype=BF16), shape_of(1, size),
                shape_of(size, half_width, dtype=BF16), shape_of(size, half_width, dtype=BF16),
            ],
            [
                pltpu.VMEM((length, half_width), BF16), pltpu.VMEM((length, half_width), BF16),
                pltpu.SemaphoreType.DMA((half_width // run,)),
            ],
            prefetch=2,
            flops=2 * length * width * size,
            moved=length * width * 2 + length * size * 18 + width * size * 2,
            name="gate",
            vmem=56,
        )(place, ranks, *grad_pieces, grad_mixed, gate, mixer_out, gain_row, stats, marks)

    def weight_part(*right):
        runs = half_width // run
        columns = [part.shape[1] for part in right]
        outs = [pl.BlockSpec((run, size), lambda j, p: (turned(j, (runs - 1).bit_length()), 0)) for size in columns]
        shapes = [shape_of(half_width, size, dtype=BF16) for size in columns]
        result = call(
            weight_kernel,
            (runs,),
            [
                pl.BlockSpec((length, run), lambda j, p: (0, 2 * j + (p[0] ^ 1))),
                pl.BlockSpec((length, run), lambda j, p: (0, 2 * j + p[0])),
            ]
            + [held((length, size)) for size in columns],
            outs + outs,
            shapes + shapes,
            prefetch=1,
            flops=2 * length * width * sum(columns),
            moved=length * width * 2 + length * sum(columns) * 2 + width * sum(columns) * 2,
            name="weights",
        )(place, normed, normed, *right)
        return result[: len(columns)], result[len(columns) :]

    all_lanes = held((length, LANES))

    def backward_part(c, grad_out):
        size = spans * GROUP
        return call(
            functools.partial(backward_kernel, heads, c * spans),
            (spans,),
            [
                chunk_spec(length, c), by_group(length), chunk_spec(length, c),
                pl.BlockSpec((blocks, states, GROUP), lambda g, *_: (0, 0, c * spans + g)),
                chunk_spec(8, c), chunk_spec(1, c), all_lanes, held((length + 8, LANES)),
                pl.BlockSpec((1, blocks * 8, SPAN), lambda g, *_: (c * spans + g, 0, 0)),
                held((length, states2)), held((states2, length)), held((length, SPAN)),
            ],
            [by_group(length), by_group(8), by_group(1), held((length, SPAN)), all_lanes, held((length, states2))],
            [
                shape_of(length, size, dtype=BF16), shape_of(8, size), shape_of(1, size),
                shape_of(length, SPAN), shape_of(length, LANES), shape_of(length, states2),
            ],
            [pltpu.VMEM((8, GROUP), F32), pltpu.VMEM((states, GROUP), F32)],
            flops=40e9 / CHUNKS,
            moved=length * size * 14,
            name="backward",
            vmem=56,
        )(
            value, grad_out, mixer_out, memory, conv_pad, skip_row, per_head, marks, rising_rows, maps, maps_t,
            cross_t,
        )

    def output_part(ks, mixed):
        return call(
            functools.partial(output_kernel, len(mixed)),
            (len(ks), quarter // 256),
            [held((length, mixed[0].shape[1]))] * len(mixed)
            + [
                pl.BlockSpec(
                    (channels, 256),
                    lambda i, j, r: (0, (r[0] ^ (ks[0] + i * (ks[-1] - ks[0]))) * (quarter // 256) + j),
                ),
            ],
            pl.BlockSpec((1, length, 256), lambda i, j, r: (i, 0, j)),
            shape_of(len(ks), length, quarter, dtype=BF16),
            prefetch=1,
            flops=2 * length * channels * quarter * len(ks),
            moved=length * channels * 2 + channels * quarter * 2 * len(ks) + length * quarter * 2 * len(ks),
            name="output",
        )(ranks, *mixed, w_out)

    def normed_part(ks, grad_gate, grad_value):
        def row(i, j, r):
            return (r[0] ^ (ks[0] + i * (ks[-1] - ks[0]))) * (quarter // 256) + j

        return call(
            functools.partial(normed_kernel, len(grad_gate)),
            (len(ks), quarter // 256),
            [held((length, part.shape[1])) for part in (*grad_gate, *grad_value)]
            + [
                held((length, states2)), held((length, LANES)),
                pl.BlockSpec((256, 2 * channels), lambda i, j, r: (row(i, j, r), 0)),
                pl.BlockSpec((256, states2), lambda i, j, r: (row(i, j, r), 0)),
                pl.BlockSpec((256, LANES), lambda i, j, r: (row(i, j, r), 0)),
            ],
            pl.BlockSpec((1, length, 256), lambda i, j, r: (i, 0, j)),
            shape_of(len(ks), length, quarter, dtype=BF16),
            prefetch=1,
            flops=2 * length * (2 * channels + states2 + LANES) * quarter * len(ks),
            moved=length * channels * 4 + channels * quarter * 4 * len(ks) + length * quarter * 2 * len(ks),
            name="normed_grad",
        )(ranks, *grad_gate, *grad_value, grad_state, grad_step, flat, w_state, step_pad)

    def over_x(send):
        return swap(send, "dp", 1 << low_bits)

    chunks = range(CHUNKS)
    gates, sum_out = [], []
    last = stats
    for c in chunks:
        gates.append(gate_part(c, tie(stats, last)))
        sum_out.append(Sum(gates[c][5], over_x(gates[c][4]), 1, low_bits))
        last = gates[c][5]
    low_mixed, grad_mixer, grad_gate, grad_gain, _, _ = zip(*gates)
    gate_send, gate_own = weight_part(tie(grad_gate[0], last), *grad_gate[1:])
    out_far = output_part((1, 3), [tie(low_mixed[0], gate_send[0]), *low_mixed[1:]])

    out_far, send = meet(sum_out[:1], out_far, gate_send[0])
    sum_gate = [Sum(gate_own[0], over_x(send), 0, low_bits)]
    out_far_got = swap(out_far, "tensor", 1)
    moved = [sum_out[0].advance(), out_far, send]
    out_near = output_part((2, 0), [tie(low_mixed[0], *moved), *low_mixed[1:]])
    back = backward_part(0, tie(grad_mixer[0], out_near))
    (value_send,), (value_own,) = weight_part(back[0])

    value_own, out_far_got, send = meet(sum_out, value_own, out_far_got, gate_send[1])
    sum_gate.append(Sum(gate_own[1], over_x(send), 0, low_bits))
    out_sum = add_low(out_near[0], out_far_got[1])
    out_y = swap(out_sum, "tensor", 2)
    moved = [sum_out[0].advance(), sum_out[1].advance(), out_sum, send, value_own]
    backs = [back, backward_part(1, tie(grad_mixer[1], *moved))]
    (value_send2,), (value_own2,) = weight_part(backs[1][0])

    value_own2, out_y, value_send = meet([*sum_out, sum_gate[0]], value_own2, out_y, value_send)
    sum_value = [Sum(value_own, over_x(value_send), 0, low_bits)]
    moved = [sum_gate[0].advance(), sum_out[1].advance(), value_send, value_own2]
    grad_value, grad_conv, grad_skip, cross_parts, folded_parts, maps_parts = zip(*backs)
    (grad_state, grad_step, grad_conv_state, grad_heads) = call(
        functools.partial(finish_kernel, heads, CHUNKS),
        (1,),
        [held((length, SPAN)), all_lanes, held((length, states2))] * CHUNKS
        + [
            all_lanes, held((length + 8, LANES)), held((length, states2)), held((8, length)),
            held((length, states2)), held((8, states2)), held((1, LANES)),
        ],
        [held((length, states2)), all_lanes, held((8, states2)), held((8, LANES))],
        [
            shape_of(length, states2, dtype=BF16), shape_of(length, LANES, dtype=BF16),
            shape_of(8, states2), shape_of(8, LANES),
        ],
        [pltpu.VMEM((8, states2), F32)],
        flops=4e9,
        moved=length * 2048 * CHUNKS + length * 5000,
        name="finish",
        vmem=56,
    )(
        tie(cross_parts[0], *moved), folded_parts[0], maps_parts[0],
        *[part for three in zip(cross_parts[1:], folded_parts[1:], maps_parts[1:]) for part in three],
        per_head, marks, maps, seg_row, pre_state, conv_state_pad, rate8,
    )


    grad_state, value_send2 = meet(sum_gate, grad_state, value_send2)
    sum_value.append(Sum(value_own2, over_x(value_send2), 0, low_bits))
    state_got = swap(grad_state, "tensor", 1)
    total_out = [sum_out[0].result()]
    moved = [sum_gate[0].advance(), sum_gate[1].advance(), total_out[0], value_send2]
    near_far = normed_part((1, 3), [tie(grad_gate[0], *moved), *grad_gate[1:]], grad_value)

    near_far, state_got = meet(sum_out[1:], near_far, state_got)
    state_sum = add_low(grad_state, state_got)
    state_got = swap(state_sum, "tensor", 2)
    near_far_got = swap(near_far, "tensor", 1)
    total_out.append(sum_out[1].result())
    near = normed_part((2, 0), [tie(grad_gate[0], near_far, state_sum, total_out[1]), *grad_gate[1:]], grad_value)

    near, near_far_got, state_got = meet(sum_gate, near, near_far_got, state_got)
    near_sum = add_low(near[0], near_far_got[1])
    over_y = swap(near_sum, "tensor", 2)
    total_gate = [sum_gate[0].result()]
    moved = [sum_gate[1].advance()]
    state_all = tie(add_low(state_sum, state_got), near_sum, *total_gate, *moved)
    grad_step, norm_gain, grad_conv_state, grad_heads, normed = lax.optimization_barrier(
        (grad_step, norm_gain, grad_conv_state, grad_heads, normed, state_all)
    )[:-1]

    branch = out_near[1].astype(F32) + out_far_got[0].astype(F32) + out_y.astype(F32)
    own_tokens = tokens.astype(F32)
    output = (own_tokens + branch).astype(BF16)

    grad_w_state = dot(normed, state_all, TN).astype(BF16)
    own_rows = piece_rows // parts
    grad_w_state = lax.dynamic_slice_in_dim(
        grad_w_state.reshape(groups, parts, own_rows, states2), rank, 1, axis=1
    )
    grad_w_step = dot(grad_step[:, :heads], normed, TN).astype(BF16)
    grad_w_step = grad_w_step.reshape(heads, groups, piece_rows).transpose(1, 0, 2)
    small = jnp.concatenate(
        [grad_w_state.reshape(groups, own_rows * states2), grad_w_step.reshape(groups, heads * piece_rows)], axis=1
    ).reshape(groups // (2 << low_bits), 2, 1 << low_bits, -1)
    small = jnp.stack([small[turned(j, high_bits)] for j in range(small.shape[0])])
    small_own = lax.dynamic_slice_in_dim(small, place[0], 1, 1).reshape(groups // 2, -1)
    small_send = lax.dynamic_slice_in_dim(small, 1 - place[0], 1, 1).reshape(groups // 2, -1)
    small_sum = Sum(small_own, over_x(small_send), 0, low_bits)
    (small_send,) = meet([*sum_value[:1], *sum_gate[1:]], small_send)
    total_gate.append(sum_gate[1].result())
    moved = [sum_value[0].advance(), total_gate[1], small_send]
    over_y, *_ = meet([*sum_value, small_sum], over_y, *moved)
    moved = [sum_value[1].advance(), sum_value[0].advance(), small_sum.advance()]
    grad_normed = near[1].astype(F32) + near_far_got[0].astype(F32) + over_y.astype(F32)
    own_gain = lax.dynamic_slice_in_dim(norm_gain, rank * quarter, quarter, 0)
    scale_in = per_head[:, 5 * heads : 5 * heads + 1]
    row_norm = sum_all(jnp.sum(own_tokens * own_gain * grad_normed, axis=1), "tensor")
    grad_tokens = (
        cotangent.astype(F32)
        + scale_in * own_gain * grad_normed
        - own_tokens * scale_in**3 * row_norm[:, None] / width
    ).astype(BF16)
    grad_norm_gain = jnp.sum(grad_normed * own_tokens * scale_in, axis=0)

    moved = meet([sum_value[1], small_sum], grad_tokens, *moved)
    grad_tokens = moved[0]
    moved = [sum_value[1].advance(), small_sum.advance()]
    small_sum = small_sum.result()[0]
    sum_state = small_sum[: own_rows * states2].reshape(own_rows, states2)
    sum_step = small_sum[own_rows * states2 :].reshape(heads, piece_rows).T

    total_value = [part.result() for part in sum_value]
    sum_out = jnp.concatenate(total_out, axis=0)
    sum_gate = jnp.concatenate(total_gate, axis=1)
    sum_value = jnp.concatenate(total_value, axis=1)
    sum_inner = jnp.stack([sum_gate, sum_value], axis=1)

    grad_conv, grad_skip, grad_gate_gain = (
        jnp.concatenate(array, axis=1) for array in (grad_conv, grad_skip, grad_gain)
    )
    grad_conv_state = sum_all(grad_conv_state[:5], "tensor")
    skip_sums = jnp.sum(grad_skip.reshape(heads, channels // heads), axis=1)
    pack = [
        grad_norm_gain, grad_conv[:5].reshape(-1), grad_conv_state.reshape(-1),
        grad_heads[0, :heads], grad_heads[1, :heads], skip_sums, grad_gate_gain[0],
    ]
    sums_all = sum_all(jnp.concatenate(pack), "dp")
    split = []
    at = 0
    for piece in pack:
        split.append(sums_all[at : at + piece.shape[0]])
        at += piece.shape[0]
    return (
        output,
        grad_tokens,
        split[0],
        sum_inner,
        sum_step,
        sum_state,
        split[1].reshape(5, channels),
        split[2].reshape(5, states2),
        split[3],
        split[4],
        split[5],
        split[6],
        sum_out,
    )


def solution(mesh):
    placed = (
        P("dp", "tensor"),
        P("dp", "tensor"),
        P("dp", None),
        P(),
        P(None, None, "tensor"),
        P(None, "tensor"),
        P(),
        P(None, "tensor"),
        P(),
        P("tensor"),
        P("tensor"),
        P("tensor"),
        P("tensor"),
        P("tensor", None),
    )
    return jax.shard_map(
        shards,
        mesh=mesh,
        in_specs=placed,
        out_specs=(
            P("dp", "tensor"),
            P("dp", "tensor"),
            P("tensor"),
            P("dp", None, "tensor"),
            P("dp", "tensor"),
            P(("dp", "tensor"), None),
            P(None, "tensor"),
            P(),
            P("tensor"),
            P("tensor"),
            P("tensor"),
            P("tensor"),
            P("tensor", "dp"),
        ),
        check_vma=False,
    )
```

```python
import functools
import math

import jax
import jax.numpy as jnp
from jax import lax
from jax.experimental import pallas as pl
from jax.experimental.pallas import tpu as pltpu
from jax.sharding import PartitionSpec as P

F32 = jnp.float32
BF16 = jnp.bfloat16
HIGHEST = lax.Precision.HIGHEST
EPSILON = 1e-05
LOG2E = math.log2(math.e)
LANES = 128
SPAN = 128
GROUP = 256
UNROLL = 8
HINT = 0.02
ROWS = 512
CHUNKS = 2

NN = (((1,), (0,)), ((), ()))
NT = (((1,), (1,)), ((), ()))
TN = (((0,), (0,)), ((), ()))


def dot(left, right, dims=NN, precision=None):
    return lax.dot_general(left, right, dims, precision=precision, preferred_element_type=F32)


def sigmoid(a):
    return 0.5 * jnp.tanh(0.5 * a) + 0.5


def iota(shape, dim):
    return lax.broadcasted_iota(jnp.int32, shape, dim)


def tri(upper):
    rows, cols = iota((SPAN, SPAN), 0), iota((SPAN, SPAN), 1)
    return ((rows <= cols) if upper else (rows >= cols)).astype(F32)


def call(body, grid, in_specs, out_specs, out_shape, scratch=(), prefetch=0, flops=0, moved=0, name=None, vmem=56):
    return pl.pallas_call(
        body,
        grid_spec=pltpu.PrefetchScalarGridSpec(
            num_scalar_prefetch=prefetch,
            grid=grid,
            in_specs=in_specs,
            out_specs=out_specs,
            scratch_shapes=list(scratch),
        ),
        out_shape=out_shape,
        compiler_params=pltpu.CompilerParams(
            vmem_limit_bytes=vmem * 1024 * 1024, dimension_semantics=("arbitrary",) * len(grid)
        ),
        cost_estimate=pl.CostEstimate(
            flops=int(flops * HINT), bytes_accessed=int(moved * HINT), transcendentals=0
        ),
        name=name,
    )


def held(shape):
    zeros = (0,) * len(shape)
    return pl.BlockSpec(shape, lambda *_: zeros, pipeline_mode=pl.Buffered(1))


def shape_of(*dims, dtype=F32):
    return jax.ShapeDtypeStruct(dims, dtype)


def conv_taps(before, now, marks, filters):
    rows = now.shape[0]
    wide = jnp.concatenate([before, now], axis=0)
    total = filters[4:5] + filters[0:1] * now
    shifted = [now]
    for k in range(1, 4):
        moved = wide[8 - k : 8 - k + rows] * marks[:, k - 1 : k]
        shifted.append(moved)
        total = total + filters[k : k + 1] * moved
    return total, shifted


def rows_before(array, start):
    return array[pl.ds(pl.multiple_of(jnp.maximum(start - 8, 0), 8), 8), :]


def conv_back(later, marks, filters):
    rows = later.shape[0] - 8
    total = filters[0:1] * later[:rows]
    for k in range(1, 4):
        total = total + filters[k : k + 1] * (later[k : k + rows] * marks[k : k + rows, k - 1 : k])
    return total


def fold_lanes(power):
    folded = power[:, :LANES]
    for tile in range(1, power.shape[1] // LANES):
        folded = folded + power[:, tile * LANES : (tile + 1) * LANES]
    return folded


def spread(table, section, heads, count):
    lane = iota((table.shape[0], LANES), 1)
    tiles = []
    for pair in range(count // 2):
        at = section * heads + 2 * pair
        tiles.append(jnp.where(lane < LANES // 2, table[:, at : at + 1], table[:, at + 1 : at + 2]))
    return jnp.concatenate(tiles, axis=1)


def front_kernel(
    parts, heads, rank, *refs,
):
    pieces, refs = refs[:parts], refs[parts:]
    (gain, w_maps, conv_maps, bias, rate, seg_row, w_gate, w_value, conv, skip, gate_gain, marks,
     normed, pre_state, maps, maps_t, per_head, rows_out, cross_t, value, gate, mixed, low_gated, memory, squares,
     proj, cross, state) = refs
    g = pl.program_id(0)
    length, quarter = pieces[0].shape
    width = quarter * parts
    blocks = length // SPAN
    states = maps.shape[1] // 2
    count = GROUP // 64
    lane = iota((SPAN, LANES), 1)

    @pl.when(g == 0)
    def _():
        squares[...] = jnp.zeros_like(squares)

        def normalise(b, _):
            at = pl.ds(pl.multiple_of(b * SPAN, SPAN), SPAN)
            wide = [piece[at, :].astype(F32) for piece in pieces]
            total = functools.reduce(jnp.add, [array * array for array in wide])
            scale = lax.rsqrt(jnp.sum(total, axis=1, keepdims=True) / width + EPSILON)
            per_head[at, :] = jnp.broadcast_to(scale, (SPAN, LANES))
            for k in range(parts):
                to = pl.multiple_of((rank[0] ^ k) * quarter, quarter)
                normed[at, pl.ds(to, quarter)] = (wide[k] * scale * gain[:, pl.ds(to, quarter)]).astype(BF16)
            return 0

        lax.fori_loop(0, blocks, normalise, 0, unroll=2)
        proj[...] = dot(normed[...], w_maps[...])

        def tables(b, _):
            start = pl.multiple_of(b * SPAN, SPAN)
            at = pl.ds(start, SPAN)
            mark = marks[at, :]
            now = proj[at, : 2 * states]
            pre_state[at, :] = now
            total, _ = conv_taps(rows_before(proj, start)[:, : 2 * states], now, mark, conv_maps[...])
            both = total * sigmoid(total)
            keys, queries = both[:, :states], both[:, states:]
            low_keys, low_queries = keys.astype(BF16), queries.astype(BF16)
            maps[at, :states] = low_keys
            maps[at, states:] = low_queries
            maps_t[:states, pl.ds(start, SPAN)] = keys.T.astype(BF16)
            maps_t[states:, pl.ds(start, SPAN)] = queries.T.astype(BF16)

            pre = proj[at, 2 * states :] + bias[...]
            size = jnp.maximum(pre, 0.0) + jnp.log1p(jnp.exp(-jnp.abs(pre)))
            rising = dot(tri(False), -rate[...] * size, precision=HIGHEST)
            entering = jnp.exp(rising) * mark[:, 3:4]
            leaving = jnp.exp(rising[SPAN - 1 :] - rising) * mark[:, 4:5]
            rising = rising * LOG2E
            section = lane // heads
            packed = jnp.where(section == 0, rising, entering)
            packed = jnp.where(section == 2, leaving, packed)
            packed = jnp.where(section == 3, size, packed)
            packed = jnp.where(section == 4, pre, packed)
            packed = jnp.where(section == 5, per_head[at, :], packed)
            per_head[at, :] = packed
            turned = rising.T
            for group in range(rows_out.shape[0]):
                rows_out[group, pl.ds(pl.multiple_of(b * 8, 8), 8), :] = turned[group * count : group * count + 8]
            same = mark[:, 6:7] == seg_row[0:1, pl.ds(start, SPAN)]
            rows, cols = iota((SPAN, SPAN), 0), iota((SPAN, SPAN), 1)
            cross[at, :] = jnp.where(same & (rows >= cols), dot(low_queries, low_keys, NT), 0.0)
            cross_t[at, :] = jnp.where(same & (rows <= cols), dot(low_keys, low_queries, NT), 0.0)
            return 0

        lax.fori_loop(0, blocks, tables, 0, unroll=2)

    both = dot(normed[...], jnp.concatenate([w_gate[...], w_value[...]], axis=1))
    gate[...] = both[:, :GROUP].astype(BF16)
    value[...] = both[:, GROUP:]
    state[...] = jnp.zeros_like(state)
    turn = lax.rem(LANES - count * g, LANES)

    def block(b, _):
        start = pl.multiple_of(b * SPAN, SPAN)
        at = pl.ds(start, SPAN)
        total, _ = conv_taps(rows_before(value, start), value[at, :], marks[at, :], conv[...])
        inputs = total * sigmoid(total)
        table = pltpu.roll(per_head[at, :], turn, 1)
        entering, leaving, size = (spread(table, s, heads, count) for s in (1, 2, 3))
        scaled = inputs * size
        keys_t = maps_t[0:states, pl.ds(start, SPAN)]
        queries = maps[at, states:]
        low_state = state[...].astype(BF16)
        memory[b] = low_state
        out = entering * dot(queries, low_state) + skip[...] * inputs
        rising_rows = rows_out[g, pl.ds(pl.multiple_of(b * 8, 8), 8), :]
        crossed = cross[at, :]
        parts_out = []
        for pair in range(count // 2):
            weights = []
            for j in (2 * pair, 2 * pair + 1):
                gap = jnp.minimum(table[:, j : j + 1] - rising_rows[j : j + 1, :], 0.0)
                weights.append((jnp.exp2(gap) * crossed).astype(BF16))
            tile = scaled[:, pair * LANES : (pair + 1) * LANES]
            stacked = jnp.concatenate(
                [
                    jnp.where(lane < LANES // 2, tile, 0.0).astype(BF16),
                    jnp.where(lane < LANES // 2, 0.0, tile).astype(BF16),
                ],
                axis=0,
            )
            parts_out.append(dot(jnp.concatenate(weights, axis=1), stacked))
        out = out + jnp.concatenate(parts_out, axis=1)
        fresh = dot(keys_t, (leaving * scaled).astype(BF16))
        state[...] = state[...] * entering[SPAN - 1 :] + fresh
        mixed[at, :] = out
        opened = gate[at, :].astype(F32)
        gated = out * (opened * sigmoid(opened))
        low_gated[at, :] = (gated * gate_gain[...]).astype(BF16)
        squares[at, :] += fold_lanes(gated * gated)
        return 0

    lax.fori_loop(0, blocks, block, 0, unroll=UNROLL)


def assemble(pieces, target, sems, where):
    copies = [
        pltpu.make_async_copy(pieces[k].at[:, pl.ds(at, size)], target.at[:, pl.ds(to, size)], sems.at[i])
        for i, (k, at, to, size) in enumerate(where)
    ]
    for copy in copies:
        copy.start()
    for copy in copies:
        copy.wait()


def cotangent_kernel(parts, rank, *refs):
    pieces, (w_out, gated, squares, grad, stats, sums, full, sems) = refs[:parts], refs[parts:]
    g = pl.program_id(0)
    length, quarter = pieces[0].shape

    @pl.when(g == 0)
    def _():
        sums[...] = jnp.zeros_like(sums)
        places = [pl.multiple_of((rank[0] ^ k) * quarter, quarter) for k in range(parts)]
        assemble(pieces, full, sems, [(k, 0, places[k], quarter) for k in range(parts)])

    grad[...] = dot(full[...], w_out[...], NT).astype(BF16)

    def chunk(i, _):
        at = pl.ds(pl.multiple_of(i * SPAN, SPAN), SPAN)
        sums[at, :] += fold_lanes(grad[at, :].astype(F32) * gated[at, :].astype(F32))
        return 0

    lax.fori_loop(0, length // SPAN, chunk, 0, unroll=2)

    @pl.when(g == pl.num_programs(0) - 1)
    def _():
        row = iota((8, LANES), 0)
        stats[...] = dot((row == 0).astype(F32), squares[...], NT, HIGHEST) + dot(
            (row == 1).astype(F32), sums[...], NT, HIGHEST
        )


def gate_kernel(parts, run, channels_all, stacked, place, rank, *refs):
    pieces, refs = refs[:parts], refs[parts:]
    (grad, gate, mixed, gain, stats, marks, low_mixed, grad_mixer, grad_gate, grad_gain), refs = refs[:10], refs[10:]
    targets, (sent, kept, sems) = refs[:-3], refs[-3:]
    length, quarter = pieces[0].shape
    grad_gain[...] = jnp.zeros_like(grad_gain)
    pairs = quarter // (2 * run)
    bits = (parts * pairs - 1).bit_length()
    copies = []
    for half, target in ((1, sent), (0, kept)):
        for k in range(parts):
            for j in range(pairs):
                at = pl.multiple_of((2 * j + (place[0] ^ half)) * run, run)
                to = pl.multiple_of(turned((rank[0] ^ k) * pairs + j, bits) * run, run)
                copies.append(
                    pltpu.make_async_copy(
                        pieces[k].at[:, pl.ds(at, run)], target.at[:, pl.ds(to, run)], sems.at[len(copies)]
                    )
                )

    @pl.when(pl.program_id(0) == 0)
    def _():
        for copy in copies:
            copy.start()

    def chunk(i, _):
        start = pl.multiple_of(i * SPAN, SPAN)
        at = pl.ds(start, SPAN)
        columns = jnp.concatenate([stats[:, pl.ds(start, SPAN)]] * (SPAN // 8), axis=0).T
        keep = marks[at, 5:6]
        scale = lax.rsqrt(columns[:, 0:1] / channels_all + EPSILON)
        factor = scale * keep
        pull = scale * scale * factor * columns[:, 1:2] / channels_all
        opened, out, now = gate[at, :].astype(F32), mixed[at, :], grad[at, :].astype(F32)
        chance = sigmoid(opened)
        swish = opened * chance
        gated = out * swish
        scaled = gated * factor
        low_mixed[at, :] = (scaled * gain[...]).astype(BF16)
        grad_gain[...] += jnp.sum(now * scaled, axis=0, keepdims=True)
        grad_gated = now * (factor * gain[...]) - gated * pull
        grad_mixer[at, :] = (grad_gated * swish).astype(BF16)
        grad_gate[at, :] = (grad_gated * out * chance * (1.0 + opened * (1.0 - chance))).astype(BF16)
        return 0

    lax.fori_loop(0, length // SPAN, chunk, 0, unroll=4)

    @pl.when(pl.program_id(0) == 0)
    def _():
        for copy in copies:
            copy.wait()

    for half, source in enumerate((sent, kept)):
        now = dot(low_mixed[...], source[...], TN).astype(BF16)
        if stacked:
            targets[0][half] = now
        else:
            targets[half][...] = now


def weight_kernel(place, left_send, left_own, *refs):
    right, targets = refs[:-2], refs[-2:]
    for left, target in zip((left_send, left_own), targets):
        at = 0
        for part in right:
            size = part.shape[1]
            target[:, at : at + size] = dot(left[...], part[...], TN).astype(BF16)
            at += size


def backward_kernel(
    heads, first, value, grad_out, mixed, memory, conv, skip, per_head, marks, rows_in, maps, maps_t, cross_t,
    grad_value, grad_conv, grad_skip, grad_cross, folded, grad_maps,
    later, grad_memory,
):
    g = pl.program_id(0) + first
    length = grad_out.shape[0]
    blocks = length // SPAN
    states = maps.shape[1] // 2
    count = GROUP // 64
    lane = iota((SPAN, LANES), 1)
    row = iota((SPAN, GROUP), 0)
    turn = lax.rem(LANES - count * g, LANES)
    channel, target = iota((GROUP, LANES), 0), iota((GROUP, LANES), 1)
    pick_rise = (target == count * g + channel // 64).astype(BF16)
    pick_size = (target == heads + count * g + channel // 64).astype(BF16)
    later[...] = jnp.zeros_like(later)
    grad_memory[...] = jnp.zeros_like(grad_memory)
    grad_conv[...] = jnp.zeros_like(grad_conv)
    grad_skip[...] = jnp.zeros_like(grad_skip)

    @pl.when(g == first)
    def _():
        grad_cross[...] = jnp.zeros_like(grad_cross)
        folded[...] = jnp.zeros_like(folded)
        grad_maps[...] = jnp.zeros_like(grad_maps)

    def block(i, _):
        b = blocks - 1 - i
        start = pl.multiple_of(b * SPAN, SPAN)
        at = pl.ds(start, SPAN)
        filters = conv[...]
        total, shifted = conv_taps(rows_before(value, start), value[at, :], marks[at, :], filters)
        chance = sigmoid(total)
        inputs = total * chance
        table = pltpu.roll(per_head[at, :], turn, 1)
        entering, leaving, size = (spread(table, s, heads, count) for s in (1, 2, 3))
        scaled = inputs * size
        low_scaled = scaled.astype(BF16)
        pulled = grad_out[at, :].astype(F32)
        keys, queries_t = maps[at, 0:states], maps_t[states:, pl.ds(start, SPAN)]
        memory_now = memory[b]
        grad_next = grad_memory[...]
        low_next = grad_next.astype(BF16)
        entered = (entering * pulled).astype(BF16)
        left = (leaving * scaled).astype(BF16)
        grad_maps[at, 0:states] += dot(left, low_next, NT)
        grad_maps[at, states:] += dot(entered, memory_now, NT)
        rising_rows = rows_in[0, pl.ds(pl.multiple_of(b * 8, 8), 8), :]
        crossed_t = cross_t[at, :]
        cross_sum = jnp.zeros((SPAN, SPAN), F32)
        parts = []
        for pair in range(count // 2):
            tile = pulled[:, pair * LANES : (pair + 1) * LANES]
            one = jnp.where(lane < LANES // 2, tile, 0.0).astype(BF16)
            two = jnp.where(lane < LANES // 2, 0.0, tile).astype(BF16)
            low_tile = low_scaled[:, pair * LANES : (pair + 1) * LANES]
            weights = []
            for j, masked in ((2 * pair, one), (2 * pair + 1, two)):
                gap = table[:, j : j + 1] - rising_rows[j : j + 1, :]
                cross_sum = cross_sum + jnp.exp2(jnp.minimum(gap, 0.0)) * dot(masked, low_tile, NT)
                weights.append((jnp.exp2(jnp.minimum(-gap, 0.0)) * crossed_t).astype(BF16))
            parts.append(dot(jnp.concatenate(weights, axis=1), jnp.concatenate([one, two], axis=0)))
        grad_cross[at, :] += cross_sum
        grad_within = jnp.concatenate(parts, axis=1)
        grad_left = dot(keys, low_next)
        grad_scaled = grad_within + leaving * grad_left
        scanned = mixed[at, :] - skip[...] * inputs
        kept = left.astype(F32) * grad_left
        rise = pulled * scanned - low_scaled.astype(F32) * grad_within - kept
        carried = entering[SPAN - 1 :] * jnp.sum(low_next.astype(F32) * memory_now.astype(F32), axis=0, keepdims=True)
        rise = rise + jnp.where(row == SPAN - 1, carried + jnp.sum(kept, axis=0, keepdims=True), 0.0)
        grown = grad_scaled * inputs
        summed = folded[at, :]
        for product, pick in ((rise, pick_rise), (grown, pick_size)):
            high = product.astype(BF16)
            rest = (product - high.astype(F32)).astype(BF16)
            summed = summed + dot(high, pick) + dot(rest, pick)
        folded[at, :] = summed
        grad_skip[...] += jnp.sum(pulled * inputs, axis=0, keepdims=True)
        grad_inputs = size * grad_scaled + skip[...] * pulled
        grad_total = grad_inputs * (chance * (1.0 + total * (1.0 - chance)))
        for k in range(4):
            grad_conv[k : k + 1] += jnp.sum(grad_total * shifted[k], axis=0, keepdims=True)
        grad_conv[4:5] += jnp.sum(grad_total, axis=0, keepdims=True)
        longer = jnp.concatenate([grad_total, later[...]], axis=0)
        later[...] = grad_total[:8]
        grad_value[at, :] = conv_back(longer, marks[pl.ds(start, SPAN + 8), :], filters).astype(BF16)
        grad_memory[...] = entering[SPAN - 1 :] * grad_next + dot(queries_t, entered)
        return 0

    lax.fori_loop(0, blocks, block, 0, unroll=UNROLL)


def finish_kernel(
    heads, calls, *refs,
):
    summed_parts, refs = refs[: 3 * calls], refs[3 * calls :]
    (per_head, marks, maps, seg_row, pre_state, conv_state, rate,
     grad_state, grad_step, grad_conv_state, grad_heads, later) = refs
    length = maps.shape[0]
    blocks = length // SPAN
    states = maps.shape[1] // 2
    later[...] = jnp.zeros_like(later)
    grad_conv_state[...] = jnp.zeros_like(grad_conv_state)
    grad_heads[...] = jnp.zeros_like(grad_heads)

    def block(i, _):
        start = pl.multiple_of((blocks - 1 - i) * SPAN, SPAN)
        at = pl.ds(start, SPAN)
        mark = marks[at, :]
        rows, cols = iota((SPAN, SPAN), 0), iota((SPAN, SPAN), 1)
        linked = (rows >= cols) & (mark[:, 6:7] == seg_row[0:1, pl.ds(start, SPAN)])
        grad_cross, summed, grad_maps = (
            functools.reduce(jnp.add, [ref[at, :] for ref in summed_parts[j::3]]) for j in range(3)
        )
        crossed = jnp.where(linked, grad_cross, 0.0)
        keys, queries = maps[at, 0:states], maps[at, states:]
        grad_keys = grad_maps[:, :states] + dot(crossed.T.astype(BF16), queries)
        grad_queries = grad_maps[:, states:] + dot(crossed.astype(BF16), keys)
        filters = conv_state[...]
        total, shifted = conv_taps(rows_before(pre_state, start), pre_state[at, :], mark, filters)
        chance = sigmoid(total)
        grad_total = jnp.concatenate([grad_keys, grad_queries], axis=1) * (chance * (1.0 + total * (1.0 - chance)))
        for k in range(4):
            grad_conv_state[k : k + 1] += jnp.sum(grad_total * shifted[k], axis=0, keepdims=True)
        grad_conv_state[4:5] += jnp.sum(grad_total, axis=0, keepdims=True)
        longer = jnp.concatenate([grad_total, later[...]], axis=0)
        later[...] = grad_total[:8]
        grad_state[at, :] = conv_back(longer, marks[pl.ds(start, SPAN + 8), :], filters).astype(BF16)

        table = per_head[at, :]
        grad_decay = dot(tri(True), summed, precision=HIGHEST)
        size = pltpu.roll(table, LANES - 3 * heads, 1)
        pre = pltpu.roll(table, LANES - 4 * heads, 1)
        grad_size = pltpu.roll(summed, LANES - heads, 1) - rate[...] * grad_decay
        valid = iota((SPAN, LANES), 1) < heads
        grad_pre = jnp.where(valid, grad_size * sigmoid(pre), 0.0)
        grad_step[at, :] = grad_pre.astype(BF16)
        grad_heads[0:1] += jnp.sum(grad_pre, axis=0, keepdims=True)
        grad_heads[1:2] += jnp.sum(-rate[...] * size * grad_decay, axis=0, keepdims=True)
        return 0

    lax.fori_loop(0, blocks, block, 0, unroll=UNROLL)


def put(far, near, total):
    step = pl.program_id(0)

    @pl.when(step < 2)
    def _():
        far[0] = total.astype(BF16)

    @pl.when(step >= 2)
    def _():
        near[0] = total.astype(BF16)


def output_kernel(rank, gated, w_out, far, near):
    put(far, near, dot(gated[...], w_out[...]))


def normed_kernel(chunks, rank, *refs):
    grads, (grad_state, grad_step, w_inner, w_maps), refs = refs[: 2 * chunks], refs[2 * chunks : 2 * chunks + 4], refs[2 * chunks + 4 :]
    outs, (joined, joined_maps) = refs[:-2], refs[-2:]

    @pl.when(pl.program_id(0) == 0)
    def _():
        for target, parts in ((joined, grads), (joined_maps, (grad_state, grad_step))):
            at = 0
            for part in parts:
                target[:, at : at + part.shape[1]] = part[...]
                at += part.shape[1]

    total = dot(joined[...], w_inner[...], NT) + dot(joined_maps[...], w_maps[...], NT)
    put(*outs, total)


def swap(array, axis, mask):
    count = lax.axis_size(axis)
    return lax.ppermute(array, axis, [(i, i ^ mask) for i in range(count)])


def gather_pieces(own, parts):
    pieces = {0: own}
    bit = parts // 2
    while bit >= 1:
        pieces.update({k | bit: swap(piece, "tensor", bit) for k, piece in list(pieces.items())})
        bit //= 2
    return [pieces[k] for k in range(parts)]


def tie(array, *first):
    return lax.optimization_barrier((array, *first))[0]


def meet(sums, *arrays):
    arrays = lax.optimization_barrier((*arrays, *(part.got for part in sums)))
    for part, got in zip(sums, arrays[len(arrays) - len(sums) :]):
        part.got = got
    return arrays[: len(arrays) - len(sums)]


def sum_all(array, axis):
    bit = 1
    while bit < lax.axis_size(axis):
        array = array + swap(array, axis, bit)
        bit *= 2
    return array


def rest_masks(low_bits):
    bits = (lax.axis_size("dp") - 1).bit_length()
    return [1 << bit for bit in (*range(low_bits + 1, bits), *range(low_bits - 1, -1, -1))]


def turned(index, bits):
    result = index * 0
    for bit in range(bits):
        result = result | (((index >> bit) & 1) << (bits - 1 - bit))
    return result


class Sum:
    def __init__(self, own, got, dim, low_bits):
        self.terms, self.got, self.dim, self.masks = [own], got, dim, rest_masks(low_bits)
        if got is None:
            self.send()

    def advance(self):
        self.terms.append(self.got)
        return self.send()

    def send(self):
        mask = self.masks.pop(0)
        top = (lax.axis_index("dp") & mask) // mask
        size = self.terms[0].shape[self.dim] // 2

        def cut(half):
            return [lax.dynamic_slice_in_dim(term, half * size, size, self.dim) for term in self.terms]

        sent = functools.reduce(jnp.add, [term.astype(F32) for term in cut(1 - top)]).astype(BF16)
        self.terms, self.got, self.sent = cut(top), swap(sent, "dp", mask), sent
        return sent

    def result(self):
        while self.masks:
            self.advance()
        return functools.reduce(jnp.add, [term.astype(F32) for term in (*self.terms, self.got)])


def add_low(left, right):
    return (left.astype(F32) + right.astype(F32)).astype(BF16)


def shards(
    tokens,
    cotangent,
    doc_lengths,
    norm_gain,
    w_inner,
    w_step,
    w_state,
    conv_inner,
    conv_state,
    step_bias,
    log_rate,
    skip_gain,
    gate_gain,
    w_out,
):
    parts = lax.axis_size("tensor")
    groups = lax.axis_size("dp")
    rank = lax.axis_index("tensor").astype(jnp.int32)
    ranks = rank.reshape(1)
    length, quarter = tokens.shape
    width = quarter * parts
    channels = w_inner.shape[2]
    heads = w_step.shape[1]
    states2 = w_state.shape[1]
    states = states2 // 2
    blocks = length // SPAN
    steps = channels // GROUP
    repeat = LANES // heads
    piece_rows = width // groups
    low_bits = 0
    while (piece_rows << low_bits) < LANES:
        low_bits += 1
    run = piece_rows << low_bits
    half_width = width // 2
    high_bits = (groups - 1).bit_length() - 1 - low_bits
    place = ((lax.axis_index("dp") >> low_bits) & 1).astype(jnp.int32).reshape(1)

    token_y = swap(tokens, "tensor", 2)
    grad_y = swap(tie(cotangent, token_y), "tensor", 2)
    flat = w_inner.reshape(width, 2 * channels)
    w_maps = jnp.concatenate([w_state, jnp.tile(w_step, (1, repeat))], axis=1)
    step_pad = jnp.pad(w_step, ((0, 0), (0, LANES - heads)))
    bias8 = jnp.tile(step_bias, repeat)[None, :]
    rate8 = jnp.exp(jnp.tile(log_rate, repeat))[None, :]
    skip_row = jnp.repeat(skip_gain, channels // heads)[None, :]
    gain_row = gate_gain[None, :]
    conv_pad = jnp.pad(conv_inner, ((0, 3), (0, 0)))
    conv_state_pad = jnp.pad(conv_state, ((0, 3), (0, 0)))

    doc_ends = jnp.cumsum(doc_lengths[0])
    positions = jnp.arange(length, dtype=jnp.int32)
    segment = jnp.sum((positions[:, None] >= doc_ends[None, :]).astype(jnp.int32), axis=1)
    present = positions < doc_ends[-1]
    by_block = segment.reshape(blocks, SPAN)
    final = by_block[:, -1:]
    before = jnp.concatenate([jnp.full((1, 1), -1, jnp.int32), final[:-1]], axis=0)
    marks = [
        jnp.concatenate([jnp.full((k,), -1, jnp.int32), segment[:-k]]) == segment for k in (1, 2, 3)
    ]
    marks += [(by_block == before).reshape(-1), (by_block == final).reshape(-1), present]
    marks = [mark.astype(F32) for mark in marks] + [segment.astype(F32)]
    marks = jnp.pad(jnp.stack(marks, axis=1), ((0, 8), (0, LANES - len(marks))))
    seg_row = jnp.broadcast_to(segment.astype(F32)[None, :], (8, length))

    token_y, flat, w_maps, step_pad, marks, seg_row, skip_row, conv_pad = lax.optimization_barrier(
        (token_y, flat, w_maps, step_pad, marks, seg_row, skip_row, conv_pad)
    )
    token_pieces = [tokens, swap(tokens, "tensor", 1), token_y, swap(token_y, "tensor", 1)]

    by_group = lambda rows: pl.BlockSpec((rows, GROUP), lambda g, *_: (0, g))
    (normed, pre_state, maps, maps_t, per_head, rising_rows, cross_t, value, gate, mixer_out, low_gated, memory, squares) = call(
        functools.partial(front_kernel, parts, heads),
        (steps,),
        [held((length, quarter))] * parts
        + [
            held((1, width)), held((width, states2 + LANES)), held((8, states2)),
            held((1, LANES)), held((1, LANES)), held((8, length)),
            pl.BlockSpec((width, GROUP), lambda g, *_: (0, g)), pl.BlockSpec((width, GROUP), lambda g, *_: (0, steps + g)),
            by_group(8), by_group(1), by_group(1), held((length + 8, LANES)),
        ],
        [
            held((length, width)), held((length, states2)), held((length, states2)), held((states2, length)),
            held((length, LANES)), held((steps, blocks * 8, SPAN)), held((length, SPAN)),
            by_group(length), by_group(length), by_group(length), by_group(length),
            pl.BlockSpec((blocks, states, GROUP), lambda g, *_: (0, 0, g)), held((length, LANES)),
        ],
        [
            shape_of(length, width, dtype=BF16), shape_of(length, states2), shape_of(length, states2, dtype=BF16),
            shape_of(states2, length, dtype=BF16), shape_of(length, LANES), shape_of(steps, blocks * 8, SPAN),
            shape_of(length, SPAN), shape_of(length, channels), shape_of(length, channels, dtype=BF16),
            shape_of(length, channels), shape_of(length, channels, dtype=BF16),
            shape_of(blocks, states, channels, dtype=BF16), shape_of(length, LANES),
        ],
        [
            pltpu.VMEM((length, states2 + LANES), F32), pltpu.VMEM((length, SPAN), F32),
            pltpu.VMEM((states, GROUP), F32),
        ],
        prefetch=1,
        flops=8 * length * width * channels,
        moved=length * width * 4 + width * channels * 4 + length * channels * 14,
        name="front",
        vmem=56,
    )(
        ranks, *token_pieces, norm_gain[None, :], w_maps, conv_state_pad, bias8, rate8, seg_row, flat, flat, conv_pad,
        skip_row, gain_row, marks,
    )

    grad_y = tie(grad_y, squares)
    grad_pieces = [cotangent, swap(cotangent, "tensor", 1), grad_y, swap(grad_y, "tensor", 1)]
    pieces_any = [pl.BlockSpec(memory_space=pl.ANY)] * parts
    double = 2 * GROUP
    by_double = lambda rows: pl.BlockSpec((rows, double), lambda g, *_: (0, g))
    grad_mixed, stats = call(
        functools.partial(cotangent_kernel, parts),
        (channels // double,),
        pieces_any
        + [
            pl.BlockSpec((double, width), lambda g, *_: (g, 0)),
            by_double(length), held((length, LANES)),
        ],
        [by_double(length), held((8, length))],
        [shape_of(length, channels, dtype=BF16), shape_of(8, length)],
        [pltpu.VMEM((length, LANES), F32), pltpu.VMEM((length, width), BF16), pltpu.SemaphoreType.DMA((parts,))],
        prefetch=1,
        flops=2 * length * width * channels,
        moved=length * width * 2 + width * channels * 2 + length * channels * 12,
        name="cotangent",
        vmem=56,
    )(ranks, *grad_pieces, w_out, low_gated, squares)
    spans = steps // CHUNKS

    def chunk_spec(rows, c):
        return pl.BlockSpec((rows, GROUP), lambda g, *_: (0, c * spans + g))

    def gate_part(c, stats, stacked):
        size = spans * GROUP
        if stacked:
            outs = [pl.BlockSpec((2, GROUP, half_width), lambda g, *_: (0, g, 0))]
            shapes = [shape_of(2, size, half_width, dtype=BF16)]
        else:
            outs = [pl.BlockSpec((GROUP, half_width), lambda g, *_: (g, 0))] * 2
            shapes = [shape_of(size, half_width, dtype=BF16)] * 2
        return call(
            functools.partial(gate_kernel, parts, run, channels * parts, stacked),
            (spans,),
            pieces_any
            + [
                chunk_spec(length, c), chunk_spec(length, c), chunk_spec(length, c), chunk_spec(1, c),
                held((8, length)), held((length + 8, LANES)),
            ],
            [by_group(length), by_group(length), by_group(length), by_group(1), *outs],
            [
                shape_of(length, size, dtype=BF16), shape_of(length, size, dtype=BF16),
                shape_of(length, size, dtype=BF16), shape_of(1, size), *shapes,
            ],
            [
                pltpu.VMEM((length, half_width), BF16), pltpu.VMEM((length, half_width), BF16),
                pltpu.SemaphoreType.DMA((width // run,)),
            ],
            prefetch=2,
            flops=2 * length * width * size,
            moved=length * width * 2 + length * size * 18 + width * size * 2,
            name="gate",
        )(place, ranks, *grad_pieces, grad_mixed, gate, mixer_out, gain_row, stats, marks)

    def weight_part(*right):
        runs = half_width // run
        columns = [part.shape[1] for part in right]
        out = pl.BlockSpec((run, sum(columns)), lambda j, p: (turned(j, (runs - 1).bit_length()), 0))
        shape = shape_of(half_width, sum(columns), dtype=BF16)
        return call(
            weight_kernel,
            (runs,),
            [
                pl.BlockSpec((length, run), lambda j, p: (0, 2 * j + (p[0] ^ 1))),
                pl.BlockSpec((length, run), lambda j, p: (0, 2 * j + p[0])),
            ]
            + [held((length, size)) for size in columns],
            [out, out],
            [shape, shape],
            prefetch=1,
            flops=2 * length * width * sum(columns),
            moved=length * width * 2 + length * sum(columns) * 2 + width * sum(columns) * 2,
            name="weights",
        )(place, normed, normed, *right)

    all_lanes = held((length, LANES))

    def backward_part(c, grad_out):
        size = spans * GROUP
        return call(
            functools.partial(backward_kernel, heads, c * spans),
            (spans,),
            [
                chunk_spec(length, c), by_group(length), chunk_spec(length, c),
                pl.BlockSpec((blocks, states, GROUP), lambda g, *_: (0, 0, c * spans + g)),
                chunk_spec(8, c), chunk_spec(1, c), all_lanes, held((length + 8, LANES)),
                pl.BlockSpec((1, blocks * 8, SPAN), lambda g, *_: (c * spans + g, 0, 0)),
                held((length, states2)), held((states2, length)), held((length, SPAN)),
            ],
            [by_group(length), by_group(8), by_group(1), held((length, SPAN)), all_lanes, held((length, states2))],
            [
                shape_of(length, size, dtype=BF16), shape_of(8, size), shape_of(1, size),
                shape_of(length, SPAN), shape_of(length, LANES), shape_of(length, states2),
            ],
            [pltpu.VMEM((8, GROUP), F32), pltpu.VMEM((states, GROUP), F32)],
            flops=40e9 / CHUNKS,
            moved=length * size * 14,
            name="backward",
            vmem=56,
        )(
            value, grad_out, mixer_out, memory, conv_pad, skip_row, per_head, marks, rising_rows, maps, maps_t,
            cross_t,
        )

    def piece_of(i, r):
        return r[0] ^ jnp.where(i == 0, 1, jnp.where(i == 1, 3, jnp.where(i == 2, 2, 0)))

    def far_near(count):
        specs = [
            pl.BlockSpec((1, length, quarter), lambda i, r: (jnp.minimum(i, 1), 0, 0)),
            pl.BlockSpec((1, length, quarter), lambda i, r: (jnp.maximum(i, 2) - 2, 0, 0)),
        ]
        return specs, [shape_of(2, length, quarter, dtype=BF16), shape_of(count, length, quarter, dtype=BF16)]

    def output_part(low_gated):
        return call(
            output_kernel,
            (4,),
            [held((length, channels)), pl.BlockSpec((channels, quarter), lambda i, r: (0, piece_of(i, r)))],
            *far_near(2),
            prefetch=1,
            flops=2 * length * channels * width,
            moved=length * channels * 2 + channels * width * 2 + length * width * 2,
            name="output",
        )(ranks, low_gated, w_out)

    def normed_part(grad_gate):
        grads = (*grad_gate, *grad_value)
        return call(
            functools.partial(normed_kernel, len(grad_gate)),
            (4,),
            [held((length, part.shape[1])) for part in grads]
            + [
                held((length, states2)), held((length, LANES)),
                pl.BlockSpec((quarter, 2 * channels), lambda i, r: (piece_of(i, r), 0)),
                pl.BlockSpec((quarter, states2 + LANES), lambda i, r: (piece_of(i, r), 0)),
            ],
            *far_near(2),
            [pltpu.VMEM((length, 2 * channels), BF16), pltpu.VMEM((length, states2 + LANES), BF16)],
            prefetch=1,
            flops=2 * length * (2 * channels + states2 + LANES) * width,
            moved=length * channels * 4 + channels * width * 4 + length * width * 2,
            name="normed_grad",
        )(ranks, *grads, grad_state, grad_step, flat, w_maps)

    def over_x(send):
        return swap(send, "dp", 1 << low_bits)

    stats = sum_all(stats, "tensor")

    first = gate_part(0, stats, False)
    sum_out = [Sum(first[5], over_x(first[4]), 1, low_bits)]
    other = gate_part(1, tie(stats, first[5]), True)
    low_mixed, grad_mixer, grad_gate, grad_gain = zip(first[:4], other[:4])
    gate_send, gate_own = weight_part(tie(grad_gate[0], other[4]), *grad_gate[1:])
    sum_gate = Sum(gate_own, over_x(gate_send), 0, low_bits)
    out_far, out_near = output_part(tie(low_gated, gate_own))

    out_far, out_near, stack = meet(sum_out, out_far, out_near, other[4])
    moved = [sum_out[0].advance(), out_far]
    out_far_got = swap(out_far, "tensor", 1)
    sum_out.append(Sum(stack, None, 2, low_bits))
    back = backward_part(0, tie(grad_mixer[0], *moved, sum_out[1].sent))

    grad_value, out_far_got = meet(sum_out[:1], back[0], out_far_got)
    moved = [sum_out[0].advance()]
    out_sum = add_low(out_near[0], out_far_got[1])
    out_y = swap(out_sum, "tensor", 2)
    value_send, value_own = weight_part(tie(grad_value, *moved, out_sum))
    sum_value = [Sum(value_own, over_x(value_send), 0, low_bits)]
    backs = [back, backward_part(1, tie(grad_mixer[1], value_own))]

    grad_value2, out_y = meet([sum_gate, *sum_out], backs[1][0], out_y)
    total_out = [sum_out[0].result()]
    moved = [sum_gate.advance(), sum_out[1].advance(), total_out[0]]
    value_send2, value_own2 = weight_part(tie(grad_value2, *moved))
    sum_value.append(Sum(value_own2, over_x(value_send2), 0, low_bits))
    moved = [value_own2]
    grad_value, grad_conv, grad_skip, cross_parts, folded_parts, maps_parts = zip(*backs)
    (grad_state, grad_step, grad_conv_state, grad_heads) = call(
        functools.partial(finish_kernel, heads, CHUNKS),
        (1,),
        [held((length, SPAN)), all_lanes, held((length, states2))] * CHUNKS
        + [
            all_lanes, held((length + 8, LANES)), held((length, states2)), held((8, length)),
            held((length, states2)), held((8, states2)), held((1, LANES)),
        ],
        [held((length, states2)), all_lanes, held((8, states2)), held((8, LANES))],
        [
            shape_of(length, states2, dtype=BF16), shape_of(length, LANES, dtype=BF16),
            shape_of(8, states2), shape_of(8, LANES),
        ],
        [pltpu.VMEM((8, states2), F32)],
        flops=4e9,
        moved=length * 2048 * CHUNKS + length * 5000,
        name="finish",
        vmem=56,
    )(
        tie(cross_parts[0], *moved), folded_parts[0], maps_parts[0],
        *[part for three in zip(cross_parts[1:], folded_parts[1:], maps_parts[1:]) for part in three],
        per_head, marks, maps, seg_row, pre_state, conv_state_pad, rate8,
    )

    (grad_state,) = meet(sum_value[:1], grad_state)
    state_got = swap(grad_state, "tensor", 1)
    moved = [sum_value[0].advance(), grad_state]
    near_far, near = normed_part([tie(grad_gate[0], *moved), *grad_gate[1:]])

    near_far, near, state_got = meet([*sum_value, sum_gate, sum_out[1]], near_far, near, state_got)
    near_far_got = swap(near_far, "tensor", 1)
    state_sum = add_low(grad_state, state_got)
    state_got = swap(state_sum, "tensor", 2)
    moved = [sum_value[1].advance(), sum_gate.advance(), state_sum]
    near, near_far_got, *_ = lax.optimization_barrier((near, near_far_got, *moved))
    near_sum = add_low(near[0], near_far_got[1])
    over_y = swap(near_sum, "tensor", 2)
    sum_value[0].got = tie(sum_value[0].got, near_sum)
    moved = [sum_value[0].advance()]
    sum_out[1].got = tie(sum_out[1].got, *moved)
    out_x = sum_out[1].result()
    out_x_low = out_x[0].astype(BF16)
    near_sum = tie(near_sum, out_x_low)
    late = (
        out_x_low, grad_step, norm_gain, grad_conv_state, grad_heads, normed, state_got,
        grad_conv, grad_skip, grad_gain, stats, marks, per_head,
    )
    (
        out_x_low, grad_step, norm_gain, grad_conv_state, grad_heads, normed, state_got,
        grad_conv, grad_skip, grad_gain, stats, marks, per_head,
    ) = lax.optimization_barrier((late, near_sum))[0]
    out_x_got = over_x(out_x_low)
    state_all = add_low(state_sum, state_got)
    own_rows = piece_rows // parts
    grad_w_state = dot(normed, state_all, TN).astype(BF16)
    grad_w_state = lax.dynamic_slice_in_dim(
        grad_w_state.reshape(groups, parts, own_rows, states2), rank, 1, axis=1
    )
    grad_w_step = dot(grad_step[:, :heads], normed, TN).astype(BF16)
    grad_w_step = grad_w_step.reshape(heads, groups, piece_rows).transpose(1, 0, 2)
    small = jnp.concatenate(
        [grad_w_state.reshape(groups, own_rows * states2), grad_w_step.reshape(groups, heads * piece_rows)], axis=1
    ).reshape(groups // (2 << low_bits), 2, 1 << low_bits, -1)
    small = jnp.stack([small[turned(j, high_bits)] for j in range(small.shape[0])])
    small_own = lax.dynamic_slice_in_dim(small, place[0], 1, 1).reshape(groups // 2, -1)
    small_send = lax.dynamic_slice_in_dim(small, 1 - place[0], 1, 1).reshape(groups // 2, -1)
    small_sum = Sum(small_own, over_x(small_send), 0, low_bits)
    (small_send,) = meet([sum_value[1], sum_gate], small_send)
    total_gate = sum_gate.result()
    moved = [sum_value[1].advance(), total_gate]
    over_y, *_ = lax.optimization_barrier((over_y, *moved))
    scale_out = lax.rsqrt(stats[0] / (channels * parts) + EPSILON)
    factor = scale_out * marks[:length, 5]
    branch = out_near[1].astype(F32) + out_far_got[0].astype(F32) + out_y.astype(F32)
    own_tokens = tokens.astype(F32)
    output = (own_tokens + factor[:, None] * branch).astype(BF16)
    grad_normed = near[1].astype(F32) + near_far_got[0].astype(F32) + over_y.astype(F32)
    own_gain = lax.dynamic_slice_in_dim(norm_gain, rank * quarter, quarter, 0)
    scale_in = per_head[:, 5 * heads : 5 * heads + 1]
    row_norm = sum_all(jnp.sum(own_tokens * own_gain * grad_normed, axis=1), "tensor")
    row_norm, out_x_got = meet([*sum_value, small_sum], row_norm, out_x_got)
    moved = [small_sum.advance()]
    total_value = [part.result() for part in sum_value]
    total_out.append(out_x[1] + out_x_got.astype(F32))
    grad_tokens = (
        cotangent.astype(F32)
        + scale_in * own_gain * grad_normed
        - own_tokens * scale_in**3 * row_norm[:, None] / width
    ).astype(BF16)
    grad_norm_gain = jnp.sum(grad_normed * own_tokens * scale_in, axis=0)

    (total_value[0],) = meet([small_sum], tie(total_value[0], *moved))
    small_sum = small_sum.result()[0]
    sum_state = small_sum[: own_rows * states2].reshape(own_rows, states2)
    sum_step = small_sum[own_rows * states2 :].reshape(heads, piece_rows).T

    sum_out = jnp.concatenate(total_out, axis=0)
    sum_gate = total_gate
    sum_value = jnp.concatenate(total_value, axis=1)
    sum_inner = jnp.stack([sum_gate, sum_value], axis=1)

    grad_conv, grad_skip, grad_gate_gain = (
        jnp.concatenate(array, axis=1) for array in (grad_conv, grad_skip, grad_gain)
    )
    grad_conv_state = sum_all(grad_conv_state[:5], "tensor")
    skip_sums = jnp.sum(grad_skip.reshape(heads, channels // heads), axis=1)
    pack = [
        grad_norm_gain, grad_conv[:5].reshape(-1), grad_conv_state.reshape(-1),
        grad_heads[0, :heads], grad_heads[1, :heads], skip_sums, grad_gate_gain[0],
    ]
    sums_all = sum_all(jnp.concatenate(pack), "dp")
    split = []
    at = 0
    for piece in pack:
        split.append(sums_all[at : at + piece.shape[0]])
        at += piece.shape[0]
    return (
        output,
        grad_tokens,
        split[0],
        sum_inner,
        sum_step,
        sum_state,
        split[1].reshape(5, channels),
        split[2].reshape(5, states2),
        split[3],
        split[4],
        split[5],
        split[6],
        sum_out,
    )


def solution(mesh):
    placed = (
        P("dp", "tensor"),
        P("dp", "tensor"),
        P("dp", None),
        P(),
        P(None, None, "tensor"),
        P(None, "tensor"),
        P(),
        P(None, "tensor"),
        P(),
        P("tensor"),
        P("tensor"),
        P("tensor"),
        P("tensor"),
        P("tensor", None),
    )
    return jax.shard_map(
        shards,
        mesh=mesh,
        in_specs=placed,
        out_specs=(
            P("dp", "tensor"),
            P("dp", "tensor"),
            P("tensor"),
            P("dp", None, "tensor"),
            P("dp", "tensor"),
            P(("dp", "tensor"), None),
            P(None, "tensor"),
            P(),
            P("tensor"),
            P("tensor"),
            P("tensor"),
            P("tensor"),
            P("tensor", "dp"),
        ),
        check_vma=False,
    )
```

```python
import functools
import math

import jax
import jax.numpy as jnp
from jax import lax
from jax.experimental import pallas as pl
from jax.experimental.pallas import tpu as pltpu
from jax.sharding import PartitionSpec as P

F32 = jnp.float32
BF16 = jnp.bfloat16
HIGHEST = lax.Precision.HIGHEST
EPSILON = 1e-05
LOG2E = math.log2(math.e)
LANES = 128
SPAN = 128
GROUP = 256
UNROLL = 8
HINT = 0.02
ROWS = 512
CHUNKS = 2

NN = (((1,), (0,)), ((), ()))
NT = (((1,), (1,)), ((), ()))
TN = (((0,), (0,)), ((), ()))


def dot(left, right, dims=NN, precision=None):
    return lax.dot_general(left, right, dims, precision=precision, preferred_element_type=F32)


def sigmoid(a):
    return 0.5 * jnp.tanh(0.5 * a) + 0.5


def iota(shape, dim):
    return lax.broadcasted_iota(jnp.int32, shape, dim)


def tri(upper):
    rows, cols = iota((SPAN, SPAN), 0), iota((SPAN, SPAN), 1)
    return ((rows <= cols) if upper else (rows >= cols)).astype(F32)


def call(body, grid, in_specs, out_specs, out_shape, scratch=(), prefetch=0, flops=0, moved=0, name=None, vmem=56):
    return pl.pallas_call(
        body,
        grid_spec=pltpu.PrefetchScalarGridSpec(
            num_scalar_prefetch=prefetch,
            grid=grid,
            in_specs=in_specs,
            out_specs=out_specs,
            scratch_shapes=list(scratch),
        ),
        out_shape=out_shape,
        compiler_params=pltpu.CompilerParams(
            vmem_limit_bytes=vmem * 1024 * 1024, dimension_semantics=("arbitrary",) * len(grid)
        ),
        cost_estimate=pl.CostEstimate(
            flops=int(flops * HINT), bytes_accessed=int(moved * HINT), transcendentals=0
        ),
        name=name,
    )


def held(shape):
    zeros = (0,) * len(shape)
    return pl.BlockSpec(shape, lambda *_: zeros, pipeline_mode=pl.Buffered(1))


def shape_of(*dims, dtype=F32):
    return jax.ShapeDtypeStruct(dims, dtype)


def conv_taps(before, now, marks, filters):
    rows = now.shape[0]
    wide = jnp.concatenate([before, now], axis=0)
    total = filters[4:5] + filters[0:1] * now
    shifted = [now]
    for k in range(1, 4):
        moved = wide[8 - k : 8 - k + rows] * marks[:, k - 1 : k]
        shifted.append(moved)
        total = total + filters[k : k + 1] * moved
    return total, shifted


def rows_before(array, start):
    return array[pl.ds(pl.multiple_of(jnp.maximum(start - 8, 0), 8), 8), :]


def conv_back(later, marks, filters):
    rows = later.shape[0] - 8
    total = filters[0:1] * later[:rows]
    for k in range(1, 4):
        total = total + filters[k : k + 1] * (later[k : k + rows] * marks[k : k + rows, k - 1 : k])
    return total


def fold_lanes(power):
    folded = power[:, :LANES]
    for tile in range(1, power.shape[1] // LANES):
        folded = folded + power[:, tile * LANES : (tile + 1) * LANES]
    return folded


def spread(table, section, heads, count):
    lane = iota((table.shape[0], LANES), 1)
    tiles = []
    for pair in range(count // 2):
        at = section * heads + 2 * pair
        tiles.append(jnp.where(lane < LANES // 2, table[:, at : at + 1], table[:, at + 1 : at + 2]))
    return jnp.concatenate(tiles, axis=1)


def front_kernel(
    parts, heads, rank, *refs,
):
    pieces, refs = refs[:parts], refs[parts:]
    (gain, w_maps, conv_maps, bias, rate, seg_row, w_gate, w_value, conv, skip, gate_gain, marks,
     normed, pre_state, maps, maps_t, per_head, rows_out, cross_t, value, gate, mixed, low_gated, memory, squares,
     proj, cross, state) = refs
    g = pl.program_id(0)
    length, quarter = pieces[0].shape
    width = quarter * parts
    blocks = length // SPAN
    states = maps.shape[1] // 2
    count = GROUP // 64
    lane = iota((SPAN, LANES), 1)

    @pl.when(g == 0)
    def _():
        squares[...] = jnp.zeros_like(squares)

        def normalise(b, _):
            at = pl.ds(pl.multiple_of(b * SPAN, SPAN), SPAN)
            wide = [piece[at, :].astype(F32) for piece in pieces]
            total = functools.reduce(jnp.add, [array * array for array in wide])
            scale = lax.rsqrt(jnp.sum(total, axis=1, keepdims=True) / width + EPSILON)
            per_head[at, :] = jnp.broadcast_to(scale, (SPAN, LANES))
            for k in range(parts):
                to = pl.multiple_of((rank[0] ^ k) * quarter, quarter)
                normed[at, pl.ds(to, quarter)] = (wide[k] * scale * gain[:, pl.ds(to, quarter)]).astype(BF16)
            return 0

        lax.fori_loop(0, blocks, normalise, 0, unroll=2)
        proj[...] = dot(normed[...], w_maps[...])

        def tables(b, _):
            start = pl.multiple_of(b * SPAN, SPAN)
            at = pl.ds(start, SPAN)
            mark = marks[at, :]
            now = proj[at, : 2 * states]
            pre_state[at, :] = now
            total, _ = conv_taps(rows_before(proj, start)[:, : 2 * states], now, mark, conv_maps[...])
            both = total * sigmoid(total)
            keys, queries = both[:, :states], both[:, states:]
            low_keys, low_queries = keys.astype(BF16), queries.astype(BF16)
            maps[at, :states] = low_keys
            maps[at, states:] = low_queries
            maps_t[:states, pl.ds(start, SPAN)] = keys.T.astype(BF16)
            maps_t[states:, pl.ds(start, SPAN)] = queries.T.astype(BF16)

            pre = proj[at, 2 * states :] + bias[...]
            size = jnp.maximum(pre, 0.0) + jnp.log1p(jnp.exp(-jnp.abs(pre)))
            rising = dot(tri(False), -rate[...] * size, precision=HIGHEST)
            entering = jnp.exp(rising) * mark[:, 3:4]
            leaving = jnp.exp(rising[SPAN - 1 :] - rising) * mark[:, 4:5]
            rising = rising * LOG2E
            section = lane // heads
            packed = jnp.where(section == 0, rising, entering)
            packed = jnp.where(section == 2, leaving, packed)
            packed = jnp.where(section == 3, size, packed)
            packed = jnp.where(section == 4, pre, packed)
            packed = jnp.where(section == 5, per_head[at, :], packed)
            per_head[at, :] = packed
            turned = rising.T
            for group in range(rows_out.shape[0]):
                rows_out[group, pl.ds(pl.multiple_of(b * 8, 8), 8), :] = turned[group * count : group * count + 8]
            same = mark[:, 6:7] == seg_row[0:1, pl.ds(start, SPAN)]
            rows, cols = iota((SPAN, SPAN), 0), iota((SPAN, SPAN), 1)
            cross[at, :] = jnp.where(same & (rows >= cols), dot(low_queries, low_keys, NT), 0.0)
            cross_t[at, :] = jnp.where(same & (rows <= cols), dot(low_keys, low_queries, NT), 0.0)
            return 0

        lax.fori_loop(0, blocks, tables, 0, unroll=2)

    both = dot(normed[...], jnp.concatenate([w_gate[...], w_value[...]], axis=1))
    gate[...] = both[:, :GROUP].astype(BF16)
    value[...] = both[:, GROUP:]
    state[...] = jnp.zeros_like(state)
    turn = lax.rem(LANES - count * g, LANES)

    def block(b, _):
        start = pl.multiple_of(b * SPAN, SPAN)
        at = pl.ds(start, SPAN)
        total, _ = conv_taps(rows_before(value, start), value[at, :], marks[at, :], conv[...])
        inputs = total * sigmoid(total)
        table = pltpu.roll(per_head[at, :], turn, 1)
        entering, leaving, size = (spread(table, s, heads, count) for s in (1, 2, 3))
        scaled = inputs * size
        keys_t = maps_t[0:states, pl.ds(start, SPAN)]
        queries = maps[at, states:]
        low_state = state[...].astype(BF16)
        memory[b] = low_state
        out = entering * dot(queries, low_state) + skip[...] * inputs
        rising_rows = rows_out[g, pl.ds(pl.multiple_of(b * 8, 8), 8), :]
        crossed = cross[at, :]
        parts_out = []
        for pair in range(count // 2):
            weights = []
            for j in (2 * pair, 2 * pair + 1):
                gap = jnp.minimum(table[:, j : j + 1] - rising_rows[j : j + 1, :], 0.0)
                weights.append((jnp.exp2(gap) * crossed).astype(BF16))
            tile = scaled[:, pair * LANES : (pair + 1) * LANES]
            stacked = jnp.concatenate(
                [
                    jnp.where(lane < LANES // 2, tile, 0.0).astype(BF16),
                    jnp.where(lane < LANES // 2, 0.0, tile).astype(BF16),
                ],
                axis=0,
            )
            parts_out.append(dot(jnp.concatenate(weights, axis=1), stacked))
        out = out + jnp.concatenate(parts_out, axis=1)
        fresh = dot(keys_t, (leaving * scaled).astype(BF16))
        state[...] = state[...] * entering[SPAN - 1 :] + fresh
        mixed[at, :] = out
        opened = gate[at, :].astype(F32)
        gated = out * (opened * sigmoid(opened))
        low_gated[at, :] = (gated * gate_gain[...]).astype(BF16)
        squares[at, :] += fold_lanes(gated * gated)
        return 0

    lax.fori_loop(0, blocks, block, 0, unroll=UNROLL)


def assemble(pieces, target, sems, where):
    copies = [
        pltpu.make_async_copy(pieces[k].at[:, pl.ds(at, size)], target.at[:, pl.ds(to, size)], sems.at[i])
        for i, (k, at, to, size) in enumerate(where)
    ]
    for copy in copies:
        copy.start()
    for copy in copies:
        copy.wait()


def cotangent_kernel(parts, rank, *refs):
    pieces, (w_out, gated, squares, grad, stats, sums, full, sems) = refs[:parts], refs[parts:]
    g = pl.program_id(0)
    length, quarter = pieces[0].shape

    @pl.when(g == 0)
    def _():
        sums[...] = jnp.zeros_like(sums)
        places = [pl.multiple_of((rank[0] ^ k) * quarter, quarter) for k in range(parts)]
        assemble(pieces, full, sems, [(k, 0, places[k], quarter) for k in range(parts)])

    grad[...] = dot(full[...], w_out[...], NT).astype(BF16)

    def chunk(i, _):
        at = pl.ds(pl.multiple_of(i * SPAN, SPAN), SPAN)
        sums[at, :] += fold_lanes(grad[at, :].astype(F32) * gated[at, :].astype(F32))
        return 0

    lax.fori_loop(0, length // SPAN, chunk, 0, unroll=2)

    @pl.when(g == pl.num_programs(0) - 1)
    def _():
        row = iota((8, LANES), 0)
        stats[...] = dot((row == 0).astype(F32), squares[...], NT, HIGHEST) + dot(
            (row == 1).astype(F32), sums[...], NT, HIGHEST
        )


def gate_kernel(parts, run, channels_all, stacked, place, rank, *refs):
    pieces, refs = refs[:parts], refs[parts:]
    (grad, gate, mixed, gain, stats, marks, low_mixed, grad_mixer, grad_gate, grad_gain), refs = refs[:10], refs[10:]
    targets, (sent, kept, sems) = refs[:-3], refs[-3:]
    length, quarter = pieces[0].shape
    grad_gain[...] = jnp.zeros_like(grad_gain)
    pairs = quarter // (2 * run)
    bits = (parts * pairs - 1).bit_length()
    copies = []
    for half, target in ((1, sent), (0, kept)):
        for k in range(parts):
            for j in range(pairs):
                at = pl.multiple_of((2 * j + (place[0] ^ half)) * run, run)
                to = pl.multiple_of(turned((rank[0] ^ k) * pairs + j, bits) * run, run)
                copies.append(
                    pltpu.make_async_copy(
                        pieces[k].at[:, pl.ds(at, run)], target.at[:, pl.ds(to, run)], sems.at[len(copies)]
                    )
                )

    @pl.when(pl.program_id(0) == 0)
    def _():
        for copy in copies:
            copy.start()

    def chunk(i, _):
        start = pl.multiple_of(i * SPAN, SPAN)
        at = pl.ds(start, SPAN)
        columns = jnp.concatenate([stats[:, pl.ds(start, SPAN)]] * (SPAN // 8), axis=0).T
        keep = marks[at, 5:6]
        scale = lax.rsqrt(columns[:, 0:1] / channels_all + EPSILON)
        factor = scale * keep
        pull = scale * scale * factor * columns[:, 1:2] / channels_all
        opened, out, now = gate[at, :].astype(F32), mixed[at, :], grad[at, :].astype(F32)
        chance = sigmoid(opened)
        swish = opened * chance
        gated = out * swish
        scaled = gated * factor
        low_mixed[at, :] = (scaled * gain[...]).astype(BF16)
        grad_gain[...] += jnp.sum(now * scaled, axis=0, keepdims=True)
        grad_gated = now * (factor * gain[...]) - gated * pull
        grad_mixer[at, :] = (grad_gated * swish).astype(BF16)
        grad_gate[at, :] = (grad_gated * out * chance * (1.0 + opened * (1.0 - chance))).astype(BF16)
        return 0

    lax.fori_loop(0, length // SPAN, chunk, 0, unroll=4)

    @pl.when(pl.program_id(0) == 0)
    def _():
        for copy in copies:
            copy.wait()

    for half, source in enumerate((sent, kept)):
        now = dot(low_mixed[...], source[...], TN).astype(BF16)
        if stacked:
            targets[0][half] = now
        else:
            targets[half][...] = now


def weight_kernel(place, left_send, left_own, *refs):
    right, targets = refs[:-2], refs[-2:]
    for left, target in zip((left_send, left_own), targets):
        at = 0
        for part in right:
            size = part.shape[1]
            target[:, at : at + size] = dot(left[...], part[...], TN).astype(BF16)
            at += size


def backward_kernel(
    heads, first, value, grad_out, mixed, memory, conv, skip, per_head, marks, rows_in, maps, maps_t, cross_t,
    grad_value, grad_conv, grad_skip, grad_cross, folded, grad_maps,
    later, grad_memory,
):
    g = pl.program_id(0) + first
    length = grad_out.shape[0]
    blocks = length // SPAN
    states = maps.shape[1] // 2
    count = GROUP // 64
    lane = iota((SPAN, LANES), 1)
    row = iota((SPAN, GROUP), 0)
    turn = lax.rem(LANES - count * g, LANES)
    channel, target = iota((GROUP, LANES), 0), iota((GROUP, LANES), 1)
    pick_rise = (target == count * g + channel // 64).astype(BF16)
    pick_size = (target == heads + count * g + channel // 64).astype(BF16)
    later[...] = jnp.zeros_like(later)
    grad_memory[...] = jnp.zeros_like(grad_memory)
    grad_conv[...] = jnp.zeros_like(grad_conv)
    grad_skip[...] = jnp.zeros_like(grad_skip)

    @pl.when(g == first)
    def _():
        grad_cross[...] = jnp.zeros_like(grad_cross)
        folded[...] = jnp.zeros_like(folded)
        grad_maps[...] = jnp.zeros_like(grad_maps)

    def block(i, _):
        b = blocks - 1 - i
        start = pl.multiple_of(b * SPAN, SPAN)
        at = pl.ds(start, SPAN)
        filters = conv[...]
        total, shifted = conv_taps(rows_before(value, start), value[at, :], marks[at, :], filters)
        chance = sigmoid(total)
        inputs = total * chance
        table = pltpu.roll(per_head[at, :], turn, 1)
        entering, leaving, size = (spread(table, s, heads, count) for s in (1, 2, 3))
        scaled = inputs * size
        low_scaled = scaled.astype(BF16)
        pulled = grad_out[at, :].astype(F32)
        keys, queries_t = maps[at, 0:states], maps_t[states:, pl.ds(start, SPAN)]
        memory_now = memory[b]
        grad_next = grad_memory[...]
        low_next = grad_next.astype(BF16)
        entered = (entering * pulled).astype(BF16)
        left = (leaving * scaled).astype(BF16)
        grad_maps[at, 0:states] += dot(left, low_next, NT)
        grad_maps[at, states:] += dot(entered, memory_now, NT)
        rising_rows = rows_in[0, pl.ds(pl.multiple_of(b * 8, 8), 8), :]
        crossed_t = cross_t[at, :]
        cross_sum = jnp.zeros((SPAN, SPAN), F32)
        parts = []
        for pair in range(count // 2):
            tile = pulled[:, pair * LANES : (pair + 1) * LANES]
            one = jnp.where(lane < LANES // 2, tile, 0.0).astype(BF16)
            two = jnp.where(lane < LANES // 2, 0.0, tile).astype(BF16)
            low_tile = low_scaled[:, pair * LANES : (pair + 1) * LANES]
            weights = []
            for j, masked in ((2 * pair, one), (2 * pair + 1, two)):
                gap = table[:, j : j + 1] - rising_rows[j : j + 1, :]
                cross_sum = cross_sum + jnp.exp2(jnp.minimum(gap, 0.0)) * dot(masked, low_tile, NT)
                weights.append((jnp.exp2(jnp.minimum(-gap, 0.0)) * crossed_t).astype(BF16))
            parts.append(dot(jnp.concatenate(weights, axis=1), jnp.concatenate([one, two], axis=0)))
        grad_cross[at, :] += cross_sum
        grad_within = jnp.concatenate(parts, axis=1)
        grad_left = dot(keys, low_next)
        grad_scaled = grad_within + leaving * grad_left
        scanned = mixed[at, :] - skip[...] * inputs
        kept = left.astype(F32) * grad_left
        rise = pulled * scanned - low_scaled.astype(F32) * grad_within - kept
        carried = entering[SPAN - 1 :] * jnp.sum(low_next.astype(F32) * memory_now.astype(F32), axis=0, keepdims=True)
        rise = rise + jnp.where(row == SPAN - 1, carried + jnp.sum(kept, axis=0, keepdims=True), 0.0)
        grown = grad_scaled * inputs
        summed = folded[at, :]
        for product, pick in ((rise, pick_rise), (grown, pick_size)):
            high = product.astype(BF16)
            rest = (product - high.astype(F32)).astype(BF16)
            summed = summed + dot(high, pick) + dot(rest, pick)
        folded[at, :] = summed
        grad_skip[...] += jnp.sum(pulled * inputs, axis=0, keepdims=True)
        grad_inputs = size * grad_scaled + skip[...] * pulled
        grad_total = grad_inputs * (chance * (1.0 + total * (1.0 - chance)))
        for k in range(4):
            grad_conv[k : k + 1] += jnp.sum(grad_total * shifted[k], axis=0, keepdims=True)
        grad_conv[4:5] += jnp.sum(grad_total, axis=0, keepdims=True)
        longer = jnp.concatenate([grad_total, later[...]], axis=0)
        later[...] = grad_total[:8]
        grad_value[at, :] = conv_back(longer, marks[pl.ds(start, SPAN + 8), :], filters).astype(BF16)
        grad_memory[...] = entering[SPAN - 1 :] * grad_next + dot(queries_t, entered)
        return 0

    lax.fori_loop(0, blocks, block, 0, unroll=UNROLL)


def finish_kernel(
    heads, calls, *refs,
):
    summed_parts, refs = refs[: 3 * calls], refs[3 * calls :]
    (per_head, marks, maps, seg_row, pre_state, conv_state, rate,
     grad_state, grad_step, grad_conv_state, grad_heads, later) = refs
    length = maps.shape[0]
    blocks = length // SPAN
    states = maps.shape[1] // 2
    later[...] = jnp.zeros_like(later)
    grad_conv_state[...] = jnp.zeros_like(grad_conv_state)
    grad_heads[...] = jnp.zeros_like(grad_heads)

    def block(i, _):
        start = pl.multiple_of((blocks - 1 - i) * SPAN, SPAN)
        at = pl.ds(start, SPAN)
        mark = marks[at, :]
        rows, cols = iota((SPAN, SPAN), 0), iota((SPAN, SPAN), 1)
        linked = (rows >= cols) & (mark[:, 6:7] == seg_row[0:1, pl.ds(start, SPAN)])
        grad_cross, summed, grad_maps = (
            functools.reduce(jnp.add, [ref[at, :] for ref in summed_parts[j::3]]) for j in range(3)
        )
        crossed = jnp.where(linked, grad_cross, 0.0)
        keys, queries = maps[at, 0:states], maps[at, states:]
        grad_keys = grad_maps[:, :states] + dot(crossed.T.astype(BF16), queries)
        grad_queries = grad_maps[:, states:] + dot(crossed.astype(BF16), keys)
        filters = conv_state[...]
        total, shifted = conv_taps(rows_before(pre_state, start), pre_state[at, :], mark, filters)
        chance = sigmoid(total)
        grad_total = jnp.concatenate([grad_keys, grad_queries], axis=1) * (chance * (1.0 + total * (1.0 - chance)))
        for k in range(4):
            grad_conv_state[k : k + 1] += jnp.sum(grad_total * shifted[k], axis=0, keepdims=True)
        grad_conv_state[4:5] += jnp.sum(grad_total, axis=0, keepdims=True)
        longer = jnp.concatenate([grad_total, later[...]], axis=0)
        later[...] = grad_total[:8]
        grad_state[at, :] = conv_back(longer, marks[pl.ds(start, SPAN + 8), :], filters).astype(BF16)

        table = per_head[at, :]
        grad_decay = dot(tri(True), summed, precision=HIGHEST)
        size = pltpu.roll(table, LANES - 3 * heads, 1)
        pre = pltpu.roll(table, LANES - 4 * heads, 1)
        grad_size = pltpu.roll(summed, LANES - heads, 1) - rate[...] * grad_decay
        valid = iota((SPAN, LANES), 1) < heads
        grad_pre = jnp.where(valid, grad_size * sigmoid(pre), 0.0)
        grad_step[at, :] = grad_pre.astype(BF16)
        grad_heads[0:1] += jnp.sum(grad_pre, axis=0, keepdims=True)
        grad_heads[1:2] += jnp.sum(-rate[...] * size * grad_decay, axis=0, keepdims=True)
        return 0

    lax.fori_loop(0, blocks, block, 0, unroll=UNROLL)


def put(far, near, total):
    step = pl.program_id(0)

    @pl.when(step < 2)
    def _():
        far[0] = total.astype(BF16)

    @pl.when(step >= 2)
    def _():
        near[0] = total.astype(BF16)


def output_kernel(rank, gated, w_out, far, near):
    put(far, near, dot(gated[...], w_out[...]))


def normed_kernel(chunks, rank, *refs):
    grads, (grad_state, grad_step, w_inner, w_maps), refs = refs[: 2 * chunks], refs[2 * chunks : 2 * chunks + 4], refs[2 * chunks + 4 :]
    outs, (joined, joined_maps) = refs[:-2], refs[-2:]

    @pl.when(pl.program_id(0) == 0)
    def _():
        for target, parts in ((joined, grads), (joined_maps, (grad_state, grad_step))):
            at = 0
            for part in parts:
                target[:, at : at + part.shape[1]] = part[...]
                at += part.shape[1]

    total = dot(joined[...], w_inner[...], NT) + dot(joined_maps[...], w_maps[...], NT)
    put(*outs, total)


def swap(array, axis, mask):
    count = lax.axis_size(axis)
    return lax.ppermute(array, axis, [(i, i ^ mask) for i in range(count)])


def gather_pieces(own, parts):
    pieces = {0: own}
    bit = parts // 2
    while bit >= 1:
        pieces.update({k | bit: swap(piece, "tensor", bit) for k, piece in list(pieces.items())})
        bit //= 2
    return [pieces[k] for k in range(parts)]


def tie(array, *first):
    return lax.optimization_barrier((array, *first))[0]


def meet(sums, *arrays):
    arrays = lax.optimization_barrier((*arrays, *(part.got for part in sums)))
    for part, got in zip(sums, arrays[len(arrays) - len(sums) :]):
        part.got = got
    return arrays[: len(arrays) - len(sums)]


def sum_all(array, axis):
    bit = 1
    while bit < lax.axis_size(axis):
        array = array + swap(array, axis, bit)
        bit *= 2
    return array


def rest_masks(low_bits):
    bits = (lax.axis_size("dp") - 1).bit_length()
    return [1 << bit for bit in (*range(low_bits + 1, bits), *range(low_bits - 1, -1, -1))]


def turned(index, bits):
    result = index * 0
    for bit in range(bits):
        result = result | (((index >> bit) & 1) << (bits - 1 - bit))
    return result


class Sum:
    def __init__(self, own, got, dim, low_bits):
        self.terms, self.got, self.dim, self.masks = [own], got, dim, rest_masks(low_bits)
        if got is None:
            self.send()

    def advance(self):
        self.terms.append(self.got)
        return self.send()

    def send(self):
        mask = self.masks.pop(0)
        top = (lax.axis_index("dp") & mask) // mask
        size = self.terms[0].shape[self.dim] // 2

        def cut(half):
            return [lax.dynamic_slice_in_dim(term, half * size, size, self.dim) for term in self.terms]

        sent = functools.reduce(jnp.add, [term.astype(F32) for term in cut(1 - top)]).astype(BF16)
        self.terms, self.got, self.sent = cut(top), swap(sent, "dp", mask), sent
        return sent

    def result(self):
        while self.masks:
            self.advance()
        return functools.reduce(jnp.add, [term.astype(F32) for term in (*self.terms, self.got)])


def add_low(left, right):
    return (left.astype(F32) + right.astype(F32)).astype(BF16)


def shards(
    tokens,
    cotangent,
    doc_lengths,
    norm_gain,
    w_inner,
    w_step,
    w_state,
    conv_inner,
    conv_state,
    step_bias,
    log_rate,
    skip_gain,
    gate_gain,
    w_out,
):
    parts = lax.axis_size("tensor")
    groups = lax.axis_size("dp")
    rank = lax.axis_index("tensor").astype(jnp.int32)
    ranks = rank.reshape(1)
    length, quarter = tokens.shape
    width = quarter * parts
    channels = w_inner.shape[2]
    heads = w_step.shape[1]
    states2 = w_state.shape[1]
    states = states2 // 2
    blocks = length // SPAN
    steps = channels // GROUP
    repeat = LANES // heads
    piece_rows = width // groups
    low_bits = 0
    while (piece_rows << low_bits) < LANES:
        low_bits += 1
    run = piece_rows << low_bits
    half_width = width // 2
    high_bits = (groups - 1).bit_length() - 1 - low_bits
    place = ((lax.axis_index("dp") >> low_bits) & 1).astype(jnp.int32).reshape(1)

    token_y = swap(tokens, "tensor", 2)
    grad_y = swap(tie(cotangent, token_y), "tensor", 2)
    flat = w_inner.reshape(width, 2 * channels)
    w_maps = jnp.concatenate([w_state, jnp.tile(w_step, (1, repeat))], axis=1)
    step_pad = jnp.pad(w_step, ((0, 0), (0, LANES - heads)))
    bias8 = jnp.tile(step_bias, repeat)[None, :]
    rate8 = jnp.exp(jnp.tile(log_rate, repeat))[None, :]
    skip_row = jnp.repeat(skip_gain, channels // heads)[None, :]
    gain_row = gate_gain[None, :]
    conv_pad = jnp.pad(conv_inner, ((0, 3), (0, 0)))
    conv_state_pad = jnp.pad(conv_state, ((0, 3), (0, 0)))

    doc_ends = jnp.cumsum(doc_lengths[0])
    positions = jnp.arange(length, dtype=jnp.int32)
    segment = jnp.sum((positions[:, None] >= doc_ends[None, :]).astype(jnp.int32), axis=1)
    present = positions < doc_ends[-1]
    by_block = segment.reshape(blocks, SPAN)
    final = by_block[:, -1:]
    before = jnp.concatenate([jnp.full((1, 1), -1, jnp.int32), final[:-1]], axis=0)
    marks = [
        jnp.concatenate([jnp.full((k,), -1, jnp.int32), segment[:-k]]) == segment for k in (1, 2, 3)
    ]
    marks += [(by_block == before).reshape(-1), (by_block == final).reshape(-1), present]
    marks = [mark.astype(F32) for mark in marks] + [segment.astype(F32)]
    marks = jnp.pad(jnp.stack(marks, axis=1), ((0, 8), (0, LANES - len(marks))))
    seg_row = jnp.broadcast_to(segment.astype(F32)[None, :], (8, length))

    token_y, flat, w_maps, step_pad, marks, seg_row, skip_row, conv_pad = lax.optimization_barrier(
        (token_y, flat, w_maps, step_pad, marks, seg_row, skip_row, conv_pad)
    )
    token_pieces = [tokens, swap(tokens, "tensor", 1), token_y, swap(token_y, "tensor", 1)]

    by_group = lambda rows: pl.BlockSpec((rows, GROUP), lambda g, *_: (0, g))
    (normed, pre_state, maps, maps_t, per_head, rising_rows, cross_t, value, gate, mixer_out, low_gated, memory, squares) = call(
        functools.partial(front_kernel, parts, heads),
        (steps,),
        [held((length, quarter))] * parts
        + [
            held((1, width)), held((width, states2 + LANES)), held((8, states2)),
            held((1, LANES)), held((1, LANES)), held((8, length)),
            pl.BlockSpec((width, GROUP), lambda g, *_: (0, g)), pl.BlockSpec((width, GROUP), lambda g, *_: (0, steps + g)),
            by_group(8), by_group(1), by_group(1), held((length + 8, LANES)),
        ],
        [
            held((length, width)), held((length, states2)), held((length, states2)), held((states2, length)),
            held((length, LANES)), held((steps, blocks * 8, SPAN)), held((length, SPAN)),
            by_group(length), by_group(length), by_group(length), by_group(length),
            pl.BlockSpec((blocks, states, GROUP), lambda g, *_: (0, 0, g)), held((length, LANES)),
        ],
        [
            shape_of(length, width, dtype=BF16), shape_of(length, states2), shape_of(length, states2, dtype=BF16),
            shape_of(states2, length, dtype=BF16), shape_of(length, LANES), shape_of(steps, blocks * 8, SPAN),
            shape_of(length, SPAN), shape_of(length, channels), shape_of(length, channels, dtype=BF16),
            shape_of(length, channels), shape_of(length, channels, dtype=BF16),
            shape_of(blocks, states, channels, dtype=BF16), shape_of(length, LANES),
        ],
        [
            pltpu.VMEM((length, states2 + LANES), F32), pltpu.VMEM((length, SPAN), F32),
            pltpu.VMEM((states, GROUP), F32),
        ],
        prefetch=1,
        flops=8 * length * width * channels,
        moved=length * width * 4 + width * channels * 4 + length * channels * 14,
        name="front",
        vmem=56,
    )(
        ranks, *token_pieces, norm_gain[None, :], w_maps, conv_state_pad, bias8, rate8, seg_row, flat, flat, conv_pad,
        skip_row, gain_row, marks,
    )

    grad_y = tie(grad_y, squares)
    grad_pieces = [cotangent, swap(cotangent, "tensor", 1), grad_y, swap(grad_y, "tensor", 1)]
    pieces_any = [pl.BlockSpec(memory_space=pl.ANY)] * parts
    double = 2 * GROUP
    by_double = lambda rows: pl.BlockSpec((rows, double), lambda g, *_: (0, g))
    grad_mixed, stats = call(
        functools.partial(cotangent_kernel, parts),
        (channels // double,),
        pieces_any
        + [
            pl.BlockSpec((double, width), lambda g, *_: (g, 0)),
            by_double(length), held((length, LANES)),
        ],
        [by_double(length), held((8, length))],
        [shape_of(length, channels, dtype=BF16), shape_of(8, length)],
        [pltpu.VMEM((length, LANES), F32), pltpu.VMEM((length, width), BF16), pltpu.SemaphoreType.DMA((parts,))],
        prefetch=1,
        flops=2 * length * width * channels,
        moved=length * width * 2 + width * channels * 2 + length * channels * 12,
        name="cotangent",
        vmem=56,
    )(ranks, *grad_pieces, w_out, low_gated, squares)
    spans = steps // CHUNKS

    def chunk_spec(rows, c):
        return pl.BlockSpec((rows, GROUP), lambda g, *_: (0, c * spans + g))

    def gate_part(c, stats, stacked):
        size = spans * GROUP
        if stacked:
            outs = [pl.BlockSpec((2, GROUP, half_width), lambda g, *_: (0, g, 0))]
            shapes = [shape_of(2, size, half_width, dtype=BF16)]
        else:
            outs = [pl.BlockSpec((GROUP, half_width), lambda g, *_: (g, 0))] * 2
            shapes = [shape_of(size, half_width, dtype=BF16)] * 2
        return call(
            functools.partial(gate_kernel, parts, run, channels * parts, stacked),
            (spans,),
            pieces_any
            + [
                chunk_spec(length, c), chunk_spec(length, c), chunk_spec(length, c), chunk_spec(1, c),
                held((8, length)), held((length + 8, LANES)),
            ],
            [by_group(length), by_group(length), by_group(length), by_group(1), *outs],
            [
                shape_of(length, size, dtype=BF16), shape_of(length, size, dtype=BF16),
                shape_of(length, size, dtype=BF16), shape_of(1, size), *shapes,
            ],
            [
                pltpu.VMEM((length, half_width), BF16), pltpu.VMEM((length, half_width), BF16),
                pltpu.SemaphoreType.DMA((width // run,)),
            ],
            prefetch=2,
            flops=2 * length * width * size,
            moved=length * width * 2 + length * size * 18 + width * size * 2,
            name="gate",
        )(place, ranks, *grad_pieces, grad_mixed, gate, mixer_out, gain_row, stats, marks)

    def weight_part(*right):
        runs = half_width // run
        columns = [part.shape[1] for part in right]
        out = pl.BlockSpec((run, sum(columns)), lambda j, p: (turned(j, (runs - 1).bit_length()), 0))
        shape = shape_of(half_width, sum(columns), dtype=BF16)
        return call(
            weight_kernel,
            (runs,),
            [
                pl.BlockSpec((length, run), lambda j, p: (0, 2 * j + (p[0] ^ 1))),
                pl.BlockSpec((length, run), lambda j, p: (0, 2 * j + p[0])),
            ]
            + [held((length, size)) for size in columns],
            [out, out],
            [shape, shape],
            prefetch=1,
            flops=2 * length * width * sum(columns),
            moved=length * width * 2 + length * sum(columns) * 2 + width * sum(columns) * 2,
            name="weights",
        )(place, normed, normed, *right)

    all_lanes = held((length, LANES))

    def backward_part(c, grad_out):
        size = spans * GROUP
        return call(
            functools.partial(backward_kernel, heads, c * spans),
            (spans,),
            [
                chunk_spec(length, c), by_group(length), chunk_spec(length, c),
                pl.BlockSpec((blocks, states, GROUP), lambda g, *_: (0, 0, c * spans + g)),
                chunk_spec(8, c), chunk_spec(1, c), all_lanes, held((length + 8, LANES)),
                pl.BlockSpec((1, blocks * 8, SPAN), lambda g, *_: (c * spans + g, 0, 0)),
                held((length, states2)), held((states2, length)), held((length, SPAN)),
            ],
            [by_group(length), by_group(8), by_group(1), held((length, SPAN)), all_lanes, held((length, states2))],
            [
                shape_of(length, size, dtype=BF16), shape_of(8, size), shape_of(1, size),
                shape_of(length, SPAN), shape_of(length, LANES), shape_of(length, states2),
            ],
            [pltpu.VMEM((8, GROUP), F32), pltpu.VMEM((states, GROUP), F32)],
            flops=40e9 / CHUNKS,
            moved=length * size * 14,
            name="backward",
            vmem=56,
        )(
            value, grad_out, mixer_out, memory, conv_pad, skip_row, per_head, marks, rising_rows, maps, maps_t,
            cross_t,
        )

    def piece_of(i, r):
        return r[0] ^ jnp.where(i == 0, 1, jnp.where(i == 1, 3, jnp.where(i == 2, 2, 0)))

    def far_near(count):
        specs = [
            pl.BlockSpec((1, length, quarter), lambda i, r: (jnp.minimum(i, 1), 0, 0)),
            pl.BlockSpec((1, length, quarter), lambda i, r: (jnp.maximum(i, 2) - 2, 0, 0)),
        ]
        return specs, [shape_of(2, length, quarter, dtype=BF16), shape_of(count, length, quarter, dtype=BF16)]

    def output_part(low_gated):
        return call(
            output_kernel,
            (4,),
            [held((length, channels)), pl.BlockSpec((channels, quarter), lambda i, r: (0, piece_of(i, r)))],
            *far_near(2),
            prefetch=1,
            flops=2 * length * channels * width,
            moved=length * channels * 2 + channels * width * 2 + length * width * 2,
            name="output",
        )(ranks, low_gated, w_out)

    def normed_part(grad_gate):
        grads = (*grad_gate, *grad_value)
        return call(
            functools.partial(normed_kernel, len(grad_gate)),
            (4,),
            [held((length, part.shape[1])) for part in grads]
            + [
                held((length, states2)), held((length, LANES)),
                pl.BlockSpec((quarter, 2 * channels), lambda i, r: (piece_of(i, r), 0)),
                pl.BlockSpec((quarter, states2 + LANES), lambda i, r: (piece_of(i, r), 0)),
            ],
            *far_near(2),
            [pltpu.VMEM((length, 2 * channels), BF16), pltpu.VMEM((length, states2 + LANES), BF16)],
            prefetch=1,
            flops=2 * length * (2 * channels + states2 + LANES) * width,
            moved=length * channels * 4 + channels * width * 4 + length * width * 2,
            name="normed_grad",
        )(ranks, *grads, grad_state, grad_step, flat, w_maps)

    def over_x(send):
        return swap(send, "dp", 1 << low_bits)

    stats = sum_all(stats, "tensor")

    first = gate_part(0, stats, False)
    sum_out = [Sum(first[5], over_x(first[4]), 1, low_bits)]
    other = gate_part(1, tie(stats, first[5]), False)
    sum_out.append(Sum(other[5], over_x(other[4]), 1, low_bits))
    low_mixed, grad_mixer, grad_gate, grad_gain = zip(first[:4], other[:4])
    gate_send, gate_own = weight_part(tie(grad_gate[0], other[5]), *grad_gate[1:])
    sum_gate = Sum(gate_own, over_x(gate_send), 0, low_bits)
    out_far, out_near = output_part(tie(low_gated, gate_own))

    out_far, out_near = meet(sum_out[:1], out_far, out_near)
    moved = [sum_out[0].advance(), out_far]
    out_far_got = swap(out_far, "tensor", 1)
    back = backward_part(0, tie(grad_mixer[0], *moved))

    grad_value, out_far_got = meet(sum_out, back[0], out_far_got)
    moved = [sum_out[1].advance(), sum_out[0].advance()]
    out_sum = add_low(out_near[0], out_far_got[1])
    out_y = swap(out_sum, "tensor", 2)
    value_send, value_own = weight_part(tie(grad_value, *moved, out_sum))
    sum_value = [Sum(value_own, over_x(value_send), 0, low_bits)]
    backs = [back, backward_part(1, tie(grad_mixer[1], value_own))]

    grad_value2, out_y = meet(sum_out, backs[1][0], out_y)
    total_out = [sum_out[0].result()]
    moved = [sum_out[1].advance(), total_out[0]]
    value_send2, value_own2 = weight_part(tie(grad_value2, *moved))
    sum_value.append(Sum(value_own2, over_x(value_send2), 0, low_bits))
    moved = [value_own2]
    grad_value, grad_conv, grad_skip, cross_parts, folded_parts, maps_parts = zip(*backs)
    (grad_state, grad_step, grad_conv_state, grad_heads) = call(
        functools.partial(finish_kernel, heads, CHUNKS),
        (1,),
        [held((length, SPAN)), all_lanes, held((length, states2))] * CHUNKS
        + [
            all_lanes, held((length + 8, LANES)), held((length, states2)), held((8, length)),
            held((length, states2)), held((8, states2)), held((1, LANES)),
        ],
        [held((length, states2)), all_lanes, held((8, states2)), held((8, LANES))],
        [
            shape_of(length, states2, dtype=BF16), shape_of(length, LANES, dtype=BF16),
            shape_of(8, states2), shape_of(8, LANES),
        ],
        [pltpu.VMEM((8, states2), F32)],
        flops=4e9,
        moved=length * 2048 * CHUNKS + length * 5000,
        name="finish",
        vmem=56,
    )(
        tie(cross_parts[0], *moved), folded_parts[0], maps_parts[0],
        *[part for three in zip(cross_parts[1:], folded_parts[1:], maps_parts[1:]) for part in three],
        per_head, marks, maps, seg_row, pre_state, conv_state_pad, rate8,
    )

    grad_state, grad_conv_state = meet([sum_gate, sum_out[1]], grad_state, grad_conv_state[:5])
    state_got = swap(grad_state, "tensor", 1)
    grad_conv_state = grad_conv_state + swap(grad_conv_state, "tensor", 1)
    conv_got = swap(grad_conv_state, "tensor", 2)
    total_out.append(sum_out[1].result())
    moved = [sum_gate.advance(), grad_state, total_out[1], grad_conv_state]
    near_far, near = normed_part([tie(grad_gate[0], *moved), *grad_gate[1:]])

    near_far, near, state_got, conv_got = meet([sum_value[0], sum_gate], near_far, near, state_got, conv_got)
    near_far_got = swap(near_far, "tensor", 1)
    state_sum = add_low(grad_state, state_got)
    state_got = swap(state_sum, "tensor", 2)
    grad_conv_state = grad_conv_state + conv_got
    moved = [sum_value[0].advance(), sum_gate.advance(), state_sum]
    near, near_far_got, *_ = lax.optimization_barrier((near, near_far_got, *moved))
    near_sum = add_low(near[0], near_far_got[1])
    over_y = swap(near_sum, "tensor", 2)
    late = (
        grad_step, norm_gain, grad_conv_state, grad_heads, normed, state_got,
        grad_conv, grad_skip, grad_gain, stats, marks, per_head,
    )
    (
        grad_step, norm_gain, grad_conv_state, grad_heads, normed, state_got,
        grad_conv, grad_skip, grad_gain, stats, marks, per_head,
    ) = lax.optimization_barrier((late, near_sum))[0]
    state_all = add_low(state_sum, state_got)
    own_rows = piece_rows // parts
    grad_w_state = dot(normed, state_all, TN).astype(BF16)
    grad_w_state = lax.dynamic_slice_in_dim(
        grad_w_state.reshape(groups, parts, own_rows, states2), rank, 1, axis=1
    )
    grad_w_step = dot(grad_step[:, :heads], normed, TN).astype(BF16)
    grad_w_state, grad_w_step, grad_conv, grad_skip, grad_gain, stats, marks = meet(
        sum_value, grad_w_state, grad_w_step, grad_conv, grad_skip, grad_gain, stats, marks
    )
    moved = [sum_value[1].advance(), sum_value[0].advance()]
    (grad_w_state, grad_w_step, grad_conv, grad_skip, grad_gain, stats, marks), _ = lax.optimization_barrier(
        ((grad_w_state, grad_w_step, grad_conv, grad_skip, grad_gain, stats, marks), moved)
    )
    grad_w_step = grad_w_step.reshape(heads, groups, piece_rows).transpose(1, 0, 2)
    small = jnp.concatenate(
        [grad_w_state.reshape(groups, own_rows * states2), grad_w_step.reshape(groups, heads * piece_rows)], axis=1
    ).reshape(groups // (2 << low_bits), 2, 1 << low_bits, -1)
    small = jnp.stack([small[turned(j, high_bits)] for j in range(small.shape[0])])
    small_own = lax.dynamic_slice_in_dim(small, place[0], 1, 1).reshape(groups // 2, -1)
    small_send = lax.dynamic_slice_in_dim(small, 1 - place[0], 1, 1).reshape(groups // 2, -1)
    small_sum = Sum(small_own, over_x(small_send), 0, low_bits)
    grad_conv, grad_skip, grad_gate_gain = (
        jnp.concatenate(array, axis=1) for array in (grad_conv, grad_skip, grad_gain)
    )
    skip_sums = jnp.sum(grad_skip.reshape(heads, channels // heads), axis=1)
    pieces = [
        grad_conv[:5].reshape(-1), grad_conv_state.reshape(-1), grad_heads[0, :heads], grad_heads[1, :heads],
        skip_sums, grad_gate_gain[0],
    ]
    rest = jnp.concatenate(pieces)
    scale_out = lax.rsqrt(stats[0] / (channels * parts) + EPSILON)
    factor = scale_out * marks[:length, 5]
    branch = out_near[1].astype(F32) + out_far_got[0].astype(F32) + out_y.astype(F32)
    own_tokens = tokens.astype(F32)
    output = (own_tokens + factor[:, None] * branch).astype(BF16)

    over_y, small_send, rest, output = meet([sum_value[1], sum_gate, small_sum], over_y, small_send, rest, output)
    moved = [sum_value[1].advance(), small_sum.advance()]
    total_gate = sum_gate.result()
    over_y = tie(over_y, *moved)
    grad_normed = near[1].astype(F32) + near_far_got[0].astype(F32) + over_y.astype(F32)
    own_gain = lax.dynamic_slice_in_dim(norm_gain, rank * quarter, quarter, 0)
    scale_in = per_head[:, 5 * heads : 5 * heads + 1]
    row_norm = jnp.sum(own_tokens * own_gain * grad_normed, axis=1)
    grad_norm_gain = jnp.sum(grad_normed * own_tokens * scale_in, axis=0)
    pack = jnp.concatenate([grad_norm_gain, rest])
    pieces = [grad_norm_gain, *pieces]

    row_got, pack_got = swap(row_norm, "tensor", 1), swap(pack, "dp", 1)
    row_norm, row_got, pack, pack_got = meet([*sum_value, small_sum], row_norm, row_got, pack, pack_got)
    moved = [small_sum.advance()]
    row_norm, pack = row_norm + row_got, pack + pack_got
    row_got, pack_got = swap(row_norm, "tensor", 2), swap(pack, "dp", 2)
    total_value = [part.result() for part in sum_value]
    row_norm, row_got, pack, pack_got, *_ = lax.optimization_barrier((row_norm, row_got, pack, pack_got, *total_value, *moved))
    row_norm, pack = row_norm + row_got, pack + pack_got
    bit = 4
    while bit < groups:
        pack = pack + swap(pack, "dp", bit)
        bit *= 2
    grad_tokens = (
        cotangent.astype(F32)
        + scale_in * own_gain * grad_normed
        - own_tokens * scale_in**3 * row_norm[:, None] / width
    ).astype(BF16)
    small_sum = small_sum.result()[0]
    sum_state = small_sum[: own_rows * states2].reshape(own_rows, states2)
    sum_step = small_sum[own_rows * states2 :].reshape(heads, piece_rows).T

    sum_out = jnp.concatenate(total_out, axis=0)
    sum_gate = total_gate
    sum_value = jnp.concatenate(total_value, axis=1)
    sum_inner = jnp.stack([sum_gate, sum_value], axis=1)

    split = []
    at = 0
    for piece in pieces:
        split.append(pack[at : at + piece.shape[0]])
        at += piece.shape[0]
    return (
        output,
        grad_tokens,
        split[0],
        sum_inner,
        sum_step,
        sum_state,
        split[1].reshape(5, channels),
        split[2].reshape(5, states2),
        split[3],
        split[4],
        split[5],
        split[6],
        sum_out,
    )


def solution(mesh):
    placed = (
        P("dp", "tensor"),
        P("dp", "tensor"),
        P("dp", None),
        P(),
        P(None, None, "tensor"),
        P(None, "tensor"),
        P(),
        P(None, "tensor"),
        P(),
        P("tensor"),
        P("tensor"),
        P("tensor"),
        P("tensor"),
        P("tensor", None),
    )
    return jax.shard_map(
        shards,
        mesh=mesh,
        in_specs=placed,
        out_specs=(
            P("dp", "tensor"),
            P("dp", "tensor"),
            P("tensor"),
            P("dp", None, "tensor"),
            P("dp", "tensor"),
            P(("dp", "tensor"), None),
            P(None, "tensor"),
            P(),
            P("tensor"),
            P("tensor"),
            P("tensor"),
            P("tensor"),
            P("tensor", "dp"),
        ),
        check_vma=False,
    )
```

```python
import functools
import math

import jax
import jax.numpy as jnp
from jax import lax
from jax.experimental import pallas as pl
from jax.experimental.pallas import tpu as pltpu
from jax.sharding import PartitionSpec as P

F32 = jnp.float32
BF16 = jnp.bfloat16
HIGHEST = lax.Precision.HIGHEST
EPSILON = 1e-05
LOG2E = math.log2(math.e)
LANES = 128
SPAN = 128
GROUP = 256
UNROLL = 8
HINT = 0.02
ROWS = 512
CHUNKS = 2

NN = (((1,), (0,)), ((), ()))
NT = (((1,), (1,)), ((), ()))
TN = (((0,), (0,)), ((), ()))


def dot(left, right, dims=NN, precision=None):
    return lax.dot_general(left, right, dims, precision=precision, preferred_element_type=F32)


def sigmoid(a):
    return 0.5 * jnp.tanh(0.5 * a) + 0.5


def iota(shape, dim):
    return lax.broadcasted_iota(jnp.int32, shape, dim)


def tri(upper):
    rows, cols = iota((SPAN, SPAN), 0), iota((SPAN, SPAN), 1)
    return ((rows <= cols) if upper else (rows >= cols)).astype(F32)


def call(body, grid, in_specs, out_specs, out_shape, scratch=(), prefetch=0, flops=0, moved=0, name=None, vmem=56):
    return pl.pallas_call(
        body,
        grid_spec=pltpu.PrefetchScalarGridSpec(
            num_scalar_prefetch=prefetch,
            grid=grid,
            in_specs=in_specs,
            out_specs=out_specs,
            scratch_shapes=list(scratch),
        ),
        out_shape=out_shape,
        compiler_params=pltpu.CompilerParams(
            vmem_limit_bytes=vmem * 1024 * 1024, dimension_semantics=("arbitrary",) * len(grid)
        ),
        cost_estimate=pl.CostEstimate(
            flops=int(flops * HINT), bytes_accessed=int(moved * HINT), transcendentals=0
        ),
        name=name,
    )


def held(shape):
    zeros = (0,) * len(shape)
    return pl.BlockSpec(shape, lambda *_: zeros, pipeline_mode=pl.Buffered(1))


def shape_of(*dims, dtype=F32):
    return jax.ShapeDtypeStruct(dims, dtype)


def conv_taps(before, now, marks, filters):
    rows = now.shape[0]
    wide = jnp.concatenate([before, now], axis=0)
    total = filters[4:5] + filters[0:1] * now
    shifted = [now]
    for k in range(1, 4):
        moved = wide[8 - k : 8 - k + rows] * marks[:, k - 1 : k]
        shifted.append(moved)
        total = total + filters[k : k + 1] * moved
    return total, shifted


def rows_before(array, start):
    return array[pl.ds(pl.multiple_of(jnp.maximum(start - 8, 0), 8), 8), :]


def conv_back(later, marks, filters):
    rows = later.shape[0] - 8
    total = filters[0:1] * later[:rows]
    for k in range(1, 4):
        total = total + filters[k : k + 1] * (later[k : k + rows] * marks[k : k + rows, k - 1 : k])
    return total


def fold_lanes(power):
    folded = power[:, :LANES]
    for tile in range(1, power.shape[1] // LANES):
        folded = folded + power[:, tile * LANES : (tile + 1) * LANES]
    return folded


def spread(table, section, heads, count):
    lane = iota((table.shape[0], LANES), 1)
    tiles = []
    for pair in range(count // 2):
        at = section * heads + 2 * pair
        tiles.append(jnp.where(lane < LANES // 2, table[:, at : at + 1], table[:, at + 1 : at + 2]))
    return jnp.concatenate(tiles, axis=1)


def front_kernel(
    parts, heads, rank, *refs,
):
    pieces, refs = refs[:parts], refs[parts:]
    (gain, w_maps, conv_maps, bias, rate, seg_row, w_gate, w_value, conv, skip, gate_gain, marks,
     normed, pre_state, maps, maps_t, per_head, rows_out, cross_t, value, gate, mixed, low_gated, memory, squares,
     proj, cross, state) = refs
    g = pl.program_id(0)
    length, quarter = pieces[0].shape
    width = quarter * parts
    blocks = length // SPAN
    states = maps.shape[1] // 2
    count = GROUP // 64
    lane = iota((SPAN, LANES), 1)

    @pl.when(g == 0)
    def _():
        squares[...] = jnp.zeros_like(squares)

        def normalise(b, _):
            at = pl.ds(pl.multiple_of(b * SPAN, SPAN), SPAN)
            wide = [piece[at, :].astype(F32) for piece in pieces]
            total = functools.reduce(jnp.add, [array * array for array in wide])
            scale = lax.rsqrt(jnp.sum(total, axis=1, keepdims=True) / width + EPSILON)
            per_head[at, :] = jnp.broadcast_to(scale, (SPAN, LANES))
            for k in range(parts):
                to = pl.multiple_of((rank[0] ^ k) * quarter, quarter)
                normed[at, pl.ds(to, quarter)] = (wide[k] * scale * gain[:, pl.ds(to, quarter)]).astype(BF16)
            return 0

        lax.fori_loop(0, blocks, normalise, 0, unroll=2)
        proj[...] = dot(normed[...], w_maps[...])

        def tables(b, _):
            start = pl.multiple_of(b * SPAN, SPAN)
            at = pl.ds(start, SPAN)
            mark = marks[at, :]
            now = proj[at, : 2 * states]
            pre_state[at, :] = now
            total, _ = conv_taps(rows_before(proj, start)[:, : 2 * states], now, mark, conv_maps[...])
            both = total * sigmoid(total)
            keys, queries = both[:, :states], both[:, states:]
            low_keys, low_queries = keys.astype(BF16), queries.astype(BF16)
            maps[at, :states] = low_keys
            maps[at, states:] = low_queries
            maps_t[:states, pl.ds(start, SPAN)] = keys.T.astype(BF16)
            maps_t[states:, pl.ds(start, SPAN)] = queries.T.astype(BF16)

            pre = proj[at, 2 * states :] + bias[...]
            size = jnp.maximum(pre, 0.0) + jnp.log1p(jnp.exp(-jnp.abs(pre)))
            rising = dot(tri(False), -rate[...] * size, precision=HIGHEST)
            entering = jnp.exp(rising) * mark[:, 3:4]
            leaving = jnp.exp(rising[SPAN - 1 :] - rising) * mark[:, 4:5]
            rising = rising * LOG2E
            section = lane // heads
            packed = jnp.where(section == 0, rising, entering)
            packed = jnp.where(section == 2, leaving, packed)
            packed = jnp.where(section == 3, size, packed)
            packed = jnp.where(section == 4, pre, packed)
            packed = jnp.where(section == 5, per_head[at, :], packed)
            per_head[at, :] = packed
            turned = rising.T
            for group in range(rows_out.shape[0]):
                rows_out[group, pl.ds(pl.multiple_of(b * 8, 8), 8), :] = turned[group * count : group * count + 8]
            same = mark[:, 6:7] == seg_row[0:1, pl.ds(start, SPAN)]
            rows, cols = iota((SPAN, SPAN), 0), iota((SPAN, SPAN), 1)
            cross[at, :] = jnp.where(same & (rows >= cols), dot(low_queries, low_keys, NT), 0.0)
            cross_t[at, :] = jnp.where(same & (rows <= cols), dot(low_keys, low_queries, NT), 0.0)
            return 0

        lax.fori_loop(0, blocks, tables, 0, unroll=2)

    both = dot(normed[...], jnp.concatenate([w_gate[...], w_value[...]], axis=1))
    gate[...] = both[:, :GROUP].astype(BF16)
    value[...] = both[:, GROUP:]
    state[...] = jnp.zeros_like(state)
    turn = lax.rem(LANES - count * g, LANES)

    def block(b, _):
        start = pl.multiple_of(b * SPAN, SPAN)
        at = pl.ds(start, SPAN)
        total, _ = conv_taps(rows_before(value, start), value[at, :], marks[at, :], conv[...])
        inputs = total * sigmoid(total)
        table = pltpu.roll(per_head[at, :], turn, 1)
        entering, leaving, size = (spread(table, s, heads, count) for s in (1, 2, 3))
        scaled = inputs * size
        keys_t = maps_t[0:states, pl.ds(start, SPAN)]
        queries = maps[at, states:]
        low_state = state[...].astype(BF16)
        memory[b] = low_state
        out = entering * dot(queries, low_state) + skip[...] * inputs
        rising_rows = rows_out[g, pl.ds(pl.multiple_of(b * 8, 8), 8), :]
        crossed = cross[at, :]
        parts_out = []
        for pair in range(count // 2):
            weights = []
            for j in (2 * pair, 2 * pair + 1):
                gap = jnp.minimum(table[:, j : j + 1] - rising_rows[j : j + 1, :], 0.0)
                weights.append((jnp.exp2(gap) * crossed).astype(BF16))
            tile = scaled[:, pair * LANES : (pair + 1) * LANES]
            stacked = jnp.concatenate(
                [
                    jnp.where(lane < LANES // 2, tile, 0.0).astype(BF16),
                    jnp.where(lane < LANES // 2, 0.0, tile).astype(BF16),
                ],
                axis=0,
            )
            parts_out.append(dot(jnp.concatenate(weights, axis=1), stacked))
        out = out + jnp.concatenate(parts_out, axis=1)
        fresh = dot(keys_t, (leaving * scaled).astype(BF16))
        state[...] = state[...] * entering[SPAN - 1 :] + fresh
        mixed[at, :] = out
        opened = gate[at, :].astype(F32)
        gated = out * (opened * sigmoid(opened))
        low_gated[at, :] = (gated * gate_gain[...]).astype(BF16)
        squares[at, :] += fold_lanes(gated * gated)
        return 0

    lax.fori_loop(0, blocks, block, 0, unroll=UNROLL)


def assemble(pieces, target, sems, where):
    copies = [
        pltpu.make_async_copy(pieces[k].at[:, pl.ds(at, size)], target.at[:, pl.ds(to, size)], sems.at[i])
        for i, (k, at, to, size) in enumerate(where)
    ]
    for copy in copies:
        copy.start()
    for copy in copies:
        copy.wait()


def cotangent_kernel(parts, rank, *refs):
    pieces, (w_out, gated, squares, grad, stats, sums, full, sems) = refs[:parts], refs[parts:]
    g = pl.program_id(0)
    length, quarter = pieces[0].shape

    @pl.when(g == 0)
    def _():
        sums[...] = jnp.zeros_like(sums)
        places = [pl.multiple_of((rank[0] ^ k) * quarter, quarter) for k in range(parts)]
        assemble(pieces, full, sems, [(k, 0, places[k], quarter) for k in range(parts)])

    grad[...] = dot(full[...], w_out[...], NT).astype(BF16)

    def chunk(i, _):
        at = pl.ds(pl.multiple_of(i * SPAN, SPAN), SPAN)
        sums[at, :] += fold_lanes(grad[at, :].astype(F32) * gated[at, :].astype(F32))
        return 0

    lax.fori_loop(0, length // SPAN, chunk, 0, unroll=2)

    @pl.when(g == pl.num_programs(0) - 1)
    def _():
        row = iota((8, LANES), 0)
        stats[...] = dot((row == 0).astype(F32), squares[...], NT, HIGHEST) + dot(
            (row == 1).astype(F32), sums[...], NT, HIGHEST
        )


def gate_kernel(parts, run, channels_all, stacked, place, rank, *refs):
    pieces, refs = refs[:parts], refs[parts:]
    (grad, gate, mixed, gain, stats, marks, low_mixed, grad_mixer, grad_gate, grad_gain), refs = refs[:10], refs[10:]
    targets, (sent, kept, sems) = refs[:-3], refs[-3:]
    length, quarter = pieces[0].shape
    grad_gain[...] = jnp.zeros_like(grad_gain)
    pairs = quarter // (2 * run)
    bits = (parts * pairs - 1).bit_length()
    copies = []
    for half, target in ((1, sent), (0, kept)):
        for k in range(parts):
            for j in range(pairs):
                at = pl.multiple_of((2 * j + (place[0] ^ half)) * run, run)
                to = pl.multiple_of(turned((rank[0] ^ k) * pairs + j, bits) * run, run)
                copies.append(
                    pltpu.make_async_copy(
                        pieces[k].at[:, pl.ds(at, run)], target.at[:, pl.ds(to, run)], sems.at[len(copies)]
                    )
                )

    @pl.when(pl.program_id(0) == 0)
    def _():
        for copy in copies:
            copy.start()

    def chunk(i, _):
        start = pl.multiple_of(i * SPAN, SPAN)
        at = pl.ds(start, SPAN)
        columns = jnp.concatenate([stats[:, pl.ds(start, SPAN)]] * (SPAN // 8), axis=0).T
        keep = marks[at, 5:6]
        scale = lax.rsqrt(columns[:, 0:1] / channels_all + EPSILON)
        factor = scale * keep
        pull = scale * scale * factor * columns[:, 1:2] / channels_all
        opened, out, now = gate[at, :].astype(F32), mixed[at, :], grad[at, :].astype(F32)
        chance = sigmoid(opened)
        swish = opened * chance
        gated = out * swish
        scaled = gated * factor
        low_mixed[at, :] = (scaled * gain[...]).astype(BF16)
        grad_gain[...] += jnp.sum(now * scaled, axis=0, keepdims=True)
        grad_gated = now * (factor * gain[...]) - gated * pull
        grad_mixer[at, :] = (grad_gated * swish).astype(BF16)
        grad_gate[at, :] = (grad_gated * out * chance * (1.0 + opened * (1.0 - chance))).astype(BF16)
        return 0

    lax.fori_loop(0, length // SPAN, chunk, 0, unroll=4)

    @pl.when(pl.program_id(0) == 0)
    def _():
        for copy in copies:
            copy.wait()

    for half, source in enumerate((sent, kept)):
        now = dot(low_mixed[...], source[...], TN).astype(BF16)
        if stacked:
            targets[0][half] = now
        else:
            targets[half][...] = now


def weight_kernel(place, left_send, left_own, *refs):
    right, targets = refs[:-2], refs[-2:]
    for left, target in zip((left_send, left_own), targets):
        at = 0
        for part in right:
            size = part.shape[1]
            target[:, at : at + size] = dot(left[...], part[...], TN).astype(BF16)
            at += size


def backward_kernel(
    heads, first, value, grad_out, mixed, memory, conv, skip, per_head, marks, rows_in, maps, maps_t, cross_t,
    grad_value, grad_conv, grad_skip, grad_cross, folded, grad_maps,
    later, grad_memory,
):
    g = pl.program_id(0) + first
    length = grad_out.shape[0]
    blocks = length // SPAN
    states = maps.shape[1] // 2
    count = GROUP // 64
    lane = iota((SPAN, LANES), 1)
    row = iota((SPAN, GROUP), 0)
    turn = lax.rem(LANES - count * g, LANES)
    channel, target = iota((GROUP, LANES), 0), iota((GROUP, LANES), 1)
    pick_rise = (target == count * g + channel // 64).astype(BF16)
    pick_size = (target == heads + count * g + channel // 64).astype(BF16)
    later[...] = jnp.zeros_like(later)
    grad_memory[...] = jnp.zeros_like(grad_memory)
    grad_conv[...] = jnp.zeros_like(grad_conv)
    grad_skip[...] = jnp.zeros_like(grad_skip)

    @pl.when(g == first)
    def _():
        grad_cross[...] = jnp.zeros_like(grad_cross)
        folded[...] = jnp.zeros_like(folded)
        grad_maps[...] = jnp.zeros_like(grad_maps)

    def block(i, _):
        b = blocks - 1 - i
        start = pl.multiple_of(b * SPAN, SPAN)
        at = pl.ds(start, SPAN)
        filters = conv[...]
        total, shifted = conv_taps(rows_before(value, start), value[at, :], marks[at, :], filters)
        chance = sigmoid(total)
        inputs = total * chance
        table = pltpu.roll(per_head[at, :], turn, 1)
        entering, leaving, size = (spread(table, s, heads, count) for s in (1, 2, 3))
        scaled = inputs * size
        low_scaled = scaled.astype(BF16)
        pulled = grad_out[at, :].astype(F32)
        keys, queries_t = maps[at, 0:states], maps_t[states:, pl.ds(start, SPAN)]
        memory_now = memory[b]
        grad_next = grad_memory[...]
        low_next = grad_next.astype(BF16)
        entered = (entering * pulled).astype(BF16)
        left = (leaving * scaled).astype(BF16)
        grad_maps[at, 0:states] += dot(left, low_next, NT)
        grad_maps[at, states:] += dot(entered, memory_now, NT)
        rising_rows = rows_in[0, pl.ds(pl.multiple_of(b * 8, 8), 8), :]
        crossed_t = cross_t[at, :]
        cross_sum = jnp.zeros((SPAN, SPAN), F32)
        parts = []
        for pair in range(count // 2):
            tile = pulled[:, pair * LANES : (pair + 1) * LANES]
            one = jnp.where(lane < LANES // 2, tile, 0.0).astype(BF16)
            two = jnp.where(lane < LANES // 2, 0.0, tile).astype(BF16)
            low_tile = low_scaled[:, pair * LANES : (pair + 1) * LANES]
            weights = []
            for j, masked in ((2 * pair, one), (2 * pair + 1, two)):
                gap = table[:, j : j + 1] - rising_rows[j : j + 1, :]
                cross_sum = cross_sum + jnp.exp2(jnp.minimum(gap, 0.0)) * dot(masked, low_tile, NT)
                weights.append((jnp.exp2(jnp.minimum(-gap, 0.0)) * crossed_t).astype(BF16))
            parts.append(dot(jnp.concatenate(weights, axis=1), jnp.concatenate([one, two], axis=0)))
        grad_cross[at, :] += cross_sum
        grad_within = jnp.concatenate(parts, axis=1)
        grad_left = dot(keys, low_next)
        grad_scaled = grad_within + leaving * grad_left
        scanned = mixed[at, :] - skip[...] * inputs
        kept = left.astype(F32) * grad_left
        rise = pulled * scanned - low_scaled.astype(F32) * grad_within - kept
        carried = entering[SPAN - 1 :] * jnp.sum(low_next.astype(F32) * memory_now.astype(F32), axis=0, keepdims=True)
        rise = rise + jnp.where(row == SPAN - 1, carried + jnp.sum(kept, axis=0, keepdims=True), 0.0)
        grown = grad_scaled * inputs
        summed = folded[at, :]
        for product, pick in ((rise, pick_rise), (grown, pick_size)):
            high = product.astype(BF16)
            rest = (product - high.astype(F32)).astype(BF16)
            summed = summed + dot(high, pick) + dot(rest, pick)
        folded[at, :] = summed
        grad_skip[...] += jnp.sum(pulled * inputs, axis=0, keepdims=True)
        grad_inputs = size * grad_scaled + skip[...] * pulled
        grad_total = grad_inputs * (chance * (1.0 + total * (1.0 - chance)))
        for k in range(4):
            grad_conv[k : k + 1] += jnp.sum(grad_total * shifted[k], axis=0, keepdims=True)
        grad_conv[4:5] += jnp.sum(grad_total, axis=0, keepdims=True)
        longer = jnp.concatenate([grad_total, later[...]], axis=0)
        later[...] = grad_total[:8]
        grad_value[at, :] = conv_back(longer, marks[pl.ds(start, SPAN + 8), :], filters).astype(BF16)
        grad_memory[...] = entering[SPAN - 1 :] * grad_next + dot(queries_t, entered)
        return 0

    lax.fori_loop(0, blocks, block, 0, unroll=UNROLL)


def finish_kernel(
    heads, calls, *refs,
):
    summed_parts, refs = refs[: 3 * calls], refs[3 * calls :]
    (per_head, marks, maps, seg_row, pre_state, conv_state, rate,
     grad_state, grad_step, grad_conv_state, grad_heads, later) = refs
    length = maps.shape[0]
    blocks = length // SPAN
    states = maps.shape[1] // 2
    later[...] = jnp.zeros_like(later)
    grad_conv_state[...] = jnp.zeros_like(grad_conv_state)
    grad_heads[...] = jnp.zeros_like(grad_heads)

    def block(i, _):
        start = pl.multiple_of((blocks - 1 - i) * SPAN, SPAN)
        at = pl.ds(start, SPAN)
        mark = marks[at, :]
        rows, cols = iota((SPAN, SPAN), 0), iota((SPAN, SPAN), 1)
        linked = (rows >= cols) & (mark[:, 6:7] == seg_row[0:1, pl.ds(start, SPAN)])
        grad_cross, summed, grad_maps = (
            functools.reduce(jnp.add, [ref[at, :] for ref in summed_parts[j::3]]) for j in range(3)
        )
        crossed = jnp.where(linked, grad_cross, 0.0)
        keys, queries = maps[at, 0:states], maps[at, states:]
        grad_keys = grad_maps[:, :states] + dot(crossed.T.astype(BF16), queries)
        grad_queries = grad_maps[:, states:] + dot(crossed.astype(BF16), keys)
        filters = conv_state[...]
        total, shifted = conv_taps(rows_before(pre_state, start), pre_state[at, :], mark, filters)
        chance = sigmoid(total)
        grad_total = jnp.concatenate([grad_keys, grad_queries], axis=1) * (chance * (1.0 + total * (1.0 - chance)))
        for k in range(4):
            grad_conv_state[k : k + 1] += jnp.sum(grad_total * shifted[k], axis=0, keepdims=True)
        grad_conv_state[4:5] += jnp.sum(grad_total, axis=0, keepdims=True)
        longer = jnp.concatenate([grad_total, later[...]], axis=0)
        later[...] = grad_total[:8]
        grad_state[at, :] = conv_back(longer, marks[pl.ds(start, SPAN + 8), :], filters).astype(BF16)

        table = per_head[at, :]
        grad_decay = dot(tri(True), summed, precision=HIGHEST)
        size = pltpu.roll(table, LANES - 3 * heads, 1)
        pre = pltpu.roll(table, LANES - 4 * heads, 1)
        grad_size = pltpu.roll(summed, LANES - heads, 1) - rate[...] * grad_decay
        valid = iota((SPAN, LANES), 1) < heads
        grad_pre = jnp.where(valid, grad_size * sigmoid(pre), 0.0)
        grad_step[at, :] = grad_pre.astype(BF16)
        grad_heads[0:1] += jnp.sum(grad_pre, axis=0, keepdims=True)
        grad_heads[1:2] += jnp.sum(-rate[...] * size * grad_decay, axis=0, keepdims=True)
        return 0

    lax.fori_loop(0, blocks, block, 0, unroll=UNROLL)


def put(far, near, total):
    step = pl.program_id(0)

    @pl.when(step < 2)
    def _():
        far[0] = total.astype(BF16)

    @pl.when(step >= 2)
    def _():
        near[0] = total.astype(BF16)


def output_kernel(rank, gated, w_out, far, near):
    put(far, near, dot(gated[...], w_out[...]))


def normed_kernel(chunks, rank, *refs):
    grads, (grad_state, grad_step, w_inner, w_maps), refs = refs[: 2 * chunks], refs[2 * chunks : 2 * chunks + 4], refs[2 * chunks + 4 :]
    outs, (joined, joined_maps) = refs[:-2], refs[-2:]

    @pl.when(pl.program_id(0) == 0)
    def _():
        for target, parts in ((joined, grads), (joined_maps, (grad_state, grad_step))):
            at = 0
            for part in parts:
                target[:, at : at + part.shape[1]] = part[...]
                at += part.shape[1]

    total = dot(joined[...], w_inner[...], NT) + dot(joined_maps[...], w_maps[...], NT)
    put(*outs, total)


def swap(array, axis, mask):
    count = lax.axis_size(axis)
    return lax.ppermute(array, axis, [(i, i ^ mask) for i in range(count)])


def gather_pieces(own, parts):
    pieces = {0: own}
    bit = parts // 2
    while bit >= 1:
        pieces.update({k | bit: swap(piece, "tensor", bit) for k, piece in list(pieces.items())})
        bit //= 2
    return [pieces[k] for k in range(parts)]


def tie(array, *first):
    return lax.optimization_barrier((array, *first))[0]


def meet(sums, *arrays):
    arrays = lax.optimization_barrier((*arrays, *(part.got for part in sums)))
    for part, got in zip(sums, arrays[len(arrays) - len(sums) :]):
        part.got = got
    return arrays[: len(arrays) - len(sums)]


def sum_all(array, axis):
    bit = 1
    while bit < lax.axis_size(axis):
        array = array + swap(array, axis, bit)
        bit *= 2
    return array


def rest_masks(low_bits):
    bits = (lax.axis_size("dp") - 1).bit_length()
    return [1 << bit for bit in (*range(low_bits + 1, bits), *range(low_bits - 1, -1, -1))]


def turned(index, bits):
    result = index * 0
    for bit in range(bits):
        result = result | (((index >> bit) & 1) << (bits - 1 - bit))
    return result


class Sum:
    def __init__(self, own, got, dim, low_bits):
        self.terms, self.got, self.dim, self.masks = [own], got, dim, rest_masks(low_bits)
        if got is None:
            self.send()

    def advance(self):
        self.terms.append(self.got)
        return self.send()

    def send(self):
        mask = self.masks.pop(0)
        top = (lax.axis_index("dp") & mask) // mask
        size = self.terms[0].shape[self.dim] // 2

        def cut(half):
            return [lax.dynamic_slice_in_dim(term, half * size, size, self.dim) for term in self.terms]

        sent = functools.reduce(jnp.add, [term.astype(F32) for term in cut(1 - top)]).astype(BF16)
        self.terms, self.got, self.sent = cut(top), swap(sent, "dp", mask), sent
        return sent

    def result(self):
        while self.masks:
            self.advance()
        return functools.reduce(jnp.add, [term.astype(F32) for term in (*self.terms, self.got)])


def add_low(left, right):
    return (left.astype(F32) + right.astype(F32)).astype(BF16)


def shards(
    tokens,
    cotangent,
    doc_lengths,
    norm_gain,
    w_inner,
    w_step,
    w_state,
    conv_inner,
    conv_state,
    step_bias,
    log_rate,
    skip_gain,
    gate_gain,
    w_out,
):
    parts = lax.axis_size("tensor")
    groups = lax.axis_size("dp")
    rank = lax.axis_index("tensor").astype(jnp.int32)
    ranks = rank.reshape(1)
    length, quarter = tokens.shape
    width = quarter * parts
    channels = w_inner.shape[2]
    heads = w_step.shape[1]
    states2 = w_state.shape[1]
    states = states2 // 2
    blocks = length // SPAN
    steps = channels // GROUP
    repeat = LANES // heads
    piece_rows = width // groups
    low_bits = 0
    while (piece_rows << low_bits) < LANES:
        low_bits += 1
    run = piece_rows << low_bits
    half_width = width // 2
    high_bits = (groups - 1).bit_length() - 1 - low_bits
    place = ((lax.axis_index("dp") >> low_bits) & 1).astype(jnp.int32).reshape(1)

    token_y = swap(tokens, "tensor", 2)
    grad_y = swap(tie(cotangent, token_y), "tensor", 2)
    flat = w_inner.reshape(width, 2 * channels)
    w_maps = jnp.concatenate([w_state, jnp.tile(w_step, (1, repeat))], axis=1)
    step_pad = jnp.pad(w_step, ((0, 0), (0, LANES - heads)))
    bias8 = jnp.tile(step_bias, repeat)[None, :]
    rate8 = jnp.exp(jnp.tile(log_rate, repeat))[None, :]
    skip_row = jnp.repeat(skip_gain, channels // heads)[None, :]
    gain_row = gate_gain[None, :]
    conv_pad = jnp.pad(conv_inner, ((0, 3), (0, 0)))
    conv_state_pad = jnp.pad(conv_state, ((0, 3), (0, 0)))

    doc_ends = jnp.cumsum(doc_lengths[0])
    positions = jnp.arange(length, dtype=jnp.int32)
    segment = jnp.sum((positions[:, None] >= doc_ends[None, :]).astype(jnp.int32), axis=1)
    present = positions < doc_ends[-1]
    by_block = segment.reshape(blocks, SPAN)
    final = by_block[:, -1:]
    before = jnp.concatenate([jnp.full((1, 1), -1, jnp.int32), final[:-1]], axis=0)
    marks = [
        jnp.concatenate([jnp.full((k,), -1, jnp.int32), segment[:-k]]) == segment for k in (1, 2, 3)
    ]
    marks += [(by_block == before).reshape(-1), (by_block == final).reshape(-1), present]
    marks = [mark.astype(F32) for mark in marks] + [segment.astype(F32)]
    marks = jnp.pad(jnp.stack(marks, axis=1), ((0, 8), (0, LANES - len(marks))))
    seg_row = jnp.broadcast_to(segment.astype(F32)[None, :], (8, length))

    token_y, flat, w_maps, step_pad, marks, seg_row, skip_row, conv_pad = lax.optimization_barrier(
        (token_y, flat, w_maps, step_pad, marks, seg_row, skip_row, conv_pad)
    )
    token_pieces = [tokens, swap(tokens, "tensor", 1), token_y, swap(token_y, "tensor", 1)]

    by_group = lambda rows: pl.BlockSpec((rows, GROUP), lambda g, *_: (0, g))
    (normed, pre_state, maps, maps_t, per_head, rising_rows, cross_t, value, gate, mixer_out, low_gated, memory, squares) = call(
        functools.partial(front_kernel, parts, heads),
        (steps,),
        [held((length, quarter))] * parts
        + [
            held((1, width)), held((width, states2 + LANES)), held((8, states2)),
            held((1, LANES)), held((1, LANES)), held((8, length)),
            pl.BlockSpec((width, GROUP), lambda g, *_: (0, g)), pl.BlockSpec((width, GROUP), lambda g, *_: (0, steps + g)),
            by_group(8), by_group(1), by_group(1), held((length + 8, LANES)),
        ],
        [
            held((length, width)), held((length, states2)), held((length, states2)), held((states2, length)),
            held((length, LANES)), held((steps, blocks * 8, SPAN)), held((length, SPAN)),
            by_group(length), by_group(length), by_group(length), by_group(length),
            pl.BlockSpec((blocks, states, GROUP), lambda g, *_: (0, 0, g)), held((length, LANES)),
        ],
        [
            shape_of(length, width, dtype=BF16), shape_of(length, states2), shape_of(length, states2, dtype=BF16),
            shape_of(states2, length, dtype=BF16), shape_of(length, LANES), shape_of(steps, blocks * 8, SPAN),
            shape_of(length, SPAN), shape_of(length, channels), shape_of(length, channels, dtype=BF16),
            shape_of(length, channels), shape_of(length, channels, dtype=BF16),
            shape_of(blocks, states, channels, dtype=BF16), shape_of(length, LANES),
        ],
        [
            pltpu.VMEM((length, states2 + LANES), F32), pltpu.VMEM((length, SPAN), F32),
            pltpu.VMEM((states, GROUP), F32),
        ],
        prefetch=1,
        flops=8 * length * width * channels,
        moved=length * width * 4 + width * channels * 4 + length * channels * 14,
        name="front",
        vmem=56,
    )(
        ranks, *token_pieces, norm_gain[None, :], w_maps, conv_state_pad, bias8, rate8, seg_row, flat, flat, conv_pad,
        skip_row, gain_row, marks,
    )

    grad_y = tie(grad_y, squares)
    grad_pieces = [cotangent, swap(cotangent, "tensor", 1), grad_y, swap(grad_y, "tensor", 1)]
    pieces_any = [pl.BlockSpec(memory_space=pl.ANY)] * parts
    double = 2 * GROUP
    by_double = lambda rows: pl.BlockSpec((rows, double), lambda g, *_: (0, g))
    grad_mixed, stats = call(
        functools.partial(cotangent_kernel, parts),
        (channels // double,),
        pieces_any
        + [
            pl.BlockSpec((double, width), lambda g, *_: (g, 0)),
            by_double(length), held((length, LANES)),
        ],
        [by_double(length), held((8, length))],
        [shape_of(length, channels, dtype=BF16), shape_of(8, length)],
        [pltpu.VMEM((length, LANES), F32), pltpu.VMEM((length, width), BF16), pltpu.SemaphoreType.DMA((parts,))],
        prefetch=1,
        flops=2 * length * width * channels,
        moved=length * width * 2 + width * channels * 2 + length * channels * 12,
        name="cotangent",
        vmem=56,
    )(ranks, *grad_pieces, w_out, low_gated, squares)
    spans = steps // CHUNKS

    def chunk_spec(rows, c):
        return pl.BlockSpec((rows, GROUP), lambda g, *_: (0, c * spans + g))

    def gate_part(c, stats, stacked):
        size = spans * GROUP
        if stacked:
            outs = [pl.BlockSpec((2, GROUP, half_width), lambda g, *_: (0, g, 0))]
            shapes = [shape_of(2, size, half_width, dtype=BF16)]
        else:
            outs = [pl.BlockSpec((GROUP, half_width), lambda g, *_: (g, 0))] * 2
            shapes = [shape_of(size, half_width, dtype=BF16)] * 2
        return call(
            functools.partial(gate_kernel, parts, run, channels * parts, stacked),
            (spans,),
            pieces_any
            + [
                chunk_spec(length, c), chunk_spec(length, c), chunk_spec(length, c), chunk_spec(1, c),
                held((8, length)), held((length + 8, LANES)),
            ],
            [by_group(length), by_group(length), by_group(length), by_group(1), *outs],
            [
                shape_of(length, size, dtype=BF16), shape_of(length, size, dtype=BF16),
                shape_of(length, size, dtype=BF16), shape_of(1, size), *shapes,
            ],
            [
                pltpu.VMEM((length, half_width), BF16), pltpu.VMEM((length, half_width), BF16),
                pltpu.SemaphoreType.DMA((width // run,)),
            ],
            prefetch=2,
            flops=2 * length * width * size,
            moved=length * width * 2 + length * size * 18 + width * size * 2,
            name="gate",
        )(place, ranks, *grad_pieces, grad_mixed, gate, mixer_out, gain_row, stats, marks)

    def weight_part(*right):
        runs = half_width // run
        columns = [part.shape[1] for part in right]
        out = pl.BlockSpec((run, sum(columns)), lambda j, p: (turned(j, (runs - 1).bit_length()), 0))
        shape = shape_of(half_width, sum(columns), dtype=BF16)
        return call(
            weight_kernel,
            (runs,),
            [
                pl.BlockSpec((length, run), lambda j, p: (0, 2 * j + (p[0] ^ 1))),
                pl.BlockSpec((length, run), lambda j, p: (0, 2 * j + p[0])),
            ]
            + [held((length, size)) for size in columns],
            [out, out],
            [shape, shape],
            prefetch=1,
            flops=2 * length * width * sum(columns),
            moved=length * width * 2 + length * sum(columns) * 2 + width * sum(columns) * 2,
            name="weights",
        )(place, normed, normed, *right)

    all_lanes = held((length, LANES))

    def backward_part(c, grad_out):
        size = spans * GROUP
        return call(
            functools.partial(backward_kernel, heads, c * spans),
            (spans,),
            [
                chunk_spec(length, c), by_group(length), chunk_spec(length, c),
                pl.BlockSpec((blocks, states, GROUP), lambda g, *_: (0, 0, c * spans + g)),
                chunk_spec(8, c), chunk_spec(1, c), all_lanes, held((length + 8, LANES)),
                pl.BlockSpec((1, blocks * 8, SPAN), lambda g, *_: (c * spans + g, 0, 0)),
                held((length, states2)), held((states2, length)), held((length, SPAN)),
            ],
            [by_group(length), by_group(8), by_group(1), held((length, SPAN)), all_lanes, held((length, states2))],
            [
                shape_of(length, size, dtype=BF16), shape_of(8, size), shape_of(1, size),
                shape_of(length, SPAN), shape_of(length, LANES), shape_of(length, states2),
            ],
            [pltpu.VMEM((8, GROUP), F32), pltpu.VMEM((states, GROUP), F32)],
            flops=40e9 / CHUNKS,
            moved=length * size * 14,
            name="backward",
            vmem=56,
        )(
            value, grad_out, mixer_out, memory, conv_pad, skip_row, per_head, marks, rising_rows, maps, maps_t,
            cross_t,
        )

    def piece_of(i, r):
        return r[0] ^ jnp.where(i == 0, 1, jnp.where(i == 1, 3, jnp.where(i == 2, 2, 0)))

    def far_near(count):
        specs = [
            pl.BlockSpec((1, length, quarter), lambda i, r: (jnp.minimum(i, 1), 0, 0)),
            pl.BlockSpec((1, length, quarter), lambda i, r: (jnp.maximum(i, 2) - 2, 0, 0)),
        ]
        return specs, [shape_of(2, length, quarter, dtype=BF16), shape_of(count, length, quarter, dtype=BF16)]

    def output_part(low_gated):
        return call(
            output_kernel,
            (4,),
            [held((length, channels)), pl.BlockSpec((channels, quarter), lambda i, r: (0, piece_of(i, r)))],
            *far_near(2),
            prefetch=1,
            flops=2 * length * channels * width,
            moved=length * channels * 2 + channels * width * 2 + length * width * 2,
            name="output",
        )(ranks, low_gated, w_out)

    def normed_part(grad_gate):
        grads = (*grad_gate, *grad_value)
        return call(
            functools.partial(normed_kernel, len(grad_gate)),
            (4,),
            [held((length, part.shape[1])) for part in grads]
            + [
                held((length, states2)), held((length, LANES)),
                pl.BlockSpec((quarter, 2 * channels), lambda i, r: (piece_of(i, r), 0)),
                pl.BlockSpec((quarter, states2 + LANES), lambda i, r: (piece_of(i, r), 0)),
            ],
            *far_near(2),
            [pltpu.VMEM((length, 2 * channels), BF16), pltpu.VMEM((length, states2 + LANES), BF16)],
            prefetch=1,
            flops=2 * length * (2 * channels + states2 + LANES) * width,
            moved=length * channels * 4 + channels * width * 4 + length * width * 2,
            name="normed_grad",
        )(ranks, *grads, grad_state, grad_step, flat, w_maps)

    def over_x(send):
        return swap(send, "dp", 1 << low_bits)

    stats = sum_all(stats, "tensor")

    first = gate_part(0, stats, False)
    sum_out = [Sum(first[5], over_x(first[4]), 1, low_bits)]
    other = gate_part(1, tie(stats, first[5]), False)
    sum_out.append(Sum(other[5], over_x(other[4]), 1, low_bits))
    low_mixed, grad_mixer, grad_gate, grad_gain = zip(first[:4], other[:4])
    gate_send, gate_own = weight_part(tie(grad_gate[0], other[5]), *grad_gate[1:])
    sum_gate = Sum(gate_own, over_x(gate_send), 0, low_bits)
    out_far, out_near = output_part(tie(low_gated, gate_own))

    out_far, out_near = meet(sum_out[:1], out_far, out_near)
    moved = [sum_out[0].advance(), out_far]
    out_far_got = swap(out_far, "tensor", 1)
    back = backward_part(0, tie(grad_mixer[0], *moved))

    grad_value, out_far_got = meet(sum_out, back[0], out_far_got)
    moved = [sum_out[1].advance(), sum_out[0].advance()]
    out_sum = add_low(out_near[0], out_far_got[1])
    out_y = swap(out_sum, "tensor", 2)
    value_send, value_own = weight_part(tie(grad_value, *moved, out_sum))
    sum_value = [Sum(value_own, over_x(value_send), 0, low_bits)]
    backs = [back, backward_part(1, tie(grad_mixer[1], value_own))]

    grad_value2, out_y = meet(sum_out, backs[1][0], out_y)
    moved = [sum_out[1].advance()]
    value_send2, value_own2 = weight_part(tie(grad_value2, *moved))
    sum_value.append(Sum(value_own2, over_x(value_send2), 0, low_bits))
    moved = [value_own2]
    grad_value, grad_conv, grad_skip, cross_parts, folded_parts, maps_parts = zip(*backs)
    (grad_state, grad_step, grad_conv_state, grad_heads) = call(
        functools.partial(finish_kernel, heads, CHUNKS),
        (1,),
        [held((length, SPAN)), all_lanes, held((length, states2))] * CHUNKS
        + [
            all_lanes, held((length + 8, LANES)), held((length, states2)), held((8, length)),
            held((length, states2)), held((8, states2)), held((1, LANES)),
        ],
        [held((length, states2)), all_lanes, held((8, states2)), held((8, LANES))],
        [
            shape_of(length, states2, dtype=BF16), shape_of(length, LANES, dtype=BF16),
            shape_of(8, states2), shape_of(8, LANES),
        ],
        [pltpu.VMEM((8, states2), F32)],
        flops=4e9,
        moved=length * 2048 * CHUNKS + length * 5000,
        name="finish",
        vmem=56,
    )(
        tie(cross_parts[0], *moved), folded_parts[0], maps_parts[0],
        *[part for three in zip(cross_parts[1:], folded_parts[1:], maps_parts[1:]) for part in three],
        per_head, marks, maps, seg_row, pre_state, conv_state_pad, rate8,
    )

    grad_state, grad_conv_state = meet([sum_gate, sum_out[1]], grad_state, grad_conv_state[:5])
    state_got = swap(grad_state, "tensor", 1)
    grad_conv_state = grad_conv_state + swap(grad_conv_state, "tensor", 1)
    conv_got = swap(grad_conv_state, "tensor", 2)
    moved = [sum_gate.advance(), grad_state, grad_conv_state]
    near_far, near = normed_part([tie(grad_gate[0], *moved), *grad_gate[1:]])

    near_far, near, state_got, conv_got = meet([sum_value[0], sum_gate], near_far, near, state_got, conv_got)
    near_far_got = swap(near_far, "tensor", 1)
    state_sum = add_low(grad_state, state_got)
    state_got = swap(state_sum, "tensor", 2)
    grad_conv_state = grad_conv_state + conv_got
    moved = [sum_value[0].advance(), sum_gate.advance(), state_sum]
    near, near_far_got, *_ = lax.optimization_barrier((near, near_far_got, *moved))
    near_sum = add_low(near[0], near_far_got[1])
    over_y = swap(near_sum, "tensor", 2)
    late = (
        grad_step, norm_gain, grad_conv_state, grad_heads, normed, state_got,
        grad_conv, grad_skip, grad_gain, stats, marks, per_head,
    )
    (
        grad_step, norm_gain, grad_conv_state, grad_heads, normed, state_got,
        grad_conv, grad_skip, grad_gain, stats, marks, per_head,
    ) = lax.optimization_barrier((late, near_sum))[0]
    state_all = add_low(state_sum, state_got)
    own_rows = piece_rows // parts
    grad_w_state = dot(normed, state_all, TN).astype(BF16)
    grad_w_state = lax.dynamic_slice_in_dim(
        grad_w_state.reshape(groups, parts, own_rows, states2), rank, 1, axis=1
    )
    grad_w_step = dot(grad_step[:, :heads], normed, TN).astype(BF16)
    grad_w_state, grad_w_step, grad_conv, grad_skip, grad_gain, stats, marks = meet(
        sum_value, grad_w_state, grad_w_step, grad_conv, grad_skip, grad_gain, stats, marks
    )
    moved = [sum_value[1].advance(), sum_value[0].advance()]
    (grad_w_state, grad_w_step, grad_conv, grad_skip, grad_gain, stats, marks), _ = lax.optimization_barrier(
        ((grad_w_state, grad_w_step, grad_conv, grad_skip, grad_gain, stats, marks), moved)
    )
    meet(sum_out, *moved)
    grad_w_step = grad_w_step.reshape(heads, groups, piece_rows).transpose(1, 0, 2)
    small = jnp.concatenate(
        [grad_w_state.reshape(groups, own_rows * states2), grad_w_step.reshape(groups, heads * piece_rows)], axis=1
    ).reshape(groups // (2 << low_bits), 2, 1 << low_bits, -1)
    small = jnp.stack([small[turned(j, high_bits)] for j in range(small.shape[0])])
    small_own = lax.dynamic_slice_in_dim(small, place[0], 1, 1).reshape(groups // 2, -1)
    small_send = lax.dynamic_slice_in_dim(small, 1 - place[0], 1, 1).reshape(groups // 2, -1)
    small_sum = Sum(small_own, over_x(small_send), 0, low_bits)
    grad_conv, grad_skip, grad_gate_gain = (
        jnp.concatenate(array, axis=1) for array in (grad_conv, grad_skip, grad_gain)
    )
    skip_sums = jnp.sum(grad_skip.reshape(heads, channels // heads), axis=1)
    pieces = [
        grad_conv[:5].reshape(-1), grad_conv_state.reshape(-1), grad_heads[0, :heads], grad_heads[1, :heads],
        skip_sums, grad_gate_gain[0],
    ]
    total_out = [part.result() for part in sum_out]
    rest = jnp.concatenate(pieces)
    scale_out = lax.rsqrt(stats[0] / (channels * parts) + EPSILON)
    factor = scale_out * marks[:length, 5]
    branch = out_near[1].astype(F32) + out_far_got[0].astype(F32) + out_y.astype(F32)
    own_tokens = tokens.astype(F32)
    output = (own_tokens + factor[:, None] * branch).astype(BF16)

    over_y, small_send, rest, output, *total_out = meet(
        [sum_value[1], sum_gate, small_sum], over_y, small_send, rest, output, *total_out
    )
    moved = [sum_value[1].advance(), small_sum.advance()]
    total_gate = sum_gate.result()
    over_y = tie(over_y, *moved)
    grad_normed = near[1].astype(F32) + near_far_got[0].astype(F32) + over_y.astype(F32)
    own_gain = lax.dynamic_slice_in_dim(norm_gain, rank * quarter, quarter, 0)
    scale_in = per_head[:, 5 * heads : 5 * heads + 1]
    row_norm = jnp.sum(own_tokens * own_gain * grad_normed, axis=1)
    grad_norm_gain = jnp.sum(grad_normed * own_tokens * scale_in, axis=0)
    pack = jnp.concatenate([grad_norm_gain, rest])
    pieces = [grad_norm_gain, *pieces]

    row_got, pack_got = swap(row_norm, "tensor", 1), swap(pack, "dp", 1)
    row_norm, row_got, pack, pack_got = meet([small_sum], row_norm, row_got, pack, pack_got)
    small_sum.advance()
    row_norm, pack = row_norm + row_got, pack + pack_got
    row_got, pack_got = swap(row_norm, "tensor", 2), swap(pack, "dp", 2)
    row_norm, row_got, pack, pack_got = meet([*sum_value, small_sum], row_norm, row_got, pack, pack_got)
    total_value = [part.result() for part in sum_value]
    row_norm, pack = row_norm + row_got, pack + pack_got
    bit = 4
    while bit < groups:
        pack = pack + swap(pack, "dp", bit)
        bit *= 2
    grad_tokens = (
        cotangent.astype(F32)
        + scale_in * own_gain * grad_normed
        - own_tokens * scale_in**3 * row_norm[:, None] / width
    ).astype(BF16)
    small_sum = small_sum.result()[0]
    sum_state = small_sum[: own_rows * states2].reshape(own_rows, states2)
    sum_step = small_sum[own_rows * states2 :].reshape(heads, piece_rows).T

    sum_out = jnp.concatenate(total_out, axis=0)
    sum_gate = total_gate
    sum_value = jnp.concatenate(total_value, axis=1)
    sum_inner = jnp.stack([sum_gate, sum_value], axis=1)

    split = []
    at = 0
    for piece in pieces:
        split.append(pack[at : at + piece.shape[0]])
        at += piece.shape[0]
    return (
        output,
        grad_tokens,
        split[0],
        sum_inner,
        sum_step,
        sum_state,
        split[1].reshape(5, channels),
        split[2].reshape(5, states2),
        split[3],
        split[4],
        split[5],
        split[6],
        sum_out,
    )


def solution(mesh):
    placed = (
        P("dp", "tensor"),
        P("dp", "tensor"),
        P("dp", None),
        P(),
        P(None, None, "tensor"),
        P(None, "tensor"),
        P(),
        P(None, "tensor"),
        P(),
        P("tensor"),
        P("tensor"),
        P("tensor"),
        P("tensor"),
        P("tensor", None),
    )
    return jax.shard_map(
        shards,
        mesh=mesh,
        in_specs=placed,
        out_specs=(
            P("dp", "tensor"),
            P("dp", "tensor"),
            P("tensor"),
            P("dp", None, "tensor"),
            P("dp", "tensor"),
            P(("dp", "tensor"), None),
            P(None, "tensor"),
            P(),
            P("tensor"),
            P("tensor"),
            P("tensor"),
            P("tensor"),
            P("tensor", "dp"),
        ),
        check_vma=False,
    )
```

```python
import functools
import math

import jax
import jax.numpy as jnp
from jax import lax
from jax.experimental import pallas as pl
from jax.experimental.pallas import tpu as pltpu
from jax.sharding import PartitionSpec as P

F32 = jnp.float32
BF16 = jnp.bfloat16
HIGHEST = lax.Precision.HIGHEST
EPSILON = 1e-05
LOG2E = math.log2(math.e)
LANES = 128
SPAN = 128
GROUP = 256
UNROLL = 8
HINT = 0.02
ROWS = 512
CHUNKS = 2

NN = (((1,), (0,)), ((), ()))
NT = (((1,), (1,)), ((), ()))
TN = (((0,), (0,)), ((), ()))


def dot(left, right, dims=NN, precision=None):
    return lax.dot_general(left, right, dims, precision=precision, preferred_element_type=F32)


def sigmoid(a):
    return 0.5 * jnp.tanh(0.5 * a) + 0.5


def iota(shape, dim):
    return lax.broadcasted_iota(jnp.int32, shape, dim)


def tri(upper):
    rows, cols = iota((SPAN, SPAN), 0), iota((SPAN, SPAN), 1)
    return ((rows <= cols) if upper else (rows >= cols)).astype(F32)


def call(body, grid, in_specs, out_specs, out_shape, scratch=(), prefetch=0, flops=0, moved=0, name=None, vmem=56):
    return pl.pallas_call(
        body,
        grid_spec=pltpu.PrefetchScalarGridSpec(
            num_scalar_prefetch=prefetch,
            grid=grid,
            in_specs=in_specs,
            out_specs=out_specs,
            scratch_shapes=list(scratch),
        ),
        out_shape=out_shape,
        compiler_params=pltpu.CompilerParams(
            vmem_limit_bytes=vmem * 1024 * 1024, dimension_semantics=("arbitrary",) * len(grid)
        ),
        cost_estimate=pl.CostEstimate(
            flops=int(flops * HINT), bytes_accessed=int(moved * HINT), transcendentals=0
        ),
        name=name,
    )


def held(shape):
    zeros = (0,) * len(shape)
    return pl.BlockSpec(shape, lambda *_: zeros, pipeline_mode=pl.Buffered(1))


def shape_of(*dims, dtype=F32):
    return jax.ShapeDtypeStruct(dims, dtype)


def conv_taps(before, now, marks, filters):
    rows = now.shape[0]
    wide = jnp.concatenate([before, now], axis=0)
    total = filters[4:5] + filters[0:1] * now
    shifted = [now]
    for k in range(1, 4):
        moved = wide[8 - k : 8 - k + rows] * marks[:, k - 1 : k]
        shifted.append(moved)
        total = total + filters[k : k + 1] * moved
    return total, shifted


def rows_before(array, start):
    return array[pl.ds(pl.multiple_of(jnp.maximum(start - 8, 0), 8), 8), :]


def conv_back(later, marks, filters):
    rows = later.shape[0] - 8
    total = filters[0:1] * later[:rows]
    for k in range(1, 4):
        total = total + filters[k : k + 1] * (later[k : k + rows] * marks[k : k + rows, k - 1 : k])
    return total


def fold_lanes(power):
    folded = power[:, :LANES]
    for tile in range(1, power.shape[1] // LANES):
        folded = folded + power[:, tile * LANES : (tile + 1) * LANES]
    return folded


def spread(table, section, heads, count):
    lane = iota((table.shape[0], LANES), 1)
    tiles = []
    for pair in range(count // 2):
        at = section * heads + 2 * pair
        tiles.append(jnp.where(lane < LANES // 2, table[:, at : at + 1], table[:, at + 1 : at + 2]))
    return jnp.concatenate(tiles, axis=1)


def front_kernel(
    parts, heads, rank, *refs,
):
    pieces, refs = refs[:parts], refs[parts:]
    (gain, w_maps, conv_maps, bias, rate, seg_row, w_gate, w_value, conv, skip, gate_gain, marks,
     *outs), (value, gate, mixed, low_gated, memory, squares, proj, cross, state), (
        normed, pre_state, maps, maps_t, per_head, rows_out, cross_t, sems
    ) = refs[:-17], refs[-17:-8], refs[-8:]
    copies = [
        pltpu.make_async_copy(source, target, sems.at[i])
        for i, (source, target) in enumerate(
            zip((normed, pre_state, maps, maps_t, per_head, rows_out, cross_t), outs)
        )
    ]
    g = pl.program_id(0)
    length, quarter = pieces[0].shape
    width = quarter * parts
    blocks = length // SPAN
    states = maps.shape[1] // 2
    count = GROUP // 64
    lane = iota((SPAN, LANES), 1)

    @pl.when(g == 0)
    def _():
        squares[...] = jnp.zeros_like(squares)

        def normalise(b, _):
            at = pl.ds(pl.multiple_of(b * SPAN, SPAN), SPAN)
            wide = [piece[at, :].astype(F32) for piece in pieces]
            total = functools.reduce(jnp.add, [array * array for array in wide])
            scale = lax.rsqrt(jnp.sum(total, axis=1, keepdims=True) / width + EPSILON)
            per_head[at, :] = jnp.broadcast_to(scale, (SPAN, LANES))
            for k in range(parts):
                to = pl.multiple_of((rank[0] ^ k) * quarter, quarter)
                normed[at, pl.ds(to, quarter)] = (wide[k] * scale * gain[:, pl.ds(to, quarter)]).astype(BF16)
            return 0

        lax.fori_loop(0, blocks, normalise, 0, unroll=2)
        copies[0].start()
        proj[...] = dot(normed[...], w_maps[...])

        def tables(b, _):
            start = pl.multiple_of(b * SPAN, SPAN)
            at = pl.ds(start, SPAN)
            mark = marks[at, :]
            now = proj[at, : 2 * states]
            pre_state[at, :] = now
            total, _ = conv_taps(rows_before(proj, start)[:, : 2 * states], now, mark, conv_maps[...])
            both = total * sigmoid(total)
            keys, queries = both[:, :states], both[:, states:]
            low_keys, low_queries = keys.astype(BF16), queries.astype(BF16)
            maps[at, :states] = low_keys
            maps[at, states:] = low_queries
            maps_t[:states, pl.ds(start, SPAN)] = keys.T.astype(BF16)
            maps_t[states:, pl.ds(start, SPAN)] = queries.T.astype(BF16)

            pre = proj[at, 2 * states :] + bias[...]
            size = jnp.maximum(pre, 0.0) + jnp.log1p(jnp.exp(-jnp.abs(pre)))
            rising = dot(tri(False), -rate[...] * size, precision=HIGHEST)
            entering = jnp.exp(rising) * mark[:, 3:4]
            leaving = jnp.exp(rising[SPAN - 1 :] - rising) * mark[:, 4:5]
            rising = rising * LOG2E
            section = lane // heads
            packed = jnp.where(section == 0, rising, entering)
            packed = jnp.where(section == 2, leaving, packed)
            packed = jnp.where(section == 3, size, packed)
            packed = jnp.where(section == 4, pre, packed)
            packed = jnp.where(section == 5, per_head[at, :], packed)
            per_head[at, :] = packed
            turned = rising.T
            for group in range(rows_out.shape[0]):
                rows_out[group, pl.ds(pl.multiple_of(b * 8, 8), 8), :] = turned[group * count : group * count + 8]
            same = mark[:, 6:7] == seg_row[0:1, pl.ds(start, SPAN)]
            rows, cols = iota((SPAN, SPAN), 0), iota((SPAN, SPAN), 1)
            cross[at, :] = jnp.where(same & (rows >= cols), dot(low_queries, low_keys, NT), 0.0)
            cross_t[at, :] = jnp.where(same & (rows <= cols), dot(low_keys, low_queries, NT), 0.0)
            return 0

        lax.fori_loop(0, blocks, tables, 0, unroll=2)
        for copy in copies[1:]:
            copy.start()

    both = dot(normed[...], jnp.concatenate([w_gate[...], w_value[...]], axis=1))
    gate[...] = both[:, :GROUP].astype(BF16)
    value[...] = both[:, GROUP:]
    state[...] = jnp.zeros_like(state)
    turn = lax.rem(LANES - count * g, LANES)

    def block(b, _):
        start = pl.multiple_of(b * SPAN, SPAN)
        at = pl.ds(start, SPAN)
        total, _ = conv_taps(rows_before(value, start), value[at, :], marks[at, :], conv[...])
        inputs = total * sigmoid(total)
        table = pltpu.roll(per_head[at, :], turn, 1)
        entering, leaving, size = (spread(table, s, heads, count) for s in (1, 2, 3))
        scaled = inputs * size
        keys_t = maps_t[0:states, pl.ds(start, SPAN)]
        queries = maps[at, states:]
        low_state = state[...].astype(BF16)
        memory[b] = low_state
        out = entering * dot(queries, low_state) + skip[...] * inputs
        rising_rows = rows_out[g, pl.ds(pl.multiple_of(b * 8, 8), 8), :]
        crossed = cross[at, :]
        parts_out = []
        for pair in range(count // 2):
            weights = []
            for j in (2 * pair, 2 * pair + 1):
                gap = jnp.minimum(table[:, j : j + 1] - rising_rows[j : j + 1, :], 0.0)
                weights.append((jnp.exp2(gap) * crossed).astype(BF16))
            tile = scaled[:, pair * LANES : (pair + 1) * LANES]
            stacked = jnp.concatenate(
                [
                    jnp.where(lane < LANES // 2, tile, 0.0).astype(BF16),
                    jnp.where(lane < LANES // 2, 0.0, tile).astype(BF16),
                ],
                axis=0,
            )
            parts_out.append(dot(jnp.concatenate(weights, axis=1), stacked))
        out = out + jnp.concatenate(parts_out, axis=1)
        fresh = dot(keys_t, (leaving * scaled).astype(BF16))
        state[...] = state[...] * entering[SPAN - 1 :] + fresh
        mixed[at, :] = out
        opened = gate[at, :].astype(F32)
        gated = out * (opened * sigmoid(opened))
        low_gated[at, :] = (gated * gate_gain[...]).astype(BF16)
        squares[at, :] += fold_lanes(gated * gated)
        return 0

    lax.fori_loop(0, blocks, block, 0, unroll=UNROLL)

    @pl.when(g == pl.num_programs(0) - 1)
    def _():
        for copy in copies:
            copy.wait()


def assemble(pieces, target, sems, where):
    copies = [
        pltpu.make_async_copy(pieces[k].at[:, pl.ds(at, size)], target.at[:, pl.ds(to, size)], sems.at[i])
        for i, (k, at, to, size) in enumerate(where)
    ]
    for copy in copies:
        copy.start()
    for copy in copies:
        copy.wait()


def cotangent_kernel(parts, rank, *refs):
    pieces, (w_out, gated, squares, grad, stats, sums, full, sems) = refs[:parts], refs[parts:]
    g = pl.program_id(0)
    length, quarter = pieces[0].shape

    @pl.when(g == 0)
    def _():
        sums[...] = jnp.zeros_like(sums)
        places = [pl.multiple_of((rank[0] ^ k) * quarter, quarter) for k in range(parts)]
        assemble(pieces, full, sems, [(k, 0, places[k], quarter) for k in range(parts)])

    grad[...] = dot(full[...], w_out[...], NT).astype(BF16)

    def chunk(i, _):
        at = pl.ds(pl.multiple_of(i * SPAN, SPAN), SPAN)
        sums[at, :] += fold_lanes(grad[at, :].astype(F32) * gated[at, :].astype(F32))
        return 0

    lax.fori_loop(0, length // SPAN, chunk, 0, unroll=2)

    @pl.when(g == pl.num_programs(0) - 1)
    def _():
        row = iota((8, LANES), 0)
        stats[...] = dot((row == 0).astype(F32), squares[...], NT, HIGHEST) + dot(
            (row == 1).astype(F32), sums[...], NT, HIGHEST
        )


def gate_kernel(parts, run, channels_all, stacked, place, rank, *refs):
    pieces, refs = refs[:parts], refs[parts:]
    (grad, gate, mixed, gain, stats, marks, low_mixed, grad_mixer, grad_gate, grad_gain), refs = refs[:10], refs[10:]
    targets, (sent, kept, sems) = refs[:-3], refs[-3:]
    length, quarter = pieces[0].shape
    grad_gain[...] = jnp.zeros_like(grad_gain)
    pairs = quarter // (2 * run)
    bits = (parts * pairs - 1).bit_length()
    copies = []
    for half, target in ((1, sent), (0, kept)):
        for k in range(parts):
            for j in range(pairs):
                at = pl.multiple_of((2 * j + (place[0] ^ half)) * run, run)
                to = pl.multiple_of(turned((rank[0] ^ k) * pairs + j, bits) * run, run)
                copies.append(
                    pltpu.make_async_copy(
                        pieces[k].at[:, pl.ds(at, run)], target.at[:, pl.ds(to, run)], sems.at[len(copies)]
                    )
                )

    @pl.when(pl.program_id(0) == 0)
    def _():
        for copy in copies:
            copy.start()

    def chunk(i, _):
        start = pl.multiple_of(i * SPAN, SPAN)
        at = pl.ds(start, SPAN)
        columns = jnp.concatenate([stats[:, pl.ds(start, SPAN)]] * (SPAN // 8), axis=0).T
        keep = marks[at, 5:6]
        scale = lax.rsqrt(columns[:, 0:1] / channels_all + EPSILON)
        factor = scale * keep
        pull = scale * scale * factor * columns[:, 1:2] / channels_all
        opened, out, now = gate[at, :].astype(F32), mixed[at, :], grad[at, :].astype(F32)
        chance = sigmoid(opened)
        swish = opened * chance
        gated = out * swish
        scaled = gated * factor
        low_mixed[at, :] = (scaled * gain[...]).astype(BF16)
        grad_gain[...] += jnp.sum(now * scaled, axis=0, keepdims=True)
        grad_gated = now * (factor * gain[...]) - gated * pull
        grad_mixer[at, :] = (grad_gated * swish).astype(BF16)
        grad_gate[at, :] = (grad_gated * out * chance * (1.0 + opened * (1.0 - chance))).astype(BF16)
        return 0

    lax.fori_loop(0, length // SPAN, chunk, 0, unroll=4)

    @pl.when(pl.program_id(0) == 0)
    def _():
        for copy in copies:
            copy.wait()

    for half, source in enumerate((sent, kept)):
        now = dot(low_mixed[...], source[...], TN).astype(BF16)
        if stacked:
            targets[0][half] = now
        else:
            targets[half][...] = now


def weight_kernel(place, left_send, left_own, *refs):
    right, targets = refs[:-2], refs[-2:]
    for left, target in zip((left_send, left_own), targets):
        at = 0
        for part in right:
            size = part.shape[1]
            target[:, at : at + size] = dot(left[...], part[...], TN).astype(BF16)
            at += size


def backward_kernel(
    heads, first, value, grad_out, mixed, memory, conv, skip, per_head, marks, rows_in, maps, maps_t, cross_t,
    grad_value, grad_conv, grad_skip, grad_cross, folded, grad_maps,
    later, grad_memory,
):
    g = pl.program_id(0) + first
    length = grad_out.shape[0]
    blocks = length // SPAN
    states = maps.shape[1] // 2
    count = GROUP // 64
    lane = iota((SPAN, LANES), 1)
    row = iota((SPAN, GROUP), 0)
    turn = lax.rem(LANES - count * g, LANES)
    channel, target = iota((GROUP, LANES), 0), iota((GROUP, LANES), 1)
    pick_rise = (target == count * g + channel // 64).astype(BF16)
    pick_size = (target == heads + count * g + channel // 64).astype(BF16)
    later[...] = jnp.zeros_like(later)
    grad_memory[...] = jnp.zeros_like(grad_memory)
    grad_conv[...] = jnp.zeros_like(grad_conv)
    grad_skip[...] = jnp.zeros_like(grad_skip)

    @pl.when(g == first)
    def _():
        grad_cross[...] = jnp.zeros_like(grad_cross)
        folded[...] = jnp.zeros_like(folded)
        grad_maps[...] = jnp.zeros_like(grad_maps)

    def block(i, _):
        b = blocks - 1 - i
        start = pl.multiple_of(b * SPAN, SPAN)
        at = pl.ds(start, SPAN)
        filters = conv[...]
        total, shifted = conv_taps(rows_before(value, start), value[at, :], marks[at, :], filters)
        chance = sigmoid(total)
        inputs = total * chance
        table = pltpu.roll(per_head[at, :], turn, 1)
        entering, leaving, size = (spread(table, s, heads, count) for s in (1, 2, 3))
        scaled = inputs * size
        low_scaled = scaled.astype(BF16)
        pulled = grad_out[at, :].astype(F32)
        keys, queries_t = maps[at, 0:states], maps_t[states:, pl.ds(start, SPAN)]
        memory_now = memory[b]
        grad_next = grad_memory[...]
        low_next = grad_next.astype(BF16)
        entered = (entering * pulled).astype(BF16)
        left = (leaving * scaled).astype(BF16)
        grad_maps[at, 0:states] += dot(left, low_next, NT)
        grad_maps[at, states:] += dot(entered, memory_now, NT)
        rising_rows = rows_in[0, pl.ds(pl.multiple_of(b * 8, 8), 8), :]
        crossed_t = cross_t[at, :]
        cross_sum = jnp.zeros((SPAN, SPAN), F32)
        parts = []
        for pair in range(count // 2):
            tile = pulled[:, pair * LANES : (pair + 1) * LANES]
            one = jnp.where(lane < LANES // 2, tile, 0.0).astype(BF16)
            two = jnp.where(lane < LANES // 2, 0.0, tile).astype(BF16)
            low_tile = low_scaled[:, pair * LANES : (pair + 1) * LANES]
            weights = []
            for j, masked in ((2 * pair, one), (2 * pair + 1, two)):
                gap = table[:, j : j + 1] - rising_rows[j : j + 1, :]
                cross_sum = cross_sum + jnp.exp2(jnp.minimum(gap, 0.0)) * dot(masked, low_tile, NT)
                weights.append((jnp.exp2(jnp.minimum(-gap, 0.0)) * crossed_t).astype(BF16))
            parts.append(dot(jnp.concatenate(weights, axis=1), jnp.concatenate([one, two], axis=0)))
        grad_cross[at, :] += cross_sum
        grad_within = jnp.concatenate(parts, axis=1)
        grad_left = dot(keys, low_next)
        grad_scaled = grad_within + leaving * grad_left
        scanned = mixed[at, :] - skip[...] * inputs
        kept = left.astype(F32) * grad_left
        rise = pulled * scanned - low_scaled.astype(F32) * grad_within - kept
        carried = entering[SPAN - 1 :] * jnp.sum(low_next.astype(F32) * memory_now.astype(F32), axis=0, keepdims=True)
        rise = rise + jnp.where(row == SPAN - 1, carried + jnp.sum(kept, axis=0, keepdims=True), 0.0)
        grown = grad_scaled * inputs
        summed = folded[at, :]
        for product, pick in ((rise, pick_rise), (grown, pick_size)):
            high = product.astype(BF16)
            rest = (product - high.astype(F32)).astype(BF16)
            summed = summed + dot(high, pick) + dot(rest, pick)
        folded[at, :] = summed
        grad_skip[...] += jnp.sum(pulled * inputs, axis=0, keepdims=True)
        grad_inputs = size * grad_scaled + skip[...] * pulled
        grad_total = grad_inputs * (chance * (1.0 + total * (1.0 - chance)))
        for k in range(4):
            grad_conv[k : k + 1] += jnp.sum(grad_total * shifted[k], axis=0, keepdims=True)
        grad_conv[4:5] += jnp.sum(grad_total, axis=0, keepdims=True)
        longer = jnp.concatenate([grad_total, later[...]], axis=0)
        later[...] = grad_total[:8]
        grad_value[at, :] = conv_back(longer, marks[pl.ds(start, SPAN + 8), :], filters).astype(BF16)
        grad_memory[...] = entering[SPAN - 1 :] * grad_next + dot(queries_t, entered)
        return 0

    lax.fori_loop(0, blocks, block, 0, unroll=UNROLL)


def finish_kernel(
    heads, calls, *refs,
):
    summed_parts, refs = refs[: 3 * calls], refs[3 * calls :]
    (per_head, marks, maps, seg_row, pre_state, conv_state, rate,
     grad_state, grad_step, grad_conv_state, grad_heads, later) = refs
    length = maps.shape[0]
    blocks = length // SPAN
    states = maps.shape[1] // 2
    later[...] = jnp.zeros_like(later)
    grad_conv_state[...] = jnp.zeros_like(grad_conv_state)
    grad_heads[...] = jnp.zeros_like(grad_heads)

    def block(i, _):
        start = pl.multiple_of((blocks - 1 - i) * SPAN, SPAN)
        at = pl.ds(start, SPAN)
        mark = marks[at, :]
        rows, cols = iota((SPAN, SPAN), 0), iota((SPAN, SPAN), 1)
        linked = (rows >= cols) & (mark[:, 6:7] == seg_row[0:1, pl.ds(start, SPAN)])
        grad_cross, summed, grad_maps = (
            functools.reduce(jnp.add, [ref[at, :] for ref in summed_parts[j::3]]) for j in range(3)
        )
        crossed = jnp.where(linked, grad_cross, 0.0)
        keys, queries = maps[at, 0:states], maps[at, states:]
        grad_keys = grad_maps[:, :states] + dot(crossed.T.astype(BF16), queries)
        grad_queries = grad_maps[:, states:] + dot(crossed.astype(BF16), keys)
        filters = conv_state[...]
        total, shifted = conv_taps(rows_before(pre_state, start), pre_state[at, :], mark, filters)
        chance = sigmoid(total)
        grad_total = jnp.concatenate([grad_keys, grad_queries], axis=1) * (chance * (1.0 + total * (1.0 - chance)))
        for k in range(4):
            grad_conv_state[k : k + 1] += jnp.sum(grad_total * shifted[k], axis=0, keepdims=True)
        grad_conv_state[4:5] += jnp.sum(grad_total, axis=0, keepdims=True)
        longer = jnp.concatenate([grad_total, later[...]], axis=0)
        later[...] = grad_total[:8]
        grad_state[at, :] = conv_back(longer, marks[pl.ds(start, SPAN + 8), :], filters).astype(BF16)

        table = per_head[at, :]
        grad_decay = dot(tri(True), summed, precision=HIGHEST)
        size = pltpu.roll(table, LANES - 3 * heads, 1)
        pre = pltpu.roll(table, LANES - 4 * heads, 1)
        grad_size = pltpu.roll(summed, LANES - heads, 1) - rate[...] * grad_decay
        valid = iota((SPAN, LANES), 1) < heads
        grad_pre = jnp.where(valid, grad_size * sigmoid(pre), 0.0)
        grad_step[at, :] = grad_pre.astype(BF16)
        grad_heads[0:1] += jnp.sum(grad_pre, axis=0, keepdims=True)
        grad_heads[1:2] += jnp.sum(-rate[...] * size * grad_decay, axis=0, keepdims=True)
        return 0

    lax.fori_loop(0, blocks, block, 0, unroll=UNROLL)


def put(far, near, total):
    step = pl.program_id(0)

    @pl.when(step < 2)
    def _():
        far[0] = total.astype(BF16)

    @pl.when(step >= 2)
    def _():
        near[0] = total.astype(BF16)


def output_kernel(rank, gated, w_out, far, near):
    put(far, near, dot(gated[...], w_out[...]))


def normed_kernel(chunks, rank, *refs):
    grads, (grad_state, grad_step, w_inner, w_maps), refs = refs[: 2 * chunks], refs[2 * chunks : 2 * chunks + 4], refs[2 * chunks + 4 :]
    outs, (joined, joined_maps) = refs[:-2], refs[-2:]

    @pl.when(pl.program_id(0) == 0)
    def _():
        for target, parts in ((joined, grads), (joined_maps, (grad_state, grad_step))):
            at = 0
            for part in parts:
                target[:, at : at + part.shape[1]] = part[...]
                at += part.shape[1]

    total = dot(joined[...], w_inner[...], NT) + dot(joined_maps[...], w_maps[...], NT)
    put(*outs, total)


def swap(array, axis, mask):
    count = lax.axis_size(axis)
    return lax.ppermute(array, axis, [(i, i ^ mask) for i in range(count)])


def gather_pieces(own, parts):
    pieces = {0: own}
    bit = parts // 2
    while bit >= 1:
        pieces.update({k | bit: swap(piece, "tensor", bit) for k, piece in list(pieces.items())})
        bit //= 2
    return [pieces[k] for k in range(parts)]


def tie(array, *first):
    return lax.optimization_barrier((array, *first))[0]


def meet(sums, *arrays):
    arrays = lax.optimization_barrier((*arrays, *(part.got for part in sums)))
    for part, got in zip(sums, arrays[len(arrays) - len(sums) :]):
        part.got = got
    return arrays[: len(arrays) - len(sums)]


def sum_all(array, axis):
    bit = 1
    while bit < lax.axis_size(axis):
        array = array + swap(array, axis, bit)
        bit *= 2
    return array


def rest_masks(low_bits):
    bits = (lax.axis_size("dp") - 1).bit_length()
    return [1 << bit for bit in (*range(low_bits + 1, bits), *range(low_bits - 1, -1, -1))]


def turned(index, bits):
    result = index * 0
    for bit in range(bits):
        result = result | (((index >> bit) & 1) << (bits - 1 - bit))
    return result


class Sum:
    def __init__(self, own, got, dim, low_bits):
        self.terms, self.got, self.dim, self.masks = [own], got, dim, rest_masks(low_bits)
        if got is None:
            self.send()

    def advance(self):
        self.terms.append(self.got)
        return self.send()

    def send(self):
        mask = self.masks.pop(0)
        top = (lax.axis_index("dp") & mask) // mask
        size = self.terms[0].shape[self.dim] // 2

        def cut(half):
            return [lax.dynamic_slice_in_dim(term, half * size, size, self.dim) for term in self.terms]

        sent = functools.reduce(jnp.add, [term.astype(F32) for term in cut(1 - top)]).astype(BF16)
        self.terms, self.got, self.sent = cut(top), swap(sent, "dp", mask), sent
        return sent

    def result(self):
        while self.masks:
            self.advance()
        return functools.reduce(jnp.add, [term.astype(F32) for term in (*self.terms, self.got)])


def add_low(left, right):
    return (left.astype(F32) + right.astype(F32)).astype(BF16)


def shards(
    tokens,
    cotangent,
    doc_lengths,
    norm_gain,
    w_inner,
    w_step,
    w_state,
    conv_inner,
    conv_state,
    step_bias,
    log_rate,
    skip_gain,
    gate_gain,
    w_out,
):
    parts = lax.axis_size("tensor")
    groups = lax.axis_size("dp")
    rank = lax.axis_index("tensor").astype(jnp.int32)
    ranks = rank.reshape(1)
    length, quarter = tokens.shape
    width = quarter * parts
    channels = w_inner.shape[2]
    heads = w_step.shape[1]
    states2 = w_state.shape[1]
    states = states2 // 2
    blocks = length // SPAN
    steps = channels // GROUP
    repeat = LANES // heads
    piece_rows = width // groups
    low_bits = 0
    while (piece_rows << low_bits) < LANES:
        low_bits += 1
    run = piece_rows << low_bits
    half_width = width // 2
    high_bits = (groups - 1).bit_length() - 1 - low_bits
    place = ((lax.axis_index("dp") >> low_bits) & 1).astype(jnp.int32).reshape(1)

    token_y = swap(tokens, "tensor", 2)
    grad_y = swap(tie(cotangent, token_y), "tensor", 2)
    flat = w_inner.reshape(width, 2 * channels)
    w_maps = jnp.concatenate([w_state, jnp.tile(w_step, (1, repeat))], axis=1)
    step_pad = jnp.pad(w_step, ((0, 0), (0, LANES - heads)))
    bias8 = jnp.tile(step_bias, repeat)[None, :]
    rate8 = jnp.exp(jnp.tile(log_rate, repeat))[None, :]
    skip_row = jnp.repeat(skip_gain, channels // heads)[None, :]
    gain_row = gate_gain[None, :]
    conv_pad = jnp.pad(conv_inner, ((0, 3), (0, 0)))
    conv_state_pad = jnp.pad(conv_state, ((0, 3), (0, 0)))

    doc_ends = jnp.cumsum(doc_lengths[0])
    positions = jnp.arange(length, dtype=jnp.int32)
    segment = jnp.sum((positions[:, None] >= doc_ends[None, :]).astype(jnp.int32), axis=1)
    present = positions < doc_ends[-1]
    by_block = segment.reshape(blocks, SPAN)
    final = by_block[:, -1:]
    before = jnp.concatenate([jnp.full((1, 1), -1, jnp.int32), final[:-1]], axis=0)
    marks = [
        jnp.concatenate([jnp.full((k,), -1, jnp.int32), segment[:-k]]) == segment for k in (1, 2, 3)
    ]
    marks += [(by_block == before).reshape(-1), (by_block == final).reshape(-1), present]
    marks = [mark.astype(F32) for mark in marks] + [segment.astype(F32)]
    marks = jnp.pad(jnp.stack(marks, axis=1), ((0, 8), (0, LANES - len(marks))))
    seg_row = jnp.broadcast_to(segment.astype(F32)[None, :], (8, length))

    token_y, flat, w_maps, step_pad, marks, seg_row, skip_row, conv_pad = lax.optimization_barrier(
        (token_y, flat, w_maps, step_pad, marks, seg_row, skip_row, conv_pad)
    )
    token_pieces = [tokens, swap(tokens, "tensor", 1), token_y, swap(token_y, "tensor", 1)]

    by_group = lambda rows: pl.BlockSpec((rows, GROUP), lambda g, *_: (0, g))
    (normed, pre_state, maps, maps_t, per_head, rising_rows, cross_t, value, gate, mixer_out, low_gated, memory, squares) = call(
        functools.partial(front_kernel, parts, heads),
        (steps,),
        [held((length, quarter))] * parts
        + [
            held((1, width)), held((width, states2 + LANES)), held((8, states2)),
            held((1, LANES)), held((1, LANES)), held((8, length)),
            pl.BlockSpec((width, GROUP), lambda g, *_: (0, g)), pl.BlockSpec((width, GROUP), lambda g, *_: (0, steps + g)),
            by_group(8), by_group(1), by_group(1), held((length + 8, LANES)),
        ],
        [
            *[pl.BlockSpec(memory_space=pl.ANY)] * 7,
            by_group(length), by_group(length), by_group(length), by_group(length),
            pl.BlockSpec((blocks, states, GROUP), lambda g, *_: (0, 0, g)), held((length, LANES)),
        ],
        [
            shape_of(length, width, dtype=BF16), shape_of(length, states2), shape_of(length, states2, dtype=BF16),
            shape_of(states2, length, dtype=BF16), shape_of(length, LANES), shape_of(steps, blocks * 8, SPAN),
            shape_of(length, SPAN), shape_of(length, channels), shape_of(length, channels, dtype=BF16),
            shape_of(length, channels), shape_of(length, channels, dtype=BF16),
            shape_of(blocks, states, channels, dtype=BF16), shape_of(length, LANES),
        ],
        [
            pltpu.VMEM((length, states2 + LANES), F32), pltpu.VMEM((length, SPAN), F32),
            pltpu.VMEM((states, GROUP), F32),
            pltpu.VMEM((length, width), BF16), pltpu.VMEM((length, states2), F32), pltpu.VMEM((length, states2), BF16),
            pltpu.VMEM((states2, length), BF16), pltpu.VMEM((length, LANES), F32),
            pltpu.VMEM((steps, blocks * 8, SPAN), F32), pltpu.VMEM((length, SPAN), F32), pltpu.SemaphoreType.DMA((7,)),
        ],
        prefetch=1,
        flops=8 * length * width * channels,
        moved=length * width * 4 + width * channels * 4 + length * channels * 14,
        name="front",
        vmem=56,
    )(
        ranks, *token_pieces, norm_gain[None, :], w_maps, conv_state_pad, bias8, rate8, seg_row, flat, flat, conv_pad,
        skip_row, gain_row, marks,
    )

    grad_y = tie(grad_y, squares)
    grad_pieces = [cotangent, swap(cotangent, "tensor", 1), grad_y, swap(grad_y, "tensor", 1)]
    pieces_any = [pl.BlockSpec(memory_space=pl.ANY)] * parts
    double = 2 * GROUP
    by_double = lambda rows: pl.BlockSpec((rows, double), lambda g, *_: (0, g))
    grad_mixed, stats = call(
        functools.partial(cotangent_kernel, parts),
        (channels // double,),
        pieces_any
        + [
            pl.BlockSpec((double, width), lambda g, *_: (g, 0)),
            by_double(length), held((length, LANES)),
        ],
        [by_double(length), held((8, length))],
        [shape_of(length, channels, dtype=BF16), shape_of(8, length)],
        [pltpu.VMEM((length, LANES), F32), pltpu.VMEM((length, width), BF16), pltpu.SemaphoreType.DMA((parts,))],
        prefetch=1,
        flops=2 * length * width * channels,
        moved=length * width * 2 + width * channels * 2 + length * channels * 12,
        name="cotangent",
        vmem=56,
    )(ranks, *grad_pieces, w_out, low_gated, squares)
    spans = steps // CHUNKS

    def chunk_spec(rows, c):
        return pl.BlockSpec((rows, GROUP), lambda g, *_: (0, c * spans + g))

    def gate_part(c, stats, stacked):
        size = spans * GROUP
        if stacked:
            outs = [pl.BlockSpec((2, GROUP, half_width), lambda g, *_: (0, g, 0))]
            shapes = [shape_of(2, size, half_width, dtype=BF16)]
        else:
            outs = [pl.BlockSpec((GROUP, half_width), lambda g, *_: (g, 0))] * 2
            shapes = [shape_of(size, half_width, dtype=BF16)] * 2
        return call(
            functools.partial(gate_kernel, parts, run, channels * parts, stacked),
            (spans,),
            pieces_any
            + [
                chunk_spec(length, c), chunk_spec(length, c), chunk_spec(length, c), chunk_spec(1, c),
                held((8, length)), held((length + 8, LANES)),
            ],
            [by_group(length), by_group(length), by_group(length), by_group(1), *outs],
            [
                shape_of(length, size, dtype=BF16), shape_of(length, size, dtype=BF16),
                shape_of(length, size, dtype=BF16), shape_of(1, size), *shapes,
            ],
            [
                pltpu.VMEM((length, half_width), BF16), pltpu.VMEM((length, half_width), BF16),
                pltpu.SemaphoreType.DMA((width // run,)),
            ],
            prefetch=2,
            flops=2 * length * width * size,
            moved=length * width * 2 + length * size * 18 + width * size * 2,
            name="gate",
        )(place, ranks, *grad_pieces, grad_mixed, gate, mixer_out, gain_row, stats, marks)

    def weight_part(*right):
        runs = half_width // run
        columns = [part.shape[1] for part in right]
        out = pl.BlockSpec((run, sum(columns)), lambda j, p: (turned(j, (runs - 1).bit_length()), 0))
        shape = shape_of(half_width, sum(columns), dtype=BF16)
        return call(
            weight_kernel,
            (runs,),
            [
                pl.BlockSpec((length, run), lambda j, p: (0, 2 * j + (p[0] ^ 1))),
                pl.BlockSpec((length, run), lambda j, p: (0, 2 * j + p[0])),
            ]
            + [held((length, size)) for size in columns],
            [out, out],
            [shape, shape],
            prefetch=1,
            flops=2 * length * width * sum(columns),
            moved=length * width * 2 + length * sum(columns) * 2 + width * sum(columns) * 2,
            name="weights",
        )(place, normed, normed, *right)

    all_lanes = held((length, LANES))

    def backward_part(c, grad_out):
        size = spans * GROUP
        return call(
            functools.partial(backward_kernel, heads, c * spans),
            (spans,),
            [
                chunk_spec(length, c), by_group(length), chunk_spec(length, c),
                pl.BlockSpec((blocks, states, GROUP), lambda g, *_: (0, 0, c * spans + g)),
                chunk_spec(8, c), chunk_spec(1, c), all_lanes, held((length + 8, LANES)),
                pl.BlockSpec((1, blocks * 8, SPAN), lambda g, *_: (c * spans + g, 0, 0)),
                held((length, states2)), held((states2, length)), held((length, SPAN)),
            ],
            [by_group(length), by_group(8), by_group(1), held((length, SPAN)), all_lanes, held((length, states2))],
            [
                shape_of(length, size, dtype=BF16), shape_of(8, size), shape_of(1, size),
                shape_of(length, SPAN), shape_of(length, LANES), shape_of(length, states2),
            ],
            [pltpu.VMEM((8, GROUP), F32), pltpu.VMEM((states, GROUP), F32)],
            flops=40e9 / CHUNKS,
            moved=length * size * 14,
            name="backward",
            vmem=56,
        )(
            value, grad_out, mixer_out, memory, conv_pad, skip_row, per_head, marks, rising_rows, maps, maps_t,
            cross_t,
        )

    def piece_of(i, r):
        return r[0] ^ jnp.where(i == 0, 1, jnp.where(i == 1, 3, jnp.where(i == 2, 2, 0)))

    def far_near(count):
        specs = [
            pl.BlockSpec((1, length, quarter), lambda i, r: (jnp.minimum(i, 1), 0, 0)),
            pl.BlockSpec((1, length, quarter), lambda i, r: (jnp.maximum(i, 2) - 2, 0, 0)),
        ]
        return specs, [shape_of(2, length, quarter, dtype=BF16), shape_of(count, length, quarter, dtype=BF16)]

    def output_part(low_gated):
        return call(
            output_kernel,
            (4,),
            [held((length, channels)), pl.BlockSpec((channels, quarter), lambda i, r: (0, piece_of(i, r)))],
            *far_near(2),
            prefetch=1,
            flops=2 * length * channels * width,
            moved=length * channels * 2 + channels * width * 2 + length * width * 2,
            name="output",
        )(ranks, low_gated, w_out)

    def normed_part(grad_gate):
        grads = (*grad_gate, *grad_value)
        return call(
            functools.partial(normed_kernel, len(grad_gate)),
            (4,),
            [held((length, part.shape[1])) for part in grads]
            + [
                held((length, states2)), held((length, LANES)),
                pl.BlockSpec((quarter, 2 * channels), lambda i, r: (piece_of(i, r), 0)),
                pl.BlockSpec((quarter, states2 + LANES), lambda i, r: (piece_of(i, r), 0)),
            ],
            *far_near(2),
            [pltpu.VMEM((length, 2 * channels), BF16), pltpu.VMEM((length, states2 + LANES), BF16)],
            prefetch=1,
            flops=2 * length * (2 * channels + states2 + LANES) * width,
            moved=length * channels * 4 + channels * width * 4 + length * width * 2,
            name="normed_grad",
        )(ranks, *grads, grad_state, grad_step, flat, w_maps)

    def over_x(send):
        return swap(send, "dp", 1 << low_bits)

    stats = sum_all(stats, "tensor")

    first = gate_part(0, stats, False)
    sum_out = [Sum(first[5], over_x(first[4]), 1, low_bits)]
    other = gate_part(1, tie(stats, first[5]), False)
    sum_out.append(Sum(other[5], over_x(other[4]), 1, low_bits))
    low_mixed, grad_mixer, grad_gate, grad_gain = zip(first[:4], other[:4])
    gate_send, gate_own = weight_part(tie(grad_gate[0], other[5]), *grad_gate[1:])
    sum_gate = Sum(gate_own, over_x(gate_send), 0, low_bits)
    out_far, out_near = output_part(tie(low_gated, gate_own))

    out_far, out_near = meet(sum_out[:1], out_far, out_near)
    moved = [sum_out[0].advance(), out_far]
    out_far_got = swap(out_far, "tensor", 1)
    back = backward_part(0, tie(grad_mixer[0], *moved))

    grad_value, out_far_got = meet(sum_out, back[0], out_far_got)
    moved = [sum_out[1].advance(), sum_out[0].advance()]
    out_sum = add_low(out_near[0], out_far_got[1])
    out_y = swap(out_sum, "tensor", 2)
    value_send, value_own = weight_part(tie(grad_value, *moved, out_sum))
    sum_value = [Sum(value_own, over_x(value_send), 0, low_bits)]
    backs = [back, backward_part(1, tie(grad_mixer[1], value_own))]

    grad_value2, out_y = meet(sum_out, backs[1][0], out_y)
    moved = [sum_out[1].advance()]
    value_send2, value_own2 = weight_part(tie(grad_value2, *moved))
    sum_value.append(Sum(value_own2, over_x(value_send2), 0, low_bits))
    moved = [value_own2]
    grad_value, grad_conv, grad_skip, cross_parts, folded_parts, maps_parts = zip(*backs)
    (grad_state, grad_step, grad_conv_state, grad_heads) = call(
        functools.partial(finish_kernel, heads, CHUNKS),
        (1,),
        [held((length, SPAN)), all_lanes, held((length, states2))] * CHUNKS
        + [
            all_lanes, held((length + 8, LANES)), held((length, states2)), held((8, length)),
            held((length, states2)), held((8, states2)), held((1, LANES)),
        ],
        [held((length, states2)), all_lanes, held((8, states2)), held((8, LANES))],
        [
            shape_of(length, states2, dtype=BF16), shape_of(length, LANES, dtype=BF16),
            shape_of(8, states2), shape_of(8, LANES),
        ],
        [pltpu.VMEM((8, states2), F32)],
        flops=4e9,
        moved=length * 2048 * CHUNKS + length * 5000,
        name="finish",
        vmem=56,
    )(
        tie(cross_parts[0], *moved), folded_parts[0], maps_parts[0],
        *[part for three in zip(cross_parts[1:], folded_parts[1:], maps_parts[1:]) for part in three],
        per_head, marks, maps, seg_row, pre_state, conv_state_pad, rate8,
    )

    grad_state, grad_conv_state = meet([sum_gate, sum_out[1]], grad_state, grad_conv_state[:5])
    state_got = swap(grad_state, "tensor", 1)
    grad_conv_state = grad_conv_state + swap(grad_conv_state, "tensor", 1)
    conv_got = swap(grad_conv_state, "tensor", 2)
    moved = [sum_gate.advance(), grad_state, grad_conv_state]
    near_far, near = normed_part([tie(grad_gate[0], *moved), *grad_gate[1:]])

    near_far, near, state_got, conv_got = meet([sum_value[0], sum_gate], near_far, near, state_got, conv_got)
    near_far_got = swap(near_far, "tensor", 1)
    state_sum = add_low(grad_state, state_got)
    state_got = swap(state_sum, "tensor", 2)
    grad_conv_state = grad_conv_state + conv_got
    moved = [sum_value[0].advance(), sum_gate.advance(), state_sum]
    near, near_far_got, *_ = lax.optimization_barrier((near, near_far_got, *moved))
    near_sum = add_low(near[0], near_far_got[1])
    over_y = swap(near_sum, "tensor", 2)
    late = (
        grad_step, norm_gain, grad_conv_state, grad_heads, normed, state_got,
        grad_conv, grad_skip, grad_gain, stats, marks, per_head,
    )
    (
        grad_step, norm_gain, grad_conv_state, grad_heads, normed, state_got,
        grad_conv, grad_skip, grad_gain, stats, marks, per_head,
    ) = lax.optimization_barrier((late, near_sum))[0]
    state_all = add_low(state_sum, state_got)
    own_rows = piece_rows // parts
    grad_w_state = dot(normed, state_all, TN).astype(BF16)
    grad_w_state = lax.dynamic_slice_in_dim(
        grad_w_state.reshape(groups, parts, own_rows, states2), rank, 1, axis=1
    )
    grad_w_step = dot(grad_step[:, :heads], normed, TN).astype(BF16)
    grad_w_state, grad_w_step, grad_conv, grad_skip, grad_gain, stats, marks = meet(
        sum_value, grad_w_state, grad_w_step, grad_conv, grad_skip, grad_gain, stats, marks
    )
    moved = [sum_value[1].advance(), sum_value[0].advance()]
    (grad_w_state, grad_w_step, grad_conv, grad_skip, grad_gain, stats, marks), _ = lax.optimization_barrier(
        ((grad_w_state, grad_w_step, grad_conv, grad_skip, grad_gain, stats, marks), moved)
    )
    meet(sum_out, *moved)
    grad_w_step = grad_w_step.reshape(heads, groups, piece_rows).transpose(1, 0, 2)
    small = jnp.concatenate(
        [grad_w_state.reshape(groups, own_rows * states2), grad_w_step.reshape(groups, heads * piece_rows)], axis=1
    ).reshape(groups // (2 << low_bits), 2, 1 << low_bits, -1)
    small = jnp.stack([small[turned(j, high_bits)] for j in range(small.shape[0])])
    small_own = lax.dynamic_slice_in_dim(small, place[0], 1, 1).reshape(groups // 2, -1)
    small_send = lax.dynamic_slice_in_dim(small, 1 - place[0], 1, 1).reshape(groups // 2, -1)
    small_sum = Sum(small_own, over_x(small_send), 0, low_bits)
    grad_conv, grad_skip, grad_gate_gain = (
        jnp.concatenate(array, axis=1) for array in (grad_conv, grad_skip, grad_gain)
    )
    skip_sums = jnp.sum(grad_skip.reshape(heads, channels // heads), axis=1)
    pieces = [
        grad_conv[:5].reshape(-1), grad_conv_state.reshape(-1), grad_heads[0, :heads], grad_heads[1, :heads],
        skip_sums, grad_gate_gain[0],
    ]
    total_out = [part.result() for part in sum_out]
    rest = jnp.concatenate(pieces)
    scale_out = lax.rsqrt(stats[0] / (channels * parts) + EPSILON)
    factor = scale_out * marks[:length, 5]
    branch = out_near[1].astype(F32) + out_far_got[0].astype(F32) + out_y.astype(F32)
    own_tokens = tokens.astype(F32)
    output = (own_tokens + factor[:, None] * branch).astype(BF16)

    over_y, small_send, rest, output, *total_out = meet(
        [sum_value[1], sum_gate, small_sum], over_y, small_send, rest, output, *total_out
    )
    moved = [sum_value[1].advance(), small_sum.advance()]
    total_gate = sum_gate.result()
    over_y = tie(over_y, *moved)
    grad_normed = near[1].astype(F32) + near_far_got[0].astype(F32) + over_y.astype(F32)
    own_gain = lax.dynamic_slice_in_dim(norm_gain, rank * quarter, quarter, 0)
    scale_in = per_head[:, 5 * heads : 5 * heads + 1]
    row_norm = jnp.sum(own_tokens * own_gain * grad_normed, axis=1)
    grad_norm_gain = jnp.sum(grad_normed * own_tokens * scale_in, axis=0)
    pack = jnp.concatenate([grad_norm_gain, rest])
    pieces = [grad_norm_gain, *pieces]

    row_got, pack_got = swap(row_norm, "tensor", 1), swap(pack, "dp", 1)
    row_norm, row_got, pack, pack_got = meet([small_sum], row_norm, row_got, pack, pack_got)
    small_sum.advance()
    row_norm, pack = row_norm + row_got, pack + pack_got
    row_got, pack_got = swap(row_norm, "tensor", 2), swap(pack, "dp", 2)
    row_norm, row_got, pack, pack_got = lax.optimization_barrier((row_norm, row_got, pack, pack_got))
    row_norm, pack = row_norm + row_got, pack + pack_got
    bit = 4
    while bit < groups:
        pack = pack + swap(pack, "dp", bit)
        bit *= 2
    grad_tokens = (
        cotangent.astype(F32)
        + scale_in * own_gain * grad_normed
        - own_tokens * scale_in**3 * row_norm[:, None] / width
    ).astype(BF16)
    (grad_tokens,) = meet([*sum_value, small_sum], grad_tokens)
    total_value = [part.result() for part in sum_value]
    small_sum = small_sum.result()[0]
    sum_state = small_sum[: own_rows * states2].reshape(own_rows, states2)
    sum_step = small_sum[own_rows * states2 :].reshape(heads, piece_rows).T

    sum_out = jnp.concatenate(total_out, axis=0)
    sum_gate = total_gate
    sum_value = jnp.concatenate(total_value, axis=1)
    sum_inner = jnp.stack([sum_gate, sum_value], axis=1)

    split = []
    at = 0
    for piece in pieces:
        split.append(pack[at : at + piece.shape[0]])
        at += piece.shape[0]
    return (
        output,
        grad_tokens,
        split[0],
        sum_inner,
        sum_step,
        sum_state,
        split[1].reshape(5, channels),
        split[2].reshape(5, states2),
        split[3],
        split[4],
        split[5],
        split[6],
        sum_out,
    )


def solution(mesh):
    placed = (
        P("dp", "tensor"),
        P("dp", "tensor"),
        P("dp", None),
        P(),
        P(None, None, "tensor"),
        P(None, "tensor"),
        P(),
        P(None, "tensor"),
        P(),
        P("tensor"),
        P("tensor"),
        P("tensor"),
        P("tensor"),
        P("tensor", None),
    )
    return jax.shard_map(
        shards,
        mesh=mesh,
        in_specs=placed,
        out_specs=(
            P("dp", "tensor"),
            P("dp", "tensor"),
            P("tensor"),
            P("dp", None, "tensor"),
            P("dp", "tensor"),
            P(("dp", "tensor"), None),
            P(None, "tensor"),
            P(),
            P("tensor"),
            P("tensor"),
            P("tensor"),
            P("tensor"),
            P("tensor", "dp"),
        ),
        check_vma=False,
    )
```

```python
import functools
import math

import jax
import jax.numpy as jnp
from jax import lax
from jax.experimental import pallas as pl
from jax.experimental.pallas import tpu as pltpu
from jax.sharding import PartitionSpec as P

F32 = jnp.float32
BF16 = jnp.bfloat16
HIGHEST = lax.Precision.HIGHEST
EPSILON = 1e-05
LOG2E = math.log2(math.e)
LANES = 128
SPAN = 128
GROUP = 256
UNROLL = 8
HINT = 0.02
ROWS = 512
CHUNKS = 2

NN = (((1,), (0,)), ((), ()))
NT = (((1,), (1,)), ((), ()))
TN = (((0,), (0,)), ((), ()))


def dot(left, right, dims=NN, precision=None):
    return lax.dot_general(left, right, dims, precision=precision, preferred_element_type=F32)


def sigmoid(a):
    return 0.5 * jnp.tanh(0.5 * a) + 0.5


def iota(shape, dim):
    return lax.broadcasted_iota(jnp.int32, shape, dim)


def tri(upper):
    rows, cols = iota((SPAN, SPAN), 0), iota((SPAN, SPAN), 1)
    return ((rows <= cols) if upper else (rows >= cols)).astype(F32)


def call(body, grid, in_specs, out_specs, out_shape, scratch=(), prefetch=0, flops=0, moved=0, name=None, vmem=56):
    return pl.pallas_call(
        body,
        grid_spec=pltpu.PrefetchScalarGridSpec(
            num_scalar_prefetch=prefetch,
            grid=grid,
            in_specs=in_specs,
            out_specs=out_specs,
            scratch_shapes=list(scratch),
        ),
        out_shape=out_shape,
        compiler_params=pltpu.CompilerParams(
            vmem_limit_bytes=vmem * 1024 * 1024, dimension_semantics=("arbitrary",) * len(grid)
        ),
        cost_estimate=pl.CostEstimate(
            flops=int(flops * HINT), bytes_accessed=int(moved * HINT), transcendentals=0
        ),
        name=name,
    )


def held(shape):
    zeros = (0,) * len(shape)
    return pl.BlockSpec(shape, lambda *_: zeros, pipeline_mode=pl.Buffered(1))


def shape_of(*dims, dtype=F32):
    return jax.ShapeDtypeStruct(dims, dtype)


def conv_taps(before, now, marks, filters):
    rows = now.shape[0]
    wide = jnp.concatenate([before, now], axis=0)
    total = filters[4:5] + filters[0:1] * now
    shifted = [now]
    for k in range(1, 4):
        moved = wide[8 - k : 8 - k + rows] * marks[:, k - 1 : k]
        shifted.append(moved)
        total = total + filters[k : k + 1] * moved
    return total, shifted


def rows_before(array, start):
    return array[pl.ds(pl.multiple_of(jnp.maximum(start - 8, 0), 8), 8), :]


def conv_back(later, marks, filters):
    rows = later.shape[0] - 8
    total = filters[0:1] * later[:rows]
    for k in range(1, 4):
        total = total + filters[k : k + 1] * (later[k : k + rows] * marks[k : k + rows, k - 1 : k])
    return total


def fold_lanes(power):
    folded = power[:, :LANES]
    for tile in range(1, power.shape[1] // LANES):
        folded = folded + power[:, tile * LANES : (tile + 1) * LANES]
    return folded


def spread(table, section, heads, count):
    lane = iota((table.shape[0], LANES), 1)
    tiles = []
    for pair in range(count // 2):
        at = section * heads + 2 * pair
        tiles.append(jnp.where(lane < LANES // 2, table[:, at : at + 1], table[:, at + 1 : at + 2]))
    return jnp.concatenate(tiles, axis=1)


def front_kernel(
    parts, heads, rank, *refs,
):
    pieces, refs = refs[:parts], refs[parts:]
    (gain, w_maps, conv_maps, bias, rate, seg_row, w_gate, w_value, conv, skip, gate_gain, marks,
     *outs), (value, gate, mixed, low_gated, memory, squares, proj, cross, state), (
        normed, pre_state, maps, maps_t, per_head, rows_out, cross_t, sems
    ) = refs[:-17], refs[-17:-8], refs[-8:]
    copies = [
        pltpu.make_async_copy(source, target, sems.at[i])
        for i, (source, target) in enumerate(
            zip((normed, pre_state, maps, maps_t, per_head, rows_out, cross_t), outs)
        )
    ]
    g = pl.program_id(0)
    length, quarter = pieces[0].shape
    width = quarter * parts
    blocks = length // SPAN
    states = maps.shape[1] // 2
    count = GROUP // 64
    lane = iota((SPAN, LANES), 1)

    @pl.when(g == 0)
    def _():
        squares[...] = jnp.zeros_like(squares)

        def normalise(b, _):
            at = pl.ds(pl.multiple_of(b * SPAN, SPAN), SPAN)
            wide = [piece[at, :].astype(F32) for piece in pieces]
            total = functools.reduce(jnp.add, [array * array for array in wide])
            scale = lax.rsqrt(jnp.sum(total, axis=1, keepdims=True) / width + EPSILON)
            per_head[at, :] = jnp.broadcast_to(scale, (SPAN, LANES))
            for k in range(parts):
                to = pl.multiple_of((rank[0] ^ k) * quarter, quarter)
                normed[at, pl.ds(to, quarter)] = (wide[k] * scale * gain[:, pl.ds(to, quarter)]).astype(BF16)
            return 0

        lax.fori_loop(0, blocks, normalise, 0, unroll=2)
        copies[0].start()
        proj[...] = dot(normed[...], w_maps[...])

        def tables(b, _):
            start = pl.multiple_of(b * SPAN, SPAN)
            at = pl.ds(start, SPAN)
            mark = marks[at, :]
            now = proj[at, : 2 * states]
            pre_state[at, :] = now
            total, _ = conv_taps(rows_before(proj, start)[:, : 2 * states], now, mark, conv_maps[...])
            both = total * sigmoid(total)
            keys, queries = both[:, :states], both[:, states:]
            low_keys, low_queries = keys.astype(BF16), queries.astype(BF16)
            maps[at, :states] = low_keys
            maps[at, states:] = low_queries
            maps_t[:states, pl.ds(start, SPAN)] = keys.T.astype(BF16)
            maps_t[states:, pl.ds(start, SPAN)] = queries.T.astype(BF16)

            pre = proj[at, 2 * states :] + bias[...]
            size = jnp.maximum(pre, 0.0) + jnp.log1p(jnp.exp(-jnp.abs(pre)))
            rising = dot(tri(False), -rate[...] * size, precision=HIGHEST)
            entering = jnp.exp(rising) * mark[:, 3:4]
            leaving = jnp.exp(rising[SPAN - 1 :] - rising) * mark[:, 4:5]
            rising = rising * LOG2E
            section = lane // heads
            packed = jnp.where(section == 0, rising, entering)
            packed = jnp.where(section == 2, leaving, packed)
            packed = jnp.where(section == 3, size, packed)
            packed = jnp.where(section == 4, pre, packed)
            packed = jnp.where(section == 5, per_head[at, :], packed)
            per_head[at, :] = packed
            turned = rising.T
            for group in range(rows_out.shape[0]):
                rows_out[group, pl.ds(pl.multiple_of(b * 8, 8), 8), :] = turned[group * count : group * count + 8]
            same = mark[:, 6:7] == seg_row[0:1, pl.ds(start, SPAN)]
            rows, cols = iota((SPAN, SPAN), 0), iota((SPAN, SPAN), 1)
            cross[at, :] = jnp.where(same & (rows >= cols), dot(low_queries, low_keys, NT), 0.0)
            cross_t[at, :] = jnp.where(same & (rows <= cols), dot(low_keys, low_queries, NT), 0.0)
            return 0

        lax.fori_loop(0, blocks, tables, 0, unroll=2)
        for copy in copies[1:]:
            copy.start()

    both = dot(normed[...], jnp.concatenate([w_gate[...], w_value[...]], axis=1))
    gate[...] = both[:, :GROUP].astype(BF16)
    value[...] = both[:, GROUP:]
    state[...] = jnp.zeros_like(state)
    turn = lax.rem(LANES - count * g, LANES)

    def block(b, _):
        start = pl.multiple_of(b * SPAN, SPAN)
        at = pl.ds(start, SPAN)
        total, _ = conv_taps(rows_before(value, start), value[at, :], marks[at, :], conv[...])
        inputs = total * sigmoid(total)
        table = pltpu.roll(per_head[at, :], turn, 1)
        entering, leaving, size = (spread(table, s, heads, count) for s in (1, 2, 3))
        scaled = inputs * size
        keys_t = maps_t[0:states, pl.ds(start, SPAN)]
        queries = maps[at, states:]
        low_state = state[...].astype(BF16)
        memory[b] = low_state
        out = entering * dot(queries, low_state) + skip[...] * inputs
        rising_rows = rows_out[g, pl.ds(pl.multiple_of(b * 8, 8), 8), :]
        crossed = cross[at, :]
        parts_out = []
        for pair in range(count // 2):
            weights = []
            for j in (2 * pair, 2 * pair + 1):
                gap = jnp.minimum(table[:, j : j + 1] - rising_rows[j : j + 1, :], 0.0)
                weights.append((jnp.exp2(gap) * crossed).astype(BF16))
            tile = scaled[:, pair * LANES : (pair + 1) * LANES]
            stacked = jnp.concatenate(
                [
                    jnp.where(lane < LANES // 2, tile, 0.0).astype(BF16),
                    jnp.where(lane < LANES // 2, 0.0, tile).astype(BF16),
                ],
                axis=0,
            )
            parts_out.append(dot(jnp.concatenate(weights, axis=1), stacked))
        out = out + jnp.concatenate(parts_out, axis=1)
        fresh = dot(keys_t, (leaving * scaled).astype(BF16))
        state[...] = state[...] * entering[SPAN - 1 :] + fresh
        mixed[at, :] = out
        opened = gate[at, :].astype(F32)
        gated = out * (opened * sigmoid(opened))
        low_gated[at, :] = (gated * gate_gain[...]).astype(BF16)
        squares[at, :] += fold_lanes(gated * gated)
        return 0

    lax.fori_loop(0, blocks, block, 0, unroll=UNROLL)

    @pl.when(g == pl.num_programs(0) - 1)
    def _():
        for copy in copies:
            copy.wait()


def assemble(pieces, target, sems, where):
    copies = [
        pltpu.make_async_copy(pieces[k].at[:, pl.ds(at, size)], target.at[:, pl.ds(to, size)], sems.at[i])
        for i, (k, at, to, size) in enumerate(where)
    ]
    for copy in copies:
        copy.start()
    for copy in copies:
        copy.wait()


def cotangent_kernel(parts, rank, *refs):
    pieces, (w_out, gated, squares, grad, stats, sums, full, sems) = refs[:parts], refs[parts:]
    g = pl.program_id(0)
    length, quarter = pieces[0].shape

    @pl.when(g == 0)
    def _():
        sums[...] = jnp.zeros_like(sums)
        places = [pl.multiple_of((rank[0] ^ k) * quarter, quarter) for k in range(parts)]
        assemble(pieces, full, sems, [(k, 0, places[k], quarter) for k in range(parts)])

    grad[...] = dot(full[...], w_out[...], NT).astype(BF16)

    def chunk(i, _):
        at = pl.ds(pl.multiple_of(i * SPAN, SPAN), SPAN)
        sums[at, :] += fold_lanes(grad[at, :].astype(F32) * gated[at, :].astype(F32))
        return 0

    lax.fori_loop(0, length // SPAN, chunk, 0, unroll=2)

    @pl.when(g == pl.num_programs(0) - 1)
    def _():
        row = iota((8, LANES), 0)
        stats[...] = dot((row == 0).astype(F32), squares[...], NT, HIGHEST) + dot(
            (row == 1).astype(F32), sums[...], NT, HIGHEST
        )


def gate_kernel(parts, run, channels_all, stacked, place, rank, *refs):
    pieces, refs = refs[:parts], refs[parts:]
    (grad, gate, mixed, gain, stats, marks, low_mixed, grad_mixer, grad_gate, grad_gain), refs = refs[:10], refs[10:]
    targets, (sent, kept, sems) = refs[:-3], refs[-3:]
    length, quarter = pieces[0].shape
    grad_gain[...] = jnp.zeros_like(grad_gain)
    pairs = quarter // (2 * run)
    bits = (parts * pairs - 1).bit_length()
    copies = []
    for half, target in ((1, sent), (0, kept)):
        for k in range(parts):
            for j in range(pairs):
                at = pl.multiple_of((2 * j + (place[0] ^ half)) * run, run)
                to = pl.multiple_of(turned((rank[0] ^ k) * pairs + j, bits) * run, run)
                copies.append(
                    pltpu.make_async_copy(
                        pieces[k].at[:, pl.ds(at, run)], target.at[:, pl.ds(to, run)], sems.at[len(copies)]
                    )
                )

    @pl.when(pl.program_id(0) == 0)
    def _():
        for copy in copies:
            copy.start()

    def chunk(i, _):
        start = pl.multiple_of(i * SPAN, SPAN)
        at = pl.ds(start, SPAN)
        columns = jnp.concatenate([stats[:, pl.ds(start, SPAN)]] * (SPAN // 8), axis=0).T
        keep = marks[at, 5:6]
        scale = lax.rsqrt(columns[:, 0:1] / channels_all + EPSILON)
        factor = scale * keep
        pull = scale * scale * factor * columns[:, 1:2] / channels_all
        opened, out, now = gate[at, :].astype(F32), mixed[at, :], grad[at, :].astype(F32)
        chance = sigmoid(opened)
        swish = opened * chance
        gated = out * swish
        scaled = gated * factor
        low_mixed[at, :] = (scaled * gain[...]).astype(BF16)
        grad_gain[...] += jnp.sum(now * scaled, axis=0, keepdims=True)
        grad_gated = now * (factor * gain[...]) - gated * pull
        grad_mixer[at, :] = (grad_gated * swish).astype(BF16)
        grad_gate[at, :] = (grad_gated * out * chance * (1.0 + opened * (1.0 - chance))).astype(BF16)
        return 0

    lax.fori_loop(0, length // SPAN, chunk, 0, unroll=4)

    @pl.when(pl.program_id(0) == 0)
    def _():
        for copy in copies:
            copy.wait()

    for half, source in enumerate((sent, kept)):
        now = dot(low_mixed[...], source[...], TN).astype(BF16)
        if stacked:
            targets[0][half] = now
        else:
            targets[half][...] = now


def weight_kernel(place, left_send, left_own, *refs):
    right, targets = refs[:-2], refs[-2:]
    for left, target in zip((left_send, left_own), targets):
        at = 0
        for part in right:
            size = part.shape[1]
            target[:, at : at + size] = dot(left[...], part[...], TN).astype(BF16)
            at += size


def backward_kernel(
    heads, first, value, grad_out, mixed, memory, conv, skip, per_head, marks, rows_in, maps, maps_t, cross_t,
    grad_value, grad_conv, grad_skip, grad_cross, folded, grad_maps,
    later, grad_memory,
):
    g = pl.program_id(0) + first
    length = grad_out.shape[0]
    blocks = length // SPAN
    states = maps.shape[1] // 2
    count = GROUP // 64
    lane = iota((SPAN, LANES), 1)
    row = iota((SPAN, GROUP), 0)
    turn = lax.rem(LANES - count * g, LANES)
    channel, target = iota((GROUP, LANES), 0), iota((GROUP, LANES), 1)
    pick_rise = (target == count * g + channel // 64).astype(BF16)
    pick_size = (target == heads + count * g + channel // 64).astype(BF16)
    later[...] = jnp.zeros_like(later)
    grad_memory[...] = jnp.zeros_like(grad_memory)
    grad_conv[...] = jnp.zeros_like(grad_conv)
    grad_skip[...] = jnp.zeros_like(grad_skip)

    @pl.when(g == first)
    def _():
        grad_cross[...] = jnp.zeros_like(grad_cross)
        folded[...] = jnp.zeros_like(folded)
        grad_maps[...] = jnp.zeros_like(grad_maps)

    def block(i, _):
        b = blocks - 1 - i
        start = pl.multiple_of(b * SPAN, SPAN)
        at = pl.ds(start, SPAN)
        filters = conv[...]
        total, shifted = conv_taps(rows_before(value, start), value[at, :], marks[at, :], filters)
        chance = sigmoid(total)
        inputs = total * chance
        table = pltpu.roll(per_head[at, :], turn, 1)
        entering, leaving, size = (spread(table, s, heads, count) for s in (1, 2, 3))
        scaled = inputs * size
        low_scaled = scaled.astype(BF16)
        pulled = grad_out[at, :].astype(F32)
        keys, queries_t = maps[at, 0:states], maps_t[states:, pl.ds(start, SPAN)]
        memory_now = memory[b]
        grad_next = grad_memory[...]
        low_next = grad_next.astype(BF16)
        entered = (entering * pulled).astype(BF16)
        left = (leaving * scaled).astype(BF16)
        grad_maps[at, 0:states] += dot(left, low_next, NT)
        grad_maps[at, states:] += dot(entered, memory_now, NT)
        rising_rows = rows_in[0, pl.ds(pl.multiple_of(b * 8, 8), 8), :]
        crossed_t = cross_t[at, :]
        cross_sum = jnp.zeros((SPAN, SPAN), F32)
        parts = []
        for pair in range(count // 2):
            tile = pulled[:, pair * LANES : (pair + 1) * LANES]
            one = jnp.where(lane < LANES // 2, tile, 0.0).astype(BF16)
            two = jnp.where(lane < LANES // 2, 0.0, tile).astype(BF16)
            low_tile = low_scaled[:, pair * LANES : (pair + 1) * LANES]
            weights = []
            for j, masked in ((2 * pair, one), (2 * pair + 1, two)):
                gap = table[:, j : j + 1] - rising_rows[j : j + 1, :]
                cross_sum = cross_sum + jnp.exp2(jnp.minimum(gap, 0.0)) * dot(masked, low_tile, NT)
                weights.append((jnp.exp2(jnp.minimum(-gap, 0.0)) * crossed_t).astype(BF16))
            parts.append(dot(jnp.concatenate(weights, axis=1), jnp.concatenate([one, two], axis=0)))
        grad_cross[at, :] += cross_sum
        grad_within = jnp.concatenate(parts, axis=1)
        grad_left = dot(keys, low_next)
        grad_scaled = grad_within + leaving * grad_left
        scanned = mixed[at, :] - skip[...] * inputs
        kept = left.astype(F32) * grad_left
        rise = pulled * scanned - low_scaled.astype(F32) * grad_within - kept
        carried = entering[SPAN - 1 :] * jnp.sum(low_next.astype(F32) * memory_now.astype(F32), axis=0, keepdims=True)
        rise = rise + jnp.where(row == SPAN - 1, carried + jnp.sum(kept, axis=0, keepdims=True), 0.0)
        grown = grad_scaled * inputs
        summed = folded[at, :]
        for product, pick in ((rise, pick_rise), (grown, pick_size)):
            high = product.astype(BF16)
            rest = (product - high.astype(F32)).astype(BF16)
            summed = summed + dot(high, pick) + dot(rest, pick)
        folded[at, :] = summed
        grad_skip[...] += jnp.sum(pulled * inputs, axis=0, keepdims=True)
        grad_inputs = size * grad_scaled + skip[...] * pulled
        grad_total = grad_inputs * (chance * (1.0 + total * (1.0 - chance)))
        for k in range(4):
            grad_conv[k : k + 1] += jnp.sum(grad_total * shifted[k], axis=0, keepdims=True)
        grad_conv[4:5] += jnp.sum(grad_total, axis=0, keepdims=True)
        longer = jnp.concatenate([grad_total, later[...]], axis=0)
        later[...] = grad_total[:8]
        grad_value[at, :] = conv_back(longer, marks[pl.ds(start, SPAN + 8), :], filters).astype(BF16)
        grad_memory[...] = entering[SPAN - 1 :] * grad_next + dot(queries_t, entered)
        return 0

    lax.fori_loop(0, blocks, block, 0, unroll=UNROLL)


def finish_kernel(
    heads, calls, *refs,
):
    summed_parts, refs = refs[: 3 * calls], refs[3 * calls :]
    (per_head, marks, maps, seg_row, pre_state, conv_state, rate,
     grad_state, grad_step, grad_conv_state, grad_heads, later) = refs
    length = maps.shape[0]
    blocks = length // SPAN
    states = maps.shape[1] // 2
    later[...] = jnp.zeros_like(later)
    grad_conv_state[...] = jnp.zeros_like(grad_conv_state)
    grad_heads[...] = jnp.zeros_like(grad_heads)

    def block(i, _):
        start = pl.multiple_of((blocks - 1 - i) * SPAN, SPAN)
        at = pl.ds(start, SPAN)
        mark = marks[at, :]
        rows, cols = iota((SPAN, SPAN), 0), iota((SPAN, SPAN), 1)
        linked = (rows >= cols) & (mark[:, 6:7] == seg_row[0:1, pl.ds(start, SPAN)])
        grad_cross, summed, grad_maps = (
            functools.reduce(jnp.add, [ref[at, :] for ref in summed_parts[j::3]]) for j in range(3)
        )
        crossed = jnp.where(linked, grad_cross, 0.0)
        keys, queries = maps[at, 0:states], maps[at, states:]
        grad_keys = grad_maps[:, :states] + dot(crossed.T.astype(BF16), queries)
        grad_queries = grad_maps[:, states:] + dot(crossed.astype(BF16), keys)
        filters = conv_state[...]
        total, shifted = conv_taps(rows_before(pre_state, start), pre_state[at, :], mark, filters)
        chance = sigmoid(total)
        grad_total = jnp.concatenate([grad_keys, grad_queries], axis=1) * (chance * (1.0 + total * (1.0 - chance)))
        for k in range(4):
            grad_conv_state[k : k + 1] += jnp.sum(grad_total * shifted[k], axis=0, keepdims=True)
        grad_conv_state[4:5] += jnp.sum(grad_total, axis=0, keepdims=True)
        longer = jnp.concatenate([grad_total, later[...]], axis=0)
        later[...] = grad_total[:8]
        grad_state[at, :] = conv_back(longer, marks[pl.ds(start, SPAN + 8), :], filters).astype(BF16)

        table = per_head[at, :]
        grad_decay = dot(tri(True), summed, precision=HIGHEST)
        size = pltpu.roll(table, LANES - 3 * heads, 1)
        pre = pltpu.roll(table, LANES - 4 * heads, 1)
        grad_size = pltpu.roll(summed, LANES - heads, 1) - rate[...] * grad_decay
        valid = iota((SPAN, LANES), 1) < heads
        grad_pre = jnp.where(valid, grad_size * sigmoid(pre), 0.0)
        grad_step[at, :] = grad_pre.astype(BF16)
        grad_heads[0:1] += jnp.sum(grad_pre, axis=0, keepdims=True)
        grad_heads[1:2] += jnp.sum(-rate[...] * size * grad_decay, axis=0, keepdims=True)
        return 0

    lax.fori_loop(0, blocks, block, 0, unroll=UNROLL)


def put(far, near, total):
    step = pl.program_id(0)

    @pl.when(step < 2)
    def _():
        far[0] = total.astype(BF16)

    @pl.when(step >= 2)
    def _():
        near[0] = total.astype(BF16)


def output_kernel(rank, gated, w_out, far, near):
    put(far, near, dot(gated[...], w_out[...]))


def normed_kernel(chunks, rank, *refs):
    grads, (grad_state, grad_step, w_inner, w_maps), refs = refs[: 2 * chunks], refs[2 * chunks : 2 * chunks + 4], refs[2 * chunks + 4 :]
    outs, (joined, joined_maps) = refs[:-2], refs[-2:]

    @pl.when(pl.program_id(0) == 0)
    def _():
        for target, parts in ((joined, grads), (joined_maps, (grad_state, grad_step))):
            at = 0
            for part in parts:
                target[:, at : at + part.shape[1]] = part[...]
                at += part.shape[1]

    total = dot(joined[...], w_inner[...], NT) + dot(joined_maps[...], w_maps[...], NT)
    put(*outs, total)


def swap(array, axis, mask):
    count = lax.axis_size(axis)
    return lax.ppermute(array, axis, [(i, i ^ mask) for i in range(count)])


def gather_pieces(own, parts):
    pieces = {0: own}
    bit = parts // 2
    while bit >= 1:
        pieces.update({k | bit: swap(piece, "tensor", bit) for k, piece in list(pieces.items())})
        bit //= 2
    return [pieces[k] for k in range(parts)]


def tie(array, *first):
    return lax.optimization_barrier((array, *first))[0]


def meet(sums, *arrays):
    arrays = lax.optimization_barrier((*arrays, *(part.got for part in sums)))
    for part, got in zip(sums, arrays[len(arrays) - len(sums) :]):
        part.got = got
    return arrays[: len(arrays) - len(sums)]


def sum_all(array, axis):
    bit = 1
    while bit < lax.axis_size(axis):
        array = array + swap(array, axis, bit)
        bit *= 2
    return array


def rest_masks(low_bits):
    bits = (lax.axis_size("dp") - 1).bit_length()
    return [1 << bit for bit in (*range(low_bits + 1, bits), *range(low_bits - 1, -1, -1))]


def turned(index, bits):
    result = index * 0
    for bit in range(bits):
        result = result | (((index >> bit) & 1) << (bits - 1 - bit))
    return result


class Sum:
    def __init__(self, own, got, dim, low_bits):
        self.terms, self.got, self.dim, self.masks = [own], got, dim, rest_masks(low_bits)
        if got is None:
            self.send()

    def advance(self):
        self.terms.append(self.got)
        return self.send()

    def send(self):
        mask = self.masks.pop(0)
        top = (lax.axis_index("dp") & mask) // mask
        size = self.terms[0].shape[self.dim] // 2

        def cut(half):
            return [lax.dynamic_slice_in_dim(term, half * size, size, self.dim) for term in self.terms]

        sent = functools.reduce(jnp.add, [term.astype(F32) for term in cut(1 - top)]).astype(BF16)
        self.terms, self.got, self.sent = cut(top), swap(sent, "dp", mask), sent
        return sent

    def result(self):
        while self.masks:
            self.advance()
        return functools.reduce(jnp.add, [term.astype(F32) for term in (*self.terms, self.got)])


def add_low(left, right):
    return (left.astype(F32) + right.astype(F32)).astype(BF16)


def shards(
    tokens,
    cotangent,
    doc_lengths,
    norm_gain,
    w_inner,
    w_step,
    w_state,
    conv_inner,
    conv_state,
    step_bias,
    log_rate,
    skip_gain,
    gate_gain,
    w_out,
):
    parts = lax.axis_size("tensor")
    groups = lax.axis_size("dp")
    rank = lax.axis_index("tensor").astype(jnp.int32)
    ranks = rank.reshape(1)
    length, quarter = tokens.shape
    width = quarter * parts
    channels = w_inner.shape[2]
    heads = w_step.shape[1]
    states2 = w_state.shape[1]
    states = states2 // 2
    blocks = length // SPAN
    steps = channels // GROUP
    repeat = LANES // heads
    piece_rows = width // groups
    low_bits = 0
    while (piece_rows << low_bits) < LANES:
        low_bits += 1
    run = piece_rows << low_bits
    half_width = width // 2
    high_bits = (groups - 1).bit_length() - 1 - low_bits
    place = ((lax.axis_index("dp") >> low_bits) & 1).astype(jnp.int32).reshape(1)

    token_y = swap(tokens, "tensor", 2)
    grad_y = swap(tie(cotangent, token_y), "tensor", 2)
    flat = w_inner.reshape(width, 2 * channels)
    w_maps = jnp.concatenate([w_state, jnp.tile(w_step, (1, repeat))], axis=1)
    step_pad = jnp.pad(w_step, ((0, 0), (0, LANES - heads)))
    bias8 = jnp.tile(step_bias, repeat)[None, :]
    rate8 = jnp.exp(jnp.tile(log_rate, repeat))[None, :]
    skip_row = jnp.repeat(skip_gain, channels // heads)[None, :]
    gain_row = gate_gain[None, :]
    conv_pad = jnp.pad(conv_inner, ((0, 3), (0, 0)))
    conv_state_pad = jnp.pad(conv_state, ((0, 3), (0, 0)))

    doc_ends = jnp.cumsum(doc_lengths[0])
    positions = jnp.arange(length, dtype=jnp.int32)
    segment = jnp.sum((positions[:, None] >= doc_ends[None, :]).astype(jnp.int32), axis=1)
    present = positions < doc_ends[-1]
    by_block = segment.reshape(blocks, SPAN)
    final = by_block[:, -1:]
    before = jnp.concatenate([jnp.full((1, 1), -1, jnp.int32), final[:-1]], axis=0)
    marks = [
        jnp.concatenate([jnp.full((k,), -1, jnp.int32), segment[:-k]]) == segment for k in (1, 2, 3)
    ]
    marks += [(by_block == before).reshape(-1), (by_block == final).reshape(-1), present]
    marks = [mark.astype(F32) for mark in marks] + [segment.astype(F32)]
    marks = jnp.pad(jnp.stack(marks, axis=1), ((0, 8), (0, LANES - len(marks))))
    seg_row = jnp.broadcast_to(segment.astype(F32)[None, :], (8, length))

    token_y, flat, w_maps, step_pad, marks, seg_row, skip_row, conv_pad = lax.optimization_barrier(
        (token_y, flat, w_maps, step_pad, marks, seg_row, skip_row, conv_pad)
    )
    token_pieces = [tokens, swap(tokens, "tensor", 1), token_y, swap(token_y, "tensor", 1)]

    by_group = lambda rows: pl.BlockSpec((rows, GROUP), lambda g, *_: (0, g))
    (normed, pre_state, maps, maps_t, per_head, rising_rows, cross_t, value, gate, mixer_out, low_gated, memory, squares) = call(
        functools.partial(front_kernel, parts, heads),
        (steps,),
        [held((length, quarter))] * parts
        + [
            held((1, width)), held((width, states2 + LANES)), held((8, states2)),
            held((1, LANES)), held((1, LANES)), held((8, length)),
            pl.BlockSpec((width, GROUP), lambda g, *_: (0, g)), pl.BlockSpec((width, GROUP), lambda g, *_: (0, steps + g)),
            by_group(8), by_group(1), by_group(1), held((length + 8, LANES)),
        ],
        [
            *[pl.BlockSpec(memory_space=pl.ANY)] * 7,
            by_group(length), by_group(length), by_group(length), by_group(length),
            pl.BlockSpec((blocks, states, GROUP), lambda g, *_: (0, 0, g)), held((length, LANES)),
        ],
        [
            shape_of(length, width, dtype=BF16), shape_of(length, states2), shape_of(length, states2, dtype=BF16),
            shape_of(states2, length, dtype=BF16), shape_of(length, LANES), shape_of(steps, blocks * 8, SPAN),
            shape_of(length, SPAN), shape_of(length, channels), shape_of(length, channels, dtype=BF16),
            shape_of(length, channels), shape_of(length, channels, dtype=BF16),
            shape_of(blocks, states, channels, dtype=BF16), shape_of(length, LANES),
        ],
        [
            pltpu.VMEM((length, states2 + LANES), F32), pltpu.VMEM((length, SPAN), F32),
            pltpu.VMEM((states, GROUP), F32),
            pltpu.VMEM((length, width), BF16), pltpu.VMEM((length, states2), F32), pltpu.VMEM((length, states2), BF16),
            pltpu.VMEM((states2, length), BF16), pltpu.VMEM((length, LANES), F32),
            pltpu.VMEM((steps, blocks * 8, SPAN), F32), pltpu.VMEM((length, SPAN), F32), pltpu.SemaphoreType.DMA((7,)),
        ],
        prefetch=1,
        flops=8 * length * width * channels,
        moved=length * width * 4 + width * channels * 4 + length * channels * 14,
        name="front",
        vmem=56,
    )(
        ranks, *token_pieces, norm_gain[None, :], w_maps, conv_state_pad, bias8, rate8, seg_row, flat, flat, conv_pad,
        skip_row, gain_row, marks,
    )

    grad_y = tie(grad_y, squares)
    grad_pieces = [cotangent, swap(cotangent, "tensor", 1), grad_y, swap(grad_y, "tensor", 1)]
    pieces_any = [pl.BlockSpec(memory_space=pl.ANY)] * parts
    double = 2 * GROUP
    by_double = lambda rows: pl.BlockSpec((rows, double), lambda g, *_: (0, g))
    grad_mixed, stats = call(
        functools.partial(cotangent_kernel, parts),
        (channels // double,),
        pieces_any
        + [
            pl.BlockSpec((double, width), lambda g, *_: (g, 0)),
            by_double(length), held((length, LANES)),
        ],
        [by_double(length), held((8, length))],
        [shape_of(length, channels, dtype=BF16), shape_of(8, length)],
        [pltpu.VMEM((length, LANES), F32), pltpu.VMEM((length, width), BF16), pltpu.SemaphoreType.DMA((parts,))],
        prefetch=1,
        flops=2 * length * width * channels,
        moved=length * width * 2 + width * channels * 2 + length * channels * 12,
        name="cotangent",
        vmem=56,
    )(ranks, *grad_pieces, w_out, low_gated, squares)
    spans = steps // CHUNKS

    def chunk_spec(rows, c):
        return pl.BlockSpec((rows, GROUP), lambda g, *_: (0, c * spans + g))

    def gate_part(c, stats, stacked):
        size = spans * GROUP
        if stacked:
            outs = [pl.BlockSpec((2, GROUP, half_width), lambda g, *_: (0, g, 0))]
            shapes = [shape_of(2, size, half_width, dtype=BF16)]
        else:
            outs = [pl.BlockSpec((GROUP, half_width), lambda g, *_: (g, 0))] * 2
            shapes = [shape_of(size, half_width, dtype=BF16)] * 2
        return call(
            functools.partial(gate_kernel, parts, run, channels * parts, stacked),
            (spans,),
            pieces_any
            + [
                chunk_spec(length, c), chunk_spec(length, c), chunk_spec(length, c), chunk_spec(1, c),
                held((8, length)), held((length + 8, LANES)),
            ],
            [by_group(length), by_group(length), by_group(length), by_group(1), *outs],
            [
                shape_of(length, size, dtype=BF16), shape_of(length, size, dtype=BF16),
                shape_of(length, size, dtype=BF16), shape_of(1, size), *shapes,
            ],
            [
                pltpu.VMEM((length, half_width), BF16), pltpu.VMEM((length, half_width), BF16),
                pltpu.SemaphoreType.DMA((width // run,)),
            ],
            prefetch=2,
            flops=2 * length * width * size,
            moved=length * width * 2 + length * size * 18 + width * size * 2,
            name="gate",
        )(place, ranks, *grad_pieces, grad_mixed, gate, mixer_out, gain_row, stats, marks)

    def weight_part(*right):
        runs = half_width // run
        columns = [part.shape[1] for part in right]
        out = pl.BlockSpec((run, sum(columns)), lambda j, p: (turned(j, (runs - 1).bit_length()), 0))
        shape = shape_of(half_width, sum(columns), dtype=BF16)
        return call(
            weight_kernel,
            (runs,),
            [
                pl.BlockSpec((length, run), lambda j, p: (0, 2 * j + (p[0] ^ 1))),
                pl.BlockSpec((length, run), lambda j, p: (0, 2 * j + p[0])),
            ]
            + [held((length, size)) for size in columns],
            [out, out],
            [shape, shape],
            prefetch=1,
            flops=2 * length * width * sum(columns),
            moved=length * width * 2 + length * sum(columns) * 2 + width * sum(columns) * 2,
            name="weights",
        )(place, normed, normed, *right)

    all_lanes = held((length, LANES))

    def backward_part(c, grad_out):
        size = spans * GROUP
        return call(
            functools.partial(backward_kernel, heads, c * spans),
            (spans,),
            [
                chunk_spec(length, c), by_group(length), chunk_spec(length, c),
                pl.BlockSpec((blocks, states, GROUP), lambda g, *_: (0, 0, c * spans + g)),
                chunk_spec(8, c), chunk_spec(1, c), all_lanes, held((length + 8, LANES)),
                pl.BlockSpec((1, blocks * 8, SPAN), lambda g, *_: (c * spans + g, 0, 0)),
                held((length, states2)), held((states2, length)), held((length, SPAN)),
            ],
            [by_group(length), by_group(8), by_group(1), held((length, SPAN)), all_lanes, held((length, states2))],
            [
                shape_of(length, size, dtype=BF16), shape_of(8, size), shape_of(1, size),
                shape_of(length, SPAN), shape_of(length, LANES), shape_of(length, states2),
            ],
            [pltpu.VMEM((8, GROUP), F32), pltpu.VMEM((states, GROUP), F32)],
            flops=40e9 / CHUNKS,
            moved=length * size * 14,
            name="backward",
            vmem=56,
        )(
            value, grad_out, mixer_out, memory, conv_pad, skip_row, per_head, marks, rising_rows, maps, maps_t,
            cross_t,
        )

    def piece_of(i, r):
        return r[0] ^ jnp.where(i == 0, 1, jnp.where(i == 1, 3, jnp.where(i == 2, 2, 0)))

    def far_near(count):
        specs = [
            pl.BlockSpec((1, length, quarter), lambda i, r: (jnp.minimum(i, 1), 0, 0)),
            pl.BlockSpec((1, length, quarter), lambda i, r: (jnp.maximum(i, 2) - 2, 0, 0)),
        ]
        return specs, [shape_of(2, length, quarter, dtype=BF16), shape_of(count, length, quarter, dtype=BF16)]

    def output_part(low_gated):
        return call(
            output_kernel,
            (4,),
            [held((length, channels)), pl.BlockSpec((channels, quarter), lambda i, r: (0, piece_of(i, r)))],
            *far_near(2),
            prefetch=1,
            flops=2 * length * channels * width,
            moved=length * channels * 2 + channels * width * 2 + length * width * 2,
            name="output",
        )(ranks, low_gated, w_out)

    def normed_part(grad_gate):
        grads = (*grad_gate, *grad_value)
        return call(
            functools.partial(normed_kernel, len(grad_gate)),
            (4,),
            [held((length, part.shape[1])) for part in grads]
            + [
                held((length, states2)), held((length, LANES)),
                pl.BlockSpec((quarter, 2 * channels), lambda i, r: (piece_of(i, r), 0)),
                pl.BlockSpec((quarter, states2 + LANES), lambda i, r: (piece_of(i, r), 0)),
            ],
            *far_near(2),
            [pltpu.VMEM((length, 2 * channels), BF16), pltpu.VMEM((length, states2 + LANES), BF16)],
            prefetch=1,
            flops=2 * length * (2 * channels + states2 + LANES) * width,
            moved=length * channels * 4 + channels * width * 4 + length * width * 2,
            name="normed_grad",
        )(ranks, *grads, grad_state, grad_step, flat, w_maps)

    def over_x(send):
        return swap(send, "dp", 1 << low_bits)

    stats = sum_all(stats, "tensor")

    first = gate_part(0, stats, False)
    sum_out = [Sum(first[5], over_x(first[4]), 1, low_bits)]
    other = gate_part(1, tie(stats, first[5]), False)
    sum_out.append(Sum(other[5], over_x(other[4]), 1, low_bits))
    low_mixed, grad_mixer, grad_gate, grad_gain = zip(first[:4], other[:4])
    gate_send, gate_own = weight_part(tie(grad_gate[0], other[5]), *grad_gate[1:])
    sum_gate = Sum(gate_own, over_x(gate_send), 0, low_bits)
    out_far, out_near = output_part(tie(low_gated, gate_own))

    out_far, out_near = meet(sum_out[:1], out_far, out_near)
    moved = [sum_out[0].advance(), out_far]
    out_far_got = swap(out_far, "tensor", 1)
    back = backward_part(0, tie(grad_mixer[0], *moved))

    grad_value, out_far_got = meet(sum_out, back[0], out_far_got)
    moved = [sum_out[1].advance(), sum_out[0].advance()]
    out_sum = add_low(out_near[0], out_far_got[1])
    out_y = swap(out_sum, "tensor", 2)
    value_send, value_own = weight_part(tie(grad_value, *moved, out_sum))
    sum_value = [Sum(value_own, over_x(value_send), 0, low_bits)]
    backs = [back, backward_part(1, tie(grad_mixer[1], value_own))]

    grad_value2, out_y = meet(sum_out, backs[1][0], out_y)
    moved = [sum_out[1].advance()]
    value_send2, value_own2 = weight_part(tie(grad_value2, *moved))
    sum_value.append(Sum(value_own2, over_x(value_send2), 0, low_bits))
    moved = [value_own2]
    grad_value, grad_conv, grad_skip, cross_parts, folded_parts, maps_parts = zip(*backs)
    (grad_state, grad_step, grad_conv_state, grad_heads) = call(
        functools.partial(finish_kernel, heads, CHUNKS),
        (1,),
        [held((length, SPAN)), all_lanes, held((length, states2))] * CHUNKS
        + [
            all_lanes, held((length + 8, LANES)), held((length, states2)), held((8, length)),
            held((length, states2)), held((8, states2)), held((1, LANES)),
        ],
        [held((length, states2)), all_lanes, held((8, states2)), held((8, LANES))],
        [
            shape_of(length, states2, dtype=BF16), shape_of(length, LANES, dtype=BF16),
            shape_of(8, states2), shape_of(8, LANES),
        ],
        [pltpu.VMEM((8, states2), F32)],
        flops=4e9,
        moved=length * 2048 * CHUNKS + length * 5000,
        name="finish",
        vmem=32,
    )(
        tie(cross_parts[0], *moved), folded_parts[0], maps_parts[0],
        *[part for three in zip(cross_parts[1:], folded_parts[1:], maps_parts[1:]) for part in three],
        per_head, marks, maps, seg_row, pre_state, conv_state_pad, rate8,
    )

    grad_state, grad_conv_state = meet([sum_gate, sum_out[1]], grad_state, grad_conv_state[:5])
    state_got = swap(grad_state, "tensor", 1)
    grad_conv_state = grad_conv_state + swap(grad_conv_state, "tensor", 1)
    conv_got = swap(grad_conv_state, "tensor", 2)
    moved = [sum_gate.advance(), grad_state, grad_conv_state]
    near_far, near = normed_part([tie(grad_gate[0], *moved), *grad_gate[1:]])

    near_far, near, state_got, conv_got = meet([sum_value[0], sum_gate], near_far, near, state_got, conv_got)
    near_far_got = swap(near_far, "tensor", 1)
    state_sum = add_low(grad_state, state_got)
    state_got = swap(state_sum, "tensor", 2)
    grad_conv_state = grad_conv_state + conv_got
    moved = [sum_value[0].advance(), sum_gate.advance(), state_sum]
    near, near_far_got, *_ = lax.optimization_barrier((near, near_far_got, *moved))
    near_sum = add_low(near[0], near_far_got[1])
    over_y = swap(near_sum, "tensor", 2)
    late = (
        grad_step, norm_gain, grad_conv_state, grad_heads, normed, state_got,
        grad_conv, grad_skip, grad_gain, stats, marks, per_head,
    )
    (
        grad_step, norm_gain, grad_conv_state, grad_heads, normed, state_got,
        grad_conv, grad_skip, grad_gain, stats, marks, per_head,
    ) = lax.optimization_barrier((late, near_sum))[0]
    state_all = add_low(state_sum, state_got)
    own_rows = piece_rows // parts
    grad_w_state = dot(normed, state_all, TN).astype(BF16)
    grad_w_state = lax.dynamic_slice_in_dim(
        grad_w_state.reshape(groups, parts, own_rows, states2), rank, 1, axis=1
    )
    grad_w_step = dot(grad_step[:, :heads], normed, TN).astype(BF16)
    grad_w_state, grad_w_step, grad_conv, grad_skip, grad_gain, stats, marks = meet(
        sum_value, grad_w_state, grad_w_step, grad_conv, grad_skip, grad_gain, stats, marks
    )
    moved = [sum_value[1].advance(), sum_value[0].advance()]
    (grad_w_state, grad_w_step, grad_conv, grad_skip, grad_gain, stats, marks), _ = lax.optimization_barrier(
        ((grad_w_state, grad_w_step, grad_conv, grad_skip, grad_gain, stats, marks), moved)
    )
    meet(sum_out, *moved)
    grad_w_step = grad_w_step.reshape(heads, groups, piece_rows).transpose(1, 0, 2)
    small = jnp.concatenate(
        [grad_w_state.reshape(groups, own_rows * states2), grad_w_step.reshape(groups, heads * piece_rows)], axis=1
    ).reshape(groups // (2 << low_bits), 2, 1 << low_bits, -1)
    small = jnp.stack([small[turned(j, high_bits)] for j in range(small.shape[0])])
    small_own = lax.dynamic_slice_in_dim(small, place[0], 1, 1).reshape(groups // 2, -1)
    small_send = lax.dynamic_slice_in_dim(small, 1 - place[0], 1, 1).reshape(groups // 2, -1)
    small_sum = Sum(small_own, over_x(small_send), 0, low_bits)
    grad_conv, grad_skip, grad_gate_gain = (
        jnp.concatenate(array, axis=1) for array in (grad_conv, grad_skip, grad_gain)
    )
    skip_sums = jnp.sum(grad_skip.reshape(heads, channels // heads), axis=1)
    pieces = [
        grad_conv[:5].reshape(-1), grad_conv_state.reshape(-1), grad_heads[0, :heads], grad_heads[1, :heads],
        skip_sums, grad_gate_gain[0],
    ]
    total_out = [part.result() for part in sum_out]
    rest = jnp.concatenate(pieces)
    scale_out = lax.rsqrt(stats[0] / (channels * parts) + EPSILON)
    factor = scale_out * marks[:length, 5]
    branch = out_near[1].astype(F32) + out_far_got[0].astype(F32) + out_y.astype(F32)
    own_tokens = tokens.astype(F32)
    output = (own_tokens + factor[:, None] * branch).astype(BF16)

    over_y, small_send, rest, output, *total_out = meet(
        [sum_value[1], sum_gate, small_sum], over_y, small_send, rest, output, *total_out
    )
    moved = [sum_value[1].advance(), small_sum.advance()]
    total_gate = sum_gate.result()
    over_y = tie(over_y, *moved)
    grad_normed = near[1].astype(F32) + near_far_got[0].astype(F32) + over_y.astype(F32)
    own_gain = lax.dynamic_slice_in_dim(norm_gain, rank * quarter, quarter, 0)
    scale_in = per_head[:, 5 * heads : 5 * heads + 1]
    row_norm = jnp.sum(own_tokens * own_gain * grad_normed, axis=1)
    grad_norm_gain = jnp.sum(grad_normed * own_tokens * scale_in, axis=0)
    pack = jnp.concatenate([grad_norm_gain, rest])
    pieces = [grad_norm_gain, *pieces]

    row_got, pack_got = swap(row_norm, "tensor", 1), swap(pack, "dp", 1)
    row_norm, row_got, pack, pack_got = meet([small_sum], row_norm, row_got, pack, pack_got)
    small_sum.advance()
    row_norm, pack = row_norm + row_got, pack + pack_got
    row_got, pack_got = swap(row_norm, "tensor", 2), swap(pack, "dp", 2)
    row_norm, row_got, pack, pack_got = lax.optimization_barrier((row_norm, row_got, pack, pack_got))
    row_norm, pack = row_norm + row_got, pack + pack_got
    bit = 4
    while bit < groups:
        pack = pack + swap(pack, "dp", bit)
        bit *= 2
    grad_tokens = (
        cotangent.astype(F32)
        + scale_in * own_gain * grad_normed
        - own_tokens * scale_in**3 * row_norm[:, None] / width
    ).astype(BF16)
    (grad_tokens,) = meet([*sum_value, small_sum], grad_tokens)
    total_value = [part.result() for part in sum_value]
    small_sum = small_sum.result()[0]
    sum_state = small_sum[: own_rows * states2].reshape(own_rows, states2)
    sum_step = small_sum[own_rows * states2 :].reshape(heads, piece_rows).T

    sum_out = jnp.concatenate(total_out, axis=0)
    sum_gate = total_gate
    sum_value = jnp.concatenate(total_value, axis=1)
    sum_inner = jnp.stack([sum_gate, sum_value], axis=1)

    split = []
    at = 0
    for piece in pieces:
        split.append(pack[at : at + piece.shape[0]])
        at += piece.shape[0]
    return (
        output,
        grad_tokens,
        split[0],
        sum_inner,
        sum_step,
        sum_state,
        split[1].reshape(5, channels),
        split[2].reshape(5, states2),
        split[3],
        split[4],
        split[5],
        split[6],
        sum_out,
    )


def solution(mesh):
    placed = (
        P("dp", "tensor"),
        P("dp", "tensor"),
        P("dp", None),
        P(),
        P(None, None, "tensor"),
        P(None, "tensor"),
        P(),
        P(None, "tensor"),
        P(),
        P("tensor"),
        P("tensor"),
        P("tensor"),
        P("tensor"),
        P("tensor", None),
    )
    return jax.shard_map(
        shards,
        mesh=mesh,
        in_specs=placed,
        out_specs=(
            P("dp", "tensor"),
            P("dp", "tensor"),
            P("tensor"),
            P("dp", None, "tensor"),
            P("dp", "tensor"),
            P(("dp", "tensor"), None),
            P(None, "tensor"),
            P(),
            P("tensor"),
            P("tensor"),
            P("tensor"),
            P("tensor"),
            P("tensor", "dp"),
        ),
        check_vma=False,
    )
```
